32 devices in a mesh: rows: 8 (over y, x, core), blk: 4 (over z).
Axes of the slice: x: 2, y: 2, z: 4, core: 2. Of those that a mesh axis runs over, the one named last changes fastest.
Arguments:
- hidden_in: bfloat16 [40, 800, 768], P('rows', 'blk'), may hold values from -6 to 6
- segment_ids: int32 [40, 800], P('rows', 'blk'), may hold values from 0 to 3, as said below
- bucket_map: int32 [1599], replicated, may hold values from 0 to 319, as said below
- qkv_weight: bfloat16 [768, 2304], P(('rows', 'blk')), may hold values from -0.21875 to 0.21875
- out_weight: bfloat16 [768, 768], P(('rows', 'blk')), may hold values from -0.875 to 0.875
- up_weight: bfloat16 [768, 3072], P(('rows', 'blk')), may hold values from -0.21875 to 0.21875
- down_weight: bfloat16 [3072, 768], P(('rows', 'blk')), may hold values from -0.109375 to 0.109375
- bias_cols: bfloat16 [768, 6], P(('rows', 'blk')), may hold values from -4 to 4
- norm_gains: bfloat16 [768, 2], P(('rows', 'blk')), may hold values from 0.25 to 1.75
- up_bias: bfloat16 [3072], P(('rows', 'blk')), may hold values from -4 to 4
- rel_table: float32 [320, 12], replicated, may hold values from -6 to 6
- gate_weight: float32 [64, 8], replicated, may hold values from -0.375 to 0.375
- gate_scale: float32 [12], replicated, may hold values from 0.5 to 2
- cotangent: bfloat16 [40, 800, 768], P('rows', 'blk'), may hold values from -6 to 6
Outputs:
- hidden_out: bfloat16 [40, 800, 768], P('rows', 'blk')
- grad_input: bfloat16 [40, 800, 768], P('rows', 'blk')
- grad_qkv: float32 [768, 2304], P(('rows', 'blk'))
- grad_out: float32 [768, 768], P(('rows', 'blk'))
- grad_up: float32 [768, 3072], P(('rows', 'blk'))
- grad_down: float32 [3072, 768], P(('rows', 'blk'))
- grad_biases: float32 [768, 6], P(('rows', 'blk'))
- grad_gains: float32 [768, 2], P(('rows', 'blk'))
- grad_upbias: float32 [3072], P(('rows', 'blk'))
- grad_table: float32 [320, 12], replicated
- grad_gate_weight: float32 [64, 8], replicated
- grad_gate_scale: float32 [12], replicated
The draws below stay inside these ranges and needn't reach their ends.
Inputs may be any that keep to these rules, and one draw needn't show every extreme that they name: `segment_ids`: along a row the utterance numbers never fall except to the padding 0, which closes every row; one utterance of each row runs from the first block of 200 frames to the last. `bucket_map`: entry d + 799 is the bucket of a key d frames after its query: 0 for d = 0, under 320 / 2 for d < 0, 160 or more for d > 0, never falling as the magnitude of d grows.
All inputs are finite; a program needn't handle non-finite values.
Results may differ from the reference program's by a relative error of at most 0.03.
Values may be sent and summed in bfloat16 or wider, within the bound.
No kernel may reach another device: no remote copies, remote signals or barrier semaphores. Data moves between devices by JAX's collectives and lax.ppermute only.
A program may use at most 256 MiB of HBM per device.

```python
import math
import jax
import jax.numpy as jnp
from jax import lax

D = 768
H = 12
DH = 64
FF = 3072
NB = 320
GATE = 8
FRAMES = 800
BF = 200
ROWS = 40


def draw_segment_ids(key, part):
    key = jax.random.fold_in(key, 11)
    first_key, second_key, third_key = jax.random.split(key, 3)
    long_begin = jax.random.randint(first_key, (ROWS, 1), 1, max(BF // 2, 2))
    padding = jax.random.randint(second_key, (ROWS, 1), 1, BF // 4 + 2)
    tail_frames = jax.random.randint(third_key, (ROWS, 1), 1, BF // 4 + 2)
    position = jnp.arange(FRAMES, dtype=jnp.int32)[None, :]
    long_end = FRAMES - padding - tail_frames
    segments = jnp.where(position < long_begin, 1, jnp.where(position < long_end, 2, jnp.where(position < FRAMES - padding, 3, 0)))
    return segments.astype(jnp.int32)


def draw_bucket_map(key, part):
    key = jax.random.fold_in(key, 23)
    half_count = NB // 2
    exact_reach = min(half_count // 2, FRAMES // 8)
    distance = jnp.arange(1, FRAMES, dtype=jnp.int32)
    coarse = (jax.random.randint(key, (FRAMES - 1,), 0, 5) == 0).astype(jnp.int32)
    increment = jnp.where(distance <= exact_reach, 1, coarse)
    level = jnp.minimum(jnp.cumsum(increment), half_count - 1)
    level = jnp.where(distance == FRAMES - 1, half_count - 1, level)
    level = jnp.concatenate([jnp.zeros((1,), jnp.int32), level.astype(jnp.int32)])
    offsets = jnp.arange(2 * FRAMES - 1, dtype=jnp.int32) - (FRAMES - 1)
    picked = level[jnp.abs(offsets)]
    return jnp.where(offsets > 0, half_count + picked, picked).astype(jnp.int32)


def steps_of(rng, extent, shards, low, high):
    def one(dim, blocks):
        steps = jax.random.uniform(jax.random.fold_in(jax.random.fold_in(rng, 6), dim), (blocks,), jnp.float32, low / len(shards), high / len(shards))
        return jnp.repeat(jnp.exp(steps), extent[dim] // blocks).reshape((-1,) + (1,) * (len(extent) - dim - 1))

    level = one(*shards[0])
    for cut in shards[1:]:
        level = level * one(*cut)
    return level


def bell_draw(rng, dims, scale, reach, cuts=(), kind=jnp.bfloat16):
    entries = jax.random.normal(rng, dims, jnp.float32) * scale
    if len(cuts) > 0:
        entries = steps_of(rng, dims, cuts, -0.22, 0.18) * entries
    return jnp.clip(entries, min=-reach, max=reach).astype(kind)


def setup_inputs(seed: int = 0) -> dict:
    streams_of = jax.random.split(jax.random.key(seed), 15)
    return {
        "hidden_in": bell_draw(streams_of[0], (ROWS, FRAMES, D), 1.0, 6.0, ((0, 8), (1, 4))),
        "segment_ids": draw_segment_ids(jax.random.fold_in(streams_of[14], 71), 0),
        "bucket_map": draw_bucket_map(jax.random.fold_in(streams_of[14], 71), 0),
        "qkv_weight": bell_draw(streams_of[3], (D, 3 * D), D ** -0.5, 0.21875, ((0, 32),)),
        "out_weight": bell_draw(streams_of[4], (D, D), (D // 16) ** -0.5, 0.875, ((0, 32),)),
        "up_weight": bell_draw(streams_of[5], (D, FF), D ** -0.5, 0.21875, ((0, 32),)),
        "down_weight": bell_draw(streams_of[6], (FF, D), FF ** -0.5, 0.109375, ((0, 32),)),
        "bias_cols": bell_draw(streams_of[7], (D, 6), 0.3, 4.0, ((0, 32),)),
        "norm_gains": jnp.clip(1.0 + 0.15 * jax.random.normal(streams_of[8], (D, 2), jnp.float32), 0.25, 1.75).astype(jnp.bfloat16),
        "up_bias": bell_draw(streams_of[9], (FF,), 0.3, 4.0, ((0, 32),)),
        "rel_table": bell_draw(streams_of[10], (NB, H), 1.0, 6.0, (), jnp.float32),
        "gate_weight": bell_draw(streams_of[11], (DH, GATE), (4 * DH) ** -0.5, 0.375, (), jnp.float32),
        "gate_scale": jnp.clip(jnp.exp(jax.random.uniform(streams_of[12], (H,), jnp.float32, math.log(0.5), math.log(2.0))), 0.5, 2.0),
        "cotangent": bell_draw(streams_of[13], (ROWS, FRAMES, D), 1.0, 6.0, ((0, 8), (1, 4))),
    }


@jax.custom_vjp
def low(v):
    return lax.optimization_barrier(v.astype(jnp.bfloat16)).astype(jnp.float32)

@jax.custom_vjp
def low_back(v):
    return v

def low_keep(v):
    return (low(v), None)

def low_pass(kept, grad):
    return (grad,)

def back_keep(v):
    return (v, None)

def back_low(kept, grad):
    return (low(grad),)
low.defvjp(low_keep, low_pass)
low_back.defvjp(back_keep, back_low)
NEG_BIG = -1e+30
EPS_NORM = 1e-05

def layer_norm(hidden, gain, shift):
    centred = hidden - lax.optimization_barrier(jnp.mean(hidden, axis=-1, keepdims=True))
    spread = lax.optimization_barrier(jnp.mean(centred * centred, axis=-1, keepdims=True))
    return centred * lax.rsqrt(spread + EPS_NORM) * gain + shift

def exact_gelu(inner):
    return jax.nn.gelu(inner, approximate=False)

def gate_values(tokens, gate_weight, gate_scale):
    head_count = gate_scale.shape[0]
    split_heads = tokens.reshape(tokens.shape[0], head_count, -1)
    first_dir = lax.optimization_barrier(jnp.sum(gate_weight[:, :4], axis=1))
    second_dir = lax.optimization_barrier(jnp.sum(gate_weight[:, 4:], axis=1))
    first_gate = jax.nn.sigmoid(jnp.einsum('nhd,d->nh', split_heads, first_dir, precision=lax.Precision.HIGHEST))
    second_gate = jax.nn.sigmoid(jnp.einsum('nhd,d->nh', split_heads, second_dir, precision=lax.Precision.HIGHEST))
    return first_gate * (second_gate * gate_scale - 1.0) + 2.0

def reference(hidden_in, segment_ids, bucket_map, qkv_weight, out_weight, up_weight, down_weight, bias_cols, norm_gains, up_bias, rel_table, gate_weight, gate_scale, cotangent):
    group_rows = math.gcd(ROWS, 4)
    block_total = ROWS // group_rows
    token_total = ROWS * FRAMES
    distance = jnp.arange(FRAMES, dtype=jnp.int32)[None, :] - jnp.arange(FRAMES, dtype=jnp.int32)[:, None] + (FRAMES - 1)
    bucket_grid = bucket_map[distance]
    seg_groups = segment_ids.reshape(block_total, group_rows, FRAMES)

    def forward(hidden, qkv_mat, out_mat, up_mat, down_mat, biases, gain_cols, inner_bias, rel_values, gate_mat, gate_factor):
        tokens = hidden.reshape(token_total, D)
        projected = jnp.dot(tokens, qkv_mat, precision=lax.Precision.HIGHEST)
        queries = low_back(low((projected[:, :D] + biases[:, 0]) * DH ** (-0.5)))
        keys = low_back(low(projected[:, D:2 * D]))
        values = low_back(low(projected[:, 2 * D:] + biases[:, 1]))
        gating = gate_values(tokens, gate_mat, gate_factor)
        table_grid = jnp.transpose(rel_values[bucket_grid], (2, 0, 1))

        def attend(items):
            query_group, key_group, value_group, gate_group, seg_group = items
            raw = low_back(jnp.einsum('rqhd,rkhd->rhqk', query_group, key_group, precision=lax.Precision.HIGHEST))
            scores = raw + jnp.transpose(gate_group, (0, 2, 1))[..., None] * table_grid[None]
            allowed = (seg_group[:, :, None] == seg_group[:, None, :])[:, None]
            scores = jnp.where(allowed, scores, NEG_BIG)
            peak = lax.optimization_barrier(jnp.max(scores, axis=-1, keepdims=True))
            weights = jnp.where(allowed, jnp.exp(scores - peak), 0.0)
            probs = low(weights / lax.optimization_barrier(jnp.sum(weights, axis=-1, keepdims=True)))
            return jnp.einsum('rhqk,rkhd->rqhd', probs, value_group, precision=lax.Precision.HIGHEST)
        grouped = (queries.reshape(block_total, group_rows, FRAMES, H, DH), keys.reshape(block_total, group_rows, FRAMES, H, DH), values.reshape(block_total, group_rows, FRAMES, H, DH), gating.reshape(block_total, group_rows, FRAMES, H), seg_groups)
        attended = lax.map(jax.checkpoint(attend), grouped).reshape(token_total, D)
        attended = low_back(low(attended))
        attn_out = low_back(jnp.dot(attended, out_mat, precision=lax.Precision.HIGHEST)) + biases[:, 2]
        normed = layer_norm(tokens + attn_out, gain_cols[:, 0], biases[:, 4])
        inner = low_back(jnp.dot(low(normed), up_mat, precision=lax.Precision.HIGHEST)) + inner_bias
        activated = low(exact_gelu(inner))
        branch = low_back(jnp.dot(activated, down_mat, precision=lax.Precision.HIGHEST)) + biases[:, 3]
        result = layer_norm(normed + branch, gain_cols[:, 1], biases[:, 5])
        return result.reshape(ROWS, FRAMES, D)
    floats = (hidden_in.astype(jnp.float32), qkv_weight.astype(jnp.float32), out_weight.astype(jnp.float32), up_weight.astype(jnp.float32), down_weight.astype(jnp.float32), bias_cols.astype(jnp.float32), norm_gains.astype(jnp.float32), up_bias.astype(jnp.float32), rel_table.astype(jnp.float32), gate_weight.astype(jnp.float32), gate_scale.astype(jnp.float32))
    result, pullback = jax.vjp(forward, *floats)
    grads = pullback(cotangent.astype(jnp.float32))
    return (result.astype(jnp.bfloat16), grads[0].astype(jnp.bfloat16), grads[1], grads[2], grads[3], grads[4], grads[5], grads[6], grads[7], grads[8], grads[9], grads[10])
```

```python
import functools

import jax
import jax.numpy as jnp
from jax import lax
from jax.experimental import pallas as pl
from jax.experimental.pallas import tpu as pltpu
from jax.sharding import PartitionSpec as P

EPS_NORM = 1e-05
LANES = 128
SMALL = 128
BF16 = jnp.bfloat16
F32 = jnp.float32
NN = (((1,), (0,)), ((), ()))
NT = (((1,), (1,)), ((), ()))
TN = (((0,), (0,)), ((), ()))
HIGHEST = lax.Precision.HIGHEST


def dotf(a, b, dims):
    return lax.dot_general(a, b, dims, preferred_element_type=F32)


def tiles_of(total, tile):
    return [(s, min(tile, total - s)) for s in range(0, total, tile)]


def exp_rows(u_ref, head, width):
    return pltpu.roll(
        jnp.broadcast_to(u_ref[head : head + 1, :], (LANES, width)), 0, 1, stride=1, stride_axis=0
    )


def forward_kernel(
    tile, flip, u_ref, q_ref, k_ref, v_ref, qa_ref, ka_ref, g_ref, o_ref, ob_ref, lse_ref, t_scr
):
    nq, nk, width = q_ref.shape[0], k_ref.shape[0], u_ref.shape[-1]
    half = LANES // 2
    shift = -(-nk // LANES)
    low = lax.broadcasted_iota(jnp.int32, (1, LANES), 1) < half
    low_rows = lax.broadcasted_iota(jnp.int32, (LANES, 1), 0) < half
    k, v, q = k_ref[...], v_ref[...], q_ref[...]
    zero = jnp.zeros((), BF16)
    khs, qhs, vzs = [], [], []
    for hh in range(2):
        t_scr[hh] = exp_rows(u_ref, hh, width)
        sel = low if hh == 0 else jnp.logical_not(low)
        khs.append(jnp.where(sel, k, ka_ref[...]))
        qhs.append(jnp.where(sel, q, qa_ref[...]))
        vzs.append(jnp.where(sel, v, zero))
    vt = v.T if flip else None
    for first, cols in tiles_of(nq, tile):
        total, scales, parts = None, [], []
        for hh in range(2):
            raw = dotf(khs[hh], qhs[hh][first : first + cols], NT)
            g = g_ref[hh : hh + 1, first : first + cols]
            scores, peak = [], None
            for f2, r2 in tiles_of(nk, LANES):
                col = (shift - f2 // LANES) * LANES + first
                s = raw[f2 : f2 + r2] + g * t_scr[hh, 0:r2, col : col + cols]
                top = jnp.max(s, axis=0, keepdims=True)
                peak = top if peak is None else jnp.maximum(peak, top)
                scores.append(s)
            probs, mass = [], None
            for s in scores:
                p = jnp.exp(s - peak)
                part = jnp.sum(p, axis=0, keepdims=True)
                mass = part if mass is None else mass + part
                probs.append(p.astype(BF16))
            lse_ref[hh : hh + 1, first : first + cols] = peak + jnp.log(mass)
            pb = jnp.concatenate(probs, axis=0)
            if flip:
                parts.append(dotf(vt[hh * half : (hh + 1) * half], pb, NN) / mass)
            else:
                x = dotf(pb, vzs[hh], TN)
                total = x if total is None else total + x
                scales.append(1.0 / mass)
        if flip:
            o = jnp.concatenate(parts, axis=0).T
        else:
            o = total * jnp.where(low_rows, scales[0], scales[1]).T
        o_ref[first : first + cols, :] = o
        ob_ref[first : first + cols, :] = o.astype(BF16)


def attend_forward(u, q, k, v, qa, ka, g, cols, tile, flip):
    nq, nk = q.shape[0], k.shape[0]
    pairs, _, width = u.shape
    col = lambda c: (lambda p: (0, c + p))
    fix = lambda p: (0, 0)
    row_spec = pl.BlockSpec((None, 2, nq), lambda p: (p, 0, 0))
    return pl.pallas_call(
        functools.partial(forward_kernel, tile, flip),
        grid=(pairs,),
        in_specs=[
            pl.BlockSpec((None, 2, width), lambda p: (p, 0, 0)),
            pl.BlockSpec((nq, LANES), col(cols[0])),
            pl.BlockSpec((nk, LANES), col(cols[1])),
            pl.BlockSpec((nk, LANES), col(cols[2])),
            pl.BlockSpec((nq, LANES), fix),
            pl.BlockSpec((nk, LANES), fix),
            row_spec,
        ],
        out_specs=[
            pl.BlockSpec((nq, LANES), lambda p: (0, p)),
            pl.BlockSpec((nq, LANES), lambda p: (0, p)),
            row_spec,
        ],
        out_shape=[
            jax.ShapeDtypeStruct((nq, pairs * LANES), F32),
            jax.ShapeDtypeStruct((nq, pairs * LANES), BF16),
            jax.ShapeDtypeStruct((pairs, 2, nq), F32),
        ],
        scratch_shapes=[pltpu.VMEM((2, LANES, width), F32)],
        compiler_params=pltpu.CompilerParams(vmem_limit_bytes=48 * 2**20),
        name="attention_forward",
    )(u, q, k, v, qa, ka, g)


def backward_kernel(
    u_ref, q_ref, k_ref, v_ref, do_ref, att_ref, qa_ref, ka_ref, g_ref, lse_ref,
    dq_ref, dkv_ref, gate_ref, diag_ref, t_scr, c_scr,
):
    nq, nk, width = q_ref.shape[0], k_ref.shape[0], u_ref.shape[-1]
    shift = -(-nk // LANES)
    low = lax.broadcasted_iota(jnp.int32, (1, LANES), 1) < LANES // 2
    k, v, q, do = k_ref[...], v_ref[...], q_ref[...], do_ref[...]
    prod = do.astype(F32) * att_ref[...]
    zero = jnp.zeros((), BF16)
    dq, dk, dv = None, None, None
    for hh in range(2):
        t_scr[hh] = exp_rows(u_ref, hh, width)
        c_scr[...] = jnp.zeros_like(c_scr)
        sel = low if hh == 0 else jnp.logical_not(low)
        ones = jnp.broadcast_to(jnp.where(sel, 1.0, 0.0), (8, LANES))
        delta = lax.dot_general(ones, prod, NT, precision=HIGHEST, preferred_element_type=F32)[0:1]
        ka = jnp.where(sel, k, ka_ref[...])
        qa = jnp.where(sel, q, qa_ref[...])
        kz, qz, doz = jnp.where(sel, k, zero), jnp.where(sel, q, zero), jnp.where(sel, do, zero)
        lse = lse_ref[hh : hh + 1, :]
        g = g_ref[hh : hh + 1, :]
        gate = jnp.zeros((1, nq), F32)
        raw = dotf(ka, qa, NT)
        dp = dotf(v, doz, NT)
        ps, ds = [], []
        for first, rows in tiles_of(nk, LANES):
            col = (shift - first // LANES) * LANES
            t = t_scr[hh, 0:rows, col : col + nq]
            p = jnp.exp(raw[first : first + rows] + (g * t - lse))
            d = p * (dp[first : first + rows] - delta)
            gate += jnp.sum(d * t, axis=0, keepdims=True)
            c_scr[0:rows, col : col + nq] += d * g
            ps.append(p.astype(BF16))
            ds.append(d.astype(BF16))
        pb, db = jnp.concatenate(ps, axis=0), jnp.concatenate(ds, axis=0)
        dk_add, dv_add, dq_add = dotf(db, qz, NN), dotf(pb, doz, NN), dotf(db, kz, TN)
        dk = dk_add if dk is None else dk + dk_add
        dv = dv_add if dv is None else dv + dv_add
        dq = dq_add if dq is None else dq + dq_add
        gate_ref[hh : hh + 1, :] = gate
        half = LANES // 2
        acc = c_scr[...]
        while half >= 8:
            acc = acc[:half] + pltpu.roll(acc[half:], width - half, 1)
            half //= 2
        row = lax.broadcasted_iota(jnp.int32, (8, 1), 0)
        for bit in (1, 2, 4):
            acc = jnp.where((row & bit) != 0, pltpu.roll(acc, width - bit, 1), acc)
        diag_ref[hh : hh + 1, :] = jnp.sum(acc, axis=0, keepdims=True)
    dq_ref[...] = (dq.astype(BF16) * (LANES // 2) ** -0.5).astype(BF16)
    dkv_ref[0] = dk.astype(BF16)
    dkv_ref[1] = dv.astype(BF16)


def attend_backward(u, q, k, v, do, att, qa, ka, g, lse, cols):
    nq, nk = q.shape[0], k.shape[0]
    pairs, _, width = u.shape
    col = lambda c: (lambda p: (0, c + p))
    fix = lambda p: (0, 0)
    row_spec = pl.BlockSpec((None, 2, nq), lambda p: (p, 0, 0))
    wide_spec = pl.BlockSpec((None, 2, width), lambda p: (p, 0, 0))
    return pl.pallas_call(
        backward_kernel,
        grid=(pairs,),
        in_specs=[
            wide_spec,
            pl.BlockSpec((nq, LANES), col(cols[0])),
            pl.BlockSpec((nk, LANES), col(cols[1])),
            pl.BlockSpec((nk, LANES), col(cols[2])),
            pl.BlockSpec((nq, LANES), col(0)),
            pl.BlockSpec((nq, LANES), col(0)),
            pl.BlockSpec((nq, LANES), fix),
            pl.BlockSpec((nk, LANES), fix),
            row_spec,
            row_spec,
        ],
        out_specs=[
            pl.BlockSpec((nq, LANES), col(0)),
            pl.BlockSpec((2, nk, LANES), lambda p: (0, 0, p)),
            row_spec,
            wide_spec,
        ],
        out_shape=[
            jax.ShapeDtypeStruct((nq, pairs * LANES), BF16),
            jax.ShapeDtypeStruct((2, nk, pairs * LANES), BF16),
            jax.ShapeDtypeStruct((pairs, 2, nq), F32),
            jax.ShapeDtypeStruct((pairs, 2, width), F32),
        ],
        scratch_shapes=[pltpu.VMEM((2, LANES, width), F32), pltpu.VMEM((LANES, width), F32)],
        compiler_params=pltpu.CompilerParams(vmem_limit_bytes=56 * 2**20),
        name="attention_backward",
    )(u, q, k, v, do, att, qa, ka, g, lse)


def project_kernel(own_ref, all_ref, loc_ref, w_ref, b_ref, own_out, q_out, kv_out):
    step = pl.program_id(0)
    w = w_ref[...]
    b = b_ref[0:1, :]
    scale = jnp.where(step == 0, (LANES // 2) ** -0.5, 1.0)
    own_out[...] = ((dotf(own_ref[...], w, NN) + b) * scale).astype(BF16)

    @pl.when(step == 0)
    def _():
        q_out[...] = ((dotf(loc_ref[...], w, NN) + b) * scale).astype(BF16)

    @pl.when(step > 0)
    def _():
        kv_out[...] = (dotf(all_ref[...], w, NN) + b).astype(BF16)


def project(x_own, x_all, x_loc, weight, bias):
    width = x_own.shape[1]
    n_own, n_all, n_loc = x_own.shape[0], x_all.shape[0], x_loc.shape[0]
    fix = lambda c: (0, 0)
    return pl.pallas_call(
        project_kernel,
        grid=(3,),
        in_specs=[
            pl.BlockSpec((n_own, width), fix),
            pl.BlockSpec((n_all, width), fix),
            pl.BlockSpec((n_loc, width), fix),
            pl.BlockSpec((width, width), lambda c: (0, c)),
            pl.BlockSpec((8, width), lambda c: (0, c)),
        ],
        out_specs=[
            pl.BlockSpec((n_own, width), lambda c: (0, c)),
            pl.BlockSpec((n_loc, width), fix),
            pl.BlockSpec((n_all, width), lambda c: (0, jnp.maximum(c - 1, 0))),
        ],
        out_shape=[
            jax.ShapeDtypeStruct((n_own, 3 * width), BF16),
            jax.ShapeDtypeStruct((n_loc, width), BF16),
            jax.ShapeDtypeStruct((n_all, 2 * width), BF16),
        ],
        compiler_params=pltpu.CompilerParams(vmem_limit_bytes=48 * 2**20),
        name="projection",
    )(x_own, x_all, x_loc, weight, bias)


def gelu_parts(x):
    size = jnp.abs(x)
    t = 1.0 / (1.0 + (0.3275911 * 0.7071067811865476) * size)
    poly = t * (
        0.254829592
        + t * (-0.284496736 + t * (1.421413741 + t * (-1.453152027 + t * 1.061405429)))
    )
    bell = jnp.exp(-0.5 * x * x)
    tail = 0.5 * poly * bell
    phi = jnp.where(x >= 0, 1.0 - tail, tail)
    return x * phi, phi + x * bell * 0.3989422804014327


def mean_last(v):
    return jnp.sum(v, axis=-1, keepdims=True) * (1.0 / v.shape[-1])


def layer_kernel(
    chunks, tiles,
    x0_ref, x1_ref, a0_ref, a1_ref, c0_ref, c1_ref, wo_ref, up_ref, down_ref, vec_ref, ub_ref,
    h0_ref, h1_ref, ga0_ref, ga1_ref, g10_ref, g11_ref, grad_ref, sums_ref, ubg_ref,
    z_scr, r_scr, nh_scr, acc_scr, gn_scr, di_scr, act_scr, der_scr, ih_scr,
):
    step = pl.program_id(0)
    width = x0_ref.shape[1]
    own = x0_ref.shape[0]

    def pick(first_ref, second_ref, first, rows):
        if first < own:
            return first_ref[first : first + rows, :]
        return second_ref[first - own : first - own + rows, :]

    def put(first_ref, second_ref, first, rows, value):
        if first < own:
            first_ref[first : first + rows, :] = value
        else:
            second_ref[first - own : first - own + rows, :] = value

    vec = lambda i: vec_ref[i : i + 1, :]

    @pl.when(step == 0)
    def _():
        sums_ref[...] = jnp.zeros_like(sums_ref)
        for first, rows in tiles:
            y = dotf(pick(a0_ref, a1_ref, first, rows), wo_ref[...], NN) + vec(0)
            y = y + pick(x0_ref, x1_ref, first, rows).astype(F32)
            y = y - mean_last(y)
            r = lax.rsqrt(mean_last(y * y) + EPS_NORM)
            z = y * r
            z_scr[first : first + rows, :] = z
            r_scr[first : first + rows, :] = r
            nh_scr[first : first + rows, :] = (z * vec(4) + vec(2)).astype(BF16)

    for j in range(chunks):
        @pl.when(step == j)
        def _():
            cols = slice(j * width, (j + 1) * width)
            for first, rows in tiles:
                here = slice(first, first + rows)
                inner = dotf(nh_scr[here, :], up_ref[...], NN) + ub_ref[j : j + 1, :]
                act, der = gelu_parts(inner)
                act = act.astype(BF16)
                act_scr[here, cols] = act
                der_scr[here, cols] = der.astype(BF16)
                add = dotf(act, down_ref[...], NN)
                acc_scr[here, :] = add if j == 0 else acc_scr[here, :] + add

    @pl.when(step == chunks)
    def _():
        for first, rows in tiles:
            here = slice(first, first + rows)
            v = z_scr[here, :] * vec(4) + vec(2) + acc_scr[here, :] + vec(1)
            v = v - mean_last(v)
            r = lax.rsqrt(mean_last(v * v) + EPS_NORM)
            z = v * r
            put(h0_ref, h1_ref, first, rows, (z * vec(5) + vec(3)).astype(BF16))
            c = pick(c0_ref, c1_ref, first, rows).astype(F32)
            q = c * vec(5)
            gt = r * (q - mean_last(q) - z * mean_last(q * z))
            gn_scr[here, :] = gt
            di_scr[here, :] = gt.astype(BF16)
            sums_ref[3:4, :] += jnp.sum(gt, axis=0, keepdims=True)
            sums_ref[5:6, :] += jnp.sum(c, axis=0, keepdims=True)
            sums_ref[7:8, :] += jnp.sum(c * z, axis=0, keepdims=True)

    for j in range(chunks):
        cols = slice(j * width, (j + 1) * width)

        @pl.when(step == chunks + 2 * j)
        def _():
            grad_ref[...] = dotf(act_scr[:, cols], di_scr[...], TN).astype(BF16)
            total = None
            for first, rows in tiles:
                here = slice(first, first + rows)
                gi = dotf(di_scr[here, :], down_ref[...], NT) * der_scr[here, cols].astype(F32)
                part = jnp.sum(gi, axis=0, keepdims=True)
                total = part if total is None else total + part
                ih_scr[here, :] = gi.astype(BF16)
            ubg_ref[j : j + 1, :] = total

        @pl.when(step == chunks + 2 * j + 1)
        def _():
            grad_ref[...] = dotf(nh_scr[...], ih_scr[...], TN).astype(BF16)
            for first, rows in tiles:
                here = slice(first, first + rows)
                gn_scr[here, :] += dotf(ih_scr[here, :], up_ref[...], NT)

    @pl.when(step == 3 * chunks)
    def _():
        for first, rows in tiles:
            here = slice(first, first + rows)
            gn = gn_scr[here, :]
            z = z_scr[here, :]
            q = gn * vec(4)
            g1 = r_scr[here, :] * (q - mean_last(q) - z * mean_last(q * z))
            put(g10_ref, g11_ref, first, rows, g1)
            ah = g1.astype(BF16)
            di_scr[here, :] = ah
            put(ga0_ref, ga1_ref, first, rows, dotf(ah, wo_ref[...], NT).astype(BF16))
            sums_ref[2:3, :] += jnp.sum(g1, axis=0, keepdims=True)
            sums_ref[4:5, :] += jnp.sum(gn, axis=0, keepdims=True)
            sums_ref[6:7, :] += jnp.sum(gn * z, axis=0, keepdims=True)
        grad_ref[...] = (
            dotf(a0_ref[...], di_scr[0:own, :], TN) + dotf(a1_ref[...], di_scr[own:, :], TN)
        ).astype(BF16)


def layer_rest(x, att, cot, weights, wo_block, up_block, down_block, vec, up_bias):
    (x0, x1), (a0, a1), (c0, c1) = x, att, cot
    own, width = x0.shape
    extra = x1.shape[0]
    total = own + extra
    chunks = up_bias.shape[0]
    tiles = [(s, r) for s, r in tiles_of(own, 272)] + [(own + s, r) for s, r in tiles_of(extra, 272)]
    fix = lambda s: (0, 0)
    once = pl.Buffered(buffer_count=1)

    def chunk_of(s):
        return jnp.where(s < chunks, s, jnp.clip((s - chunks) // 2, 0, chunks - 1))

    def const(shape):
        return pl.BlockSpec(shape, fix, pipeline_mode=once)

    rows0, rows1 = const((own, width)), const((extra, width))
    square = (width, width)
    return pl.pallas_call(
        functools.partial(layer_kernel, chunks, tiles),
        grid=(3 * chunks + 1,),
        in_specs=[
            rows0, rows1, rows0, rows1, rows0, rows1,
            pl.BlockSpec(square, lambda s: (0, wo_block), pipeline_mode=once),
            pl.BlockSpec(square, lambda s: (0, up_block + chunk_of(s))),
            pl.BlockSpec(square, lambda s: (0, down_block + chunk_of(s))),
            const(vec.shape),
            const(up_bias.shape),
        ],
        out_specs=[
            rows0, rows1, rows0, rows1, rows0, rows1,
            pl.BlockSpec(square, lambda s: (0, jnp.maximum(s - chunks, 0))),
            const((8, width)),
            const(up_bias.shape),
        ],
        out_shape=[
            jax.ShapeDtypeStruct((own, width), BF16),
            jax.ShapeDtypeStruct((extra, width), BF16),
            jax.ShapeDtypeStruct((own, width), BF16),
            jax.ShapeDtypeStruct((extra, width), BF16),
            jax.ShapeDtypeStruct((own, width), F32),
            jax.ShapeDtypeStruct((extra, width), F32),
            jax.ShapeDtypeStruct((width, (2 * chunks + 1) * width), BF16),
            jax.ShapeDtypeStruct((8, width), F32),
            jax.ShapeDtypeStruct(up_bias.shape, F32),
        ],
        scratch_shapes=[
            pltpu.VMEM((total, width), F32),
            pltpu.VMEM((total, 1), F32),
            pltpu.VMEM((total, width), BF16),
            pltpu.VMEM((total, width), F32),
            pltpu.VMEM((total, width), F32),
            pltpu.VMEM((total, width), BF16),
            pltpu.VMEM((total, chunks * width), BF16),
            pltpu.VMEM((total, chunks * width), BF16),
            pltpu.VMEM((total, width), BF16),
        ],
        compiler_params=pltpu.CompilerParams(vmem_limit_bytes=60 * 2**20),
        name="layer_rest",
    )(x0, x1, a0, a1, c0, c1, weights, weights, weights, vec, up_bias)


def shared_input_kernel(dq_ref, dkv_ref, w_ref, part_ref, loc_ref, acc):
    step = pl.program_id(0)

    @pl.when(step == 0)
    def _():
        loc_ref[...] = dotf(dq_ref[...], w_ref[...], NT)

    @pl.when(step == 1)
    def _():
        acc[...] = dotf(dkv_ref[...], w_ref[...], NT)

    @pl.when(step == 2)
    def _():
        part_ref[...] = (acc[...] + dotf(dkv_ref[...], w_ref[...], NT)).astype(BF16)


def shared_input(dq, dkv, weight):
    n_loc, width = dq.shape
    n_all = dkv.shape[1]
    fix = lambda c: (0, 0)
    return pl.pallas_call(
        shared_input_kernel,
        grid=(3,),
        in_specs=[
            pl.BlockSpec((n_loc, width), fix),
            pl.BlockSpec((None, n_all, width), lambda c: (jnp.maximum(c - 1, 0), 0, 0)),
            pl.BlockSpec((width, width), lambda c: (0, c)),
        ],
        out_specs=[pl.BlockSpec((n_all, width), fix), pl.BlockSpec((n_loc, width), fix)],
        out_shape=[
            jax.ShapeDtypeStruct((n_all, width), BF16),
            jax.ShapeDtypeStruct((n_loc, width), F32),
        ],
        scratch_shapes=[pltpu.VMEM((n_all, width), F32)],
        compiler_params=pltpu.CompilerParams(vmem_limit_bytes=48 * 2**20),
        name="shared_input",
    )(dq, dkv, weight)


def tail_kernel(
    x0_ref, x4_ref, loc_ref, dq_ref, dkv_ref, dq4_ref, dkv4_ref, w_ref, base_ref,
    dx_ref, grad_ref, sums_ref, acc,
):
    step = pl.program_id(0)
    w = w_ref[...]

    def column_sums(row, first, second):
        sums_ref[row : row + 1, :] = jnp.sum(first.astype(F32), axis=0, keepdims=True) + jnp.sum(
            second.astype(F32), axis=0, keepdims=True
        )

    @pl.when(step == 0)
    def _():
        sums_ref[...] = jnp.zeros_like(sums_ref)
        dq, dq4 = dq_ref[...], dq4_ref[...]
        grad_ref[...] = (dotf(x0_ref[...], dq, TN) + dotf(loc_ref[...], dq4, TN)).astype(BF16)
        column_sums(0, dq, dq4)
        acc[...] = base_ref[...] + dotf(dq, w, NT)

    for c in (1, 2):
        @pl.when(step == c)
        def _():
            d, d4 = dkv_ref[...], dkv4_ref[...]
            grad_ref[...] = (dotf(x0_ref[...], d, TN) + dotf(x4_ref[...], d4, TN)).astype(BF16)
            total = acc[...] + dotf(d, w, NT)
            if c == 1:
                acc[...] = total
            else:
                column_sums(1, d, d4)
                dx_ref[...] = total.astype(BF16)


def tail(x_own, x_all, x_loc, dq, dkv, dq4, dkv4, weight, base):
    own, width = x_own.shape
    n_all, n_loc = x_all.shape[0], x_loc.shape[0]
    fix = lambda c: (0, 0)
    half = lambda c: (jnp.maximum(c - 1, 0), 0, 0)
    return pl.pallas_call(
        tail_kernel,
        grid=(3,),
        in_specs=[
            pl.BlockSpec((own, width), fix),
            pl.BlockSpec((n_all, width), fix),
            pl.BlockSpec((n_loc, width), fix),
            pl.BlockSpec((own, width), fix),
            pl.BlockSpec((None, own, width), half),
            pl.BlockSpec((n_loc, width), fix),
            pl.BlockSpec((None, n_all, width), half),
            pl.BlockSpec((width, width), lambda c: (0, c)),
            pl.BlockSpec((own, width), fix),
        ],
        out_specs=[
            pl.BlockSpec((own, width), fix),
            pl.BlockSpec((width, width), lambda c: (0, c)),
            pl.BlockSpec((8, width), fix),
        ],
        out_shape=[
            jax.ShapeDtypeStruct((own, width), BF16),
            jax.ShapeDtypeStruct((width, 3 * width), BF16),
            jax.ShapeDtypeStruct((8, width), F32),
        ],
        scratch_shapes=[pltpu.VMEM((own, width), F32)],
        compiler_params=pltpu.CompilerParams(vmem_limit_bytes=60 * 2**20),
        name="projection_backward",
    )(x_own, x_all, x_loc, dq, dkv, dq4, dkv4, weight, base)


def gate_logits(x, dirs):
    return lax.dot_general(dirs, x.astype(F32), (((0,), (1,)), ((), ())), precision=HIGHEST)


def shards(
    hidden_in,
    segment_ids,
    bucket_map,
    qkv_weight,
    out_weight,
    up_weight,
    down_weight,
    bias_cols,
    norm_gains,
    up_bias,
    rel_table,
    gate_weight,
    gate_scale,
    cotangent,
):
    row_count, block_len, width = hidden_in.shape
    heads = gate_scale.shape[0]
    pairs = heads // 2
    head_dim = width // heads
    bucket_count = rel_table.shape[0]
    cycle = lax.axis_size("blk")
    place = lax.axis_index("blk")
    frames = block_len * cycle
    shared = row_count - 1
    inner_width = up_weight.shape[1]
    chunks = inner_width // width
    local_rows = qkv_weight.shape[0]
    every = ("rows", "blk")
    assert row_count == cycle + 1

    def hop(array, s):
        return lax.ppermute(array, "blk", [(i, (i + s) % cycle) for i in range(cycle)])

    def take(array, index):
        return lax.dynamic_index_in_dim(array, index, 0, keepdims=False)

    def spread(blocks):
        out = jnp.zeros((cycle,) + blocks[0].shape, blocks[0].dtype)
        for s, block in enumerate(blocks):
            out = lax.dynamic_update_index_in_dim(out, block, (place - s) % cycle, 0)
        return out.reshape((cycle * blocks[0].shape[0],) + blocks[0].shape[1:])

    seg_rows = jnp.pad(
        segment_ids.astype(BF16), ((0, 0), (0, width - block_len))
    )
    own_blocks, shared_blocks, own_segs, shared_segs = [], [], [], []
    for s in range(cycle):
        target = (place + s) % cycle
        packed = jnp.concatenate(
            [
                take(hidden_in, target),
                hidden_in[shared],
                jnp.pad(
                    jnp.stack([take(seg_rows, target), seg_rows[shared]]), ((0, 14), (0, 0))
                ),
            ],
            axis=0,
        )
        got = packed if s == 0 else hop(packed, s)
        own_blocks.append(got[:block_len])
        shared_blocks.append(got[block_len : 2 * block_len])
        own_segs.append(got[2 * block_len, :block_len])
        shared_segs.append(got[2 * block_len + 1, :block_len])
    x_own, x_all = spread(own_blocks), spread(shared_blocks)
    x_loc = hidden_in[shared]
    seg_own, seg_all = spread(own_segs), spread(shared_segs)

    extras = jnp.concatenate(
        [bias_cols, norm_gains, up_bias.reshape(local_rows, chunks)], axis=1
    )
    qkv_pack = jnp.concatenate(
        [qkv_weight, jnp.pad(extras, ((0, 0), (0, SMALL - extras.shape[1])))], axis=1
    )
    up_turned = up_weight.reshape(local_rows, width, chunks).transpose(0, 2, 1)
    rest_pack = jnp.concatenate(
        [
            up_turned.reshape(local_rows, inner_width),
            down_weight.reshape(local_rows, inner_width),
            out_weight,
        ],
        axis=1,
    )
    qkv_full = lax.all_gather(qkv_pack, every, axis=0, tiled=True)
    rest_full = lax.all_gather(rest_pack, every, axis=0, tiled=True)
    small = qkv_full[:, 3 * width :].astype(F32).T
    biases, gains = small[0:6], small[6:8]
    up_bias_rows = small[8 : 8 + chunks]

    cot_blocks = []
    for s in range(cycle):
        part = take(cotangent, (place + s) % cycle)
        cot_blocks.append(part if s == 0 else hop(part, s))
    c_own, c_loc = spread(cot_blocks), cotangent[shared]

    first_dir = jnp.sum(gate_weight[:, :4], axis=1)
    second_dir = jnp.sum(gate_weight[:, 4:], axis=1)
    picks = jnp.repeat(jnp.eye(heads, dtype=F32), head_dim, axis=0)
    dirs = jnp.concatenate(
        [picks * jnp.tile(first_dir, heads)[:, None], picks * jnp.tile(second_dir, heads)[:, None]],
        axis=1,
    )

    def gates(x):
        logits = jax.nn.sigmoid(gate_logits(x, dirs))
        a, b = logits[:heads], logits[heads:]
        return a, b, a * (b * gate_scale[:, None] - 1.0) + 2.0

    a_own, b_own, g_own = gates(x_own)
    a_loc, b_loc, g_loc = gates(x_loc)

    shift = -(-frames // LANES)
    span = 2 * frames - 1
    lead = shift * LANES - (frames - 1)
    table_width = 2 * shift * LANES
    turned = bucket_map[::-1]
    slots = jnp.pad(turned, (lead, table_width - lead - span), constant_values=-1)
    slots_loc = lax.dynamic_slice_in_dim(
        jnp.pad(slots, (0, frames), constant_values=-1), place * block_len, table_width
    )
    bucket_ids = jnp.arange(bucket_count, dtype=jnp.int32)

    def table_rows(slot):
        hot = (bucket_ids[:, None] == slot[None, :]).astype(F32)
        rows = lax.dot_general(rel_table, hot, (((0,), (0,)), ((), ())), precision=HIGHEST)
        return hot, rows.reshape(pairs, 2, table_width)

    hot_own, u_own = table_rows(slots)
    hot_loc, u_loc = table_rows(slots_loc)

    lane = jnp.arange(LANES) % (LANES // 2)

    def penalty(seg):
        seg = seg.astype(jnp.int32)
        return jnp.where((lane < 4)[None, :] & (lane[None, :] != seg[:, None]), -1e30, 0.0).astype(BF16)

    def member(seg):
        return (lane[None, :] == seg.astype(jnp.int32)[:, None]).astype(BF16)

    qa_own, ka_own = penalty(seg_own), member(seg_own)
    qa_loc, ka_all = penalty(segment_ids[shared]), member(seg_all)

    zeros = jnp.zeros((width,), F32)
    proj_bias = jnp.broadcast_to(
        jnp.concatenate([biases[0], zeros, biases[1]])[None, :], (8, 3 * width)
    )
    qkv_own, q_loc, kv_all = project(x_own, x_all, x_loc, qkv_full, proj_bias)
    pair_rows = lambda v: v.reshape(pairs, 2, -1)
    own_cols = (0, pairs, 2 * pairs)
    loc_cols = (0, 0, pairs)
    att_own, atth_own, lse_own = attend_forward(
        u_own, qkv_own, qkv_own, qkv_own, qa_own, ka_own, pair_rows(g_own), own_cols, frames, True
    )
    att_loc, atth_loc, lse_loc = attend_forward(
        u_loc, q_loc, kv_all, kv_all, qa_loc, ka_all, pair_rows(g_loc), loc_cols, frames, False
    )
    vec = jnp.stack(
        [biases[2], biases[3], biases[4], biases[5], gains[0], gains[1], zeros, zeros]
    )
    h_own, h_loc, ga_own, ga_loc, g1_own, g1_loc, rest_grad, sums, up_bias_grad = layer_rest(
        (x_own, x_loc), (atth_own, atth_loc), (c_own, c_loc), rest_full,
        2 * chunks, 0, chunks, vec, up_bias_rows,
    )

    def send_home(own, mine):
        blocks = own.reshape(cycle, block_len, width)
        out = jnp.zeros((row_count, block_len, width), own.dtype)
        out = lax.dynamic_update_index_in_dim(out, mine, shared, 0)
        for s in range(cycle):
            part = take(blocks, (place + s) % cycle)
            got = part if s == 0 else hop(part, s)
            out = lax.dynamic_update_index_in_dim(out, got, (place - s) % cycle, 0)
        return out

    hidden_out = send_home(h_own, h_loc)
    rest_sum = lax.psum_scatter(rest_grad, every, scatter_dimension=0, tiled=True)

    dq_loc, dkv_all, gate_loc, diag_loc = attend_backward(
        u_loc, q_loc, kv_all, kv_all, ga_loc, att_loc, qa_loc, ka_all, pair_rows(g_loc), lse_loc, loc_cols
    )
    part_all, dx_loc = shared_input(dq_loc, dkv_all, qkv_full)
    part_blocks = part_all.reshape(cycle, block_len, width)
    for s in range(cycle):
        part = take(part_blocks, (place + s) % cycle)
        dx_loc = dx_loc + (part if s == 0 else hop(part, s)).astype(F32)

    dq_own, dkv_own, gate_own, diag_own = attend_backward(
        u_own, qkv_own, qkv_own, qkv_own, ga_own, att_own, qa_own, ka_own, pair_rows(g_own), lse_own, own_cols
    )

    def gate_back(grad, a, b, x):
        grad = grad.reshape(heads, -1)
        c = gate_scale[:, None]
        da = grad * (b * c - 1.0) * a * (1.0 - a)
        db = grad * a * c * b * (1.0 - b)
        d = jnp.concatenate([da, db], axis=0)
        dx = lax.dot_general(d, dirs, (((0,), (1,)), ((), ())), precision=HIGHEST)
        dw = jnp.dot(d, x.astype(F32), precision=HIGHEST)
        return dx, dw, jnp.sum(grad * a * b, axis=1)

    gx_own, gw_own, gs_own = gate_back(gate_own, a_own, b_own, x_own)
    gx_loc, gw_loc, gs_loc = gate_back(gate_loc, a_loc, b_loc, x_loc)
    dx_own, qkv_grad, tail_sums = tail(
        x_own, x_all, x_loc, dq_own, dkv_own, dq_loc, dkv_all, qkv_full, g1_own + gx_own
    )
    grad_input = send_home(dx_own, (dx_loc + g1_loc + gx_loc).astype(BF16))

    dw = (gw_own + gw_loc).reshape(2, heads, heads, head_dim)
    dw = jnp.einsum("sggd->sd", dw)
    gate_weight_grad = jnp.broadcast_to(dw[:, None, :], (2, 4, head_dim)).reshape(8, head_dim).T
    diag = lambda hot, d: jnp.dot(hot, d.reshape(heads, -1).T, precision=HIGHEST)
    table_grad = diag(hot_own, diag_own) + diag(hot_loc, diag_loc)
    table_sum, gate_weight_sum, gate_scale_sum = lax.psum(
        (table_grad, gate_weight_grad, gs_own + gs_loc), every
    )

    small_grad = jnp.concatenate(
        [tail_sums[0:2], sums[2:8], up_bias_grad], axis=0
    ).T
    small_grad = jnp.pad(small_grad, ((0, 0), (0, SMALL - small_grad.shape[1]))).astype(BF16)
    last_sum = lax.psum_scatter(
        jnp.concatenate([qkv_grad, small_grad], axis=1), every, scatter_dimension=0, tiled=True
    ).astype(F32)
    rest_sum = rest_sum.astype(F32)
    up_sum = rest_sum.reshape(local_rows, 2 * chunks + 1, width)
    grad_down = up_sum[:, 0 : 2 * chunks : 2].reshape(local_rows * chunks, width)
    grad_up = up_sum[:, 1 : 2 * chunks : 2].transpose(0, 2, 1).reshape(local_rows, inner_width)
    grad_out = up_sum[:, 2 * chunks]
    extra_sum = last_sum[:, 3 * width :]
    return (
        hidden_out,
        grad_input,
        last_sum[:, : 3 * width],
        grad_out,
        grad_up,
        grad_down,
        extra_sum[:, 0:6],
        extra_sum[:, 6:8],
        extra_sum[:, 8 : 8 + chunks].reshape(-1),
        table_sum,
        gate_weight_sum,
        gate_scale_sum,
    )


def solution(mesh):
    placed = (
        P("rows", "blk", None),
        P("rows", "blk"),
        P(),
        P(("rows", "blk"), None),
        P(("rows", "blk"), None),
        P(("rows", "blk"), None),
        P(("rows", "blk"), None),
        P(("rows", "blk"), None),
        P(("rows", "blk"), None),
        P(("rows", "blk")),
        P(),
        P(),
        P(),
        P("rows", "blk", None),
    )
    return jax.shard_map(
        shards,
        mesh=mesh,
        in_specs=placed,
        out_specs=(
            P("rows", "blk", None),
            P("rows", "blk", None),
            P(("rows", "blk"), None),
            P(("rows", "blk"), None),
            P(("rows", "blk"), None),
            P(("rows", "blk"), None),
            P(("rows", "blk"), None),
            P(("rows", "blk"), None),
            P(("rows", "blk")),
            P(),
            P(),
            P(),
        ),
        check_vma=False,
    )
```

```python
import functools

import jax
import jax.numpy as jnp
from jax import lax
from jax.experimental import pallas as pl
from jax.experimental.pallas import tpu as pltpu
from jax.sharding import PartitionSpec as P

EPS_NORM = 1e-05
LANES = 128
SMALL = 128
BF16 = jnp.bfloat16
F32 = jnp.float32
NN = (((1,), (0,)), ((), ()))
NT = (((1,), (1,)), ((), ()))
TN = (((0,), (0,)), ((), ()))
HIGHEST = lax.Precision.HIGHEST


def dotf(a, b, dims):
    return lax.dot_general(a, b, dims, preferred_element_type=F32)


def tiles_of(total, tile):
    return [(s, min(tile, total - s)) for s in range(0, total, tile)]


ANY_SPEC = pl.BlockSpec(memory_space=pl.ANY)


def ignoring(kernel, inputs, count):
    return lambda *refs: kernel(*refs[:inputs], *refs[inputs + count :])


def cost(us):
    return pl.CostEstimate(flops=int(us * 1.1e9), bytes_accessed=0, transcendentals=0)


SMEM_SPEC = pl.BlockSpec(memory_space=pltpu.SMEM)


def table_rows_of(u, width):
    return pltpu.roll(jnp.broadcast_to(u, (LANES, width)), 0, 1, stride=1, stride_axis=0)


def forward_kernel(
    tile, flip, u_ref, q_ref, k_ref, v_ref, qa_ref, ka_ref, g_ref, _o, _ob,
    o_ref, ob_ref, lse_ref, t_scr,
):
    nq, nk, width = q_ref.shape[0], k_ref.shape[0], u_ref.shape[-1]
    pair = pl.program_id(0)
    half = LANES // 2
    shift = -(-nk // LANES)
    low = lax.broadcasted_iota(jnp.int32, (1, LANES), 1) < half
    low_rows = lax.broadcasted_iota(jnp.int32, (LANES, 1), 0) < half
    k, v, q = k_ref[...], v_ref[...], q_ref[...]
    zero = jnp.zeros((), BF16)
    khs, qhs, vzs, gs = [], [], [], []
    for hh in range(2):
        head = pl.ds(2 * pair + hh, 1)
        t_scr[hh] = table_rows_of(u_ref[head, :], width)
        gs.append(g_ref[head, :])
        sel = low if hh == 0 else jnp.logical_not(low)
        khs.append(jnp.where(sel, k, ka_ref[...]))
        qhs.append(jnp.where(sel, q, qa_ref[...]))
        vzs.append(jnp.where(sel, v, zero))
    vt = v.T if flip else None
    for first, cols in tiles_of(nq, tile):
        total, scales, parts = None, [], []
        for hh in range(2):
            raw = dotf(khs[hh], qhs[hh][first : first + cols], NT)
            g = gs[hh][:, first : first + cols]
            scores, peak = [], None
            for f2, r2 in tiles_of(nk, LANES):
                col = (shift - f2 // LANES) * LANES + first
                s = raw[f2 : f2 + r2] + g * t_scr[hh, 0:r2, col : col + cols]
                top = jnp.max(s, axis=0, keepdims=True)
                peak = top if peak is None else jnp.maximum(peak, top)
                scores.append(s)
            probs, mass = [], None
            for s in scores:
                p = jnp.exp(s - peak)
                part = jnp.sum(p, axis=0, keepdims=True)
                mass = part if mass is None else mass + part
                probs.append(p.astype(BF16))
            lse_ref[pl.ds(2 * pair + hh, 1), first : first + cols] = peak + jnp.log(mass)
            pb = jnp.concatenate(probs, axis=0)
            if flip:
                parts.append(dotf(vt[hh * half : (hh + 1) * half], pb, NN) / mass)
            else:
                x = dotf(pb, vzs[hh], TN)
                total = x if total is None else total + x
                scales.append(1.0 / mass)
        if flip:
            o = jnp.concatenate(parts, axis=0).T
        else:
            o = total * jnp.where(low_rows, scales[0], scales[1]).T
        o_ref[first : first + cols, :] = o
        ob_ref[first : first + cols, :] = o.astype(BF16)


def attend_forward(
    u, q, k, v, qa, ka, g, cols, tile, flip, into, row_block, us, deps=()
):
    nq, nk = qa.shape[0], ka.shape[0]
    heads, width = u.shape
    pairs = heads // 2
    col = lambda c: (lambda p: (0, c + p))
    fix = lambda p: (0, 0)
    out_spec = pl.BlockSpec((nq, LANES), lambda p: (row_block, p))
    return pl.pallas_call(
        ignoring(functools.partial(forward_kernel, tile, flip), 9, len(deps)),
        grid=(pairs,),
        in_specs=[
            pl.BlockSpec(u.shape, fix),
            pl.BlockSpec((nq, LANES), col(cols[0])),
            pl.BlockSpec((nk, LANES), col(cols[1])),
            pl.BlockSpec((nk, LANES), col(cols[2])),
            pl.BlockSpec((nq, LANES), fix),
            pl.BlockSpec((nk, LANES), fix),
            pl.BlockSpec(g.shape, fix),
            ANY_SPEC,
            ANY_SPEC,
        ]
        + [ANY_SPEC] * len(deps),
        out_specs=[out_spec, out_spec, pl.BlockSpec((heads, nq), fix)],
        out_shape=[
            jax.ShapeDtypeStruct(into[0].shape, F32),
            jax.ShapeDtypeStruct(into[1].shape, BF16),
            jax.ShapeDtypeStruct((heads, nq), F32),
        ],
        input_output_aliases={7: 0, 8: 1},
        scratch_shapes=[pltpu.VMEM((2, LANES, width), F32)],
        compiler_params=pltpu.CompilerParams(vmem_limit_bytes=48 * 2**20),
        cost_estimate=cost(us),
        name="attention_forward",
    )(u, q, k, v, qa, ka, g, *into, *deps)


def backward_kernel(
    start, u_ref, q_ref, k_ref, v_ref, do_ref, att_ref, qa_ref, ka_ref, g_ref, lse_ref,
    gate_in, diag_in, dq_ref, dkv_ref, col_ref, gate_ref, diag_ref, t_scr, c_scr,
):
    nq, nk, width = q_ref.shape[0], k_ref.shape[0], u_ref.shape[-1]
    step = pl.program_id(0)
    shift = -(-nk // LANES)

    @pl.when(step == 0)
    def _():
        gate_ref[...] = gate_in[...]
        diag_ref[...] = diag_in[...]

    low = lax.broadcasted_iota(jnp.int32, (1, LANES), 1) < LANES // 2
    k, v, q, do = k_ref[...], v_ref[...], q_ref[...], do_ref[...]
    prod = do.astype(F32) * att_ref[...]
    zero = jnp.zeros((), BF16)
    dq, dk, dv = None, None, None
    for hh in range(2):
        head = pl.ds(2 * (start + step) + hh, 1)
        t_scr[hh] = table_rows_of(u_ref[head, :], width)
        c_scr[hh] = jnp.zeros_like(c_scr[hh])
        sel = low if hh == 0 else jnp.logical_not(low)
        ones = jnp.broadcast_to(jnp.where(sel, 1.0, 0.0), (8, LANES))
        delta = lax.dot_general(ones, prod, NT, precision=HIGHEST, preferred_element_type=F32)[0:1]
        ka = jnp.where(sel, k, ka_ref[...])
        qa = jnp.where(sel, q, qa_ref[...])
        kz, qz, doz = jnp.where(sel, k, zero), jnp.where(sel, q, zero), jnp.where(sel, do, zero)
        lse = lse_ref[head, :]
        g = g_ref[head, :]
        gate = jnp.zeros((1, nq), F32)
        raw = dotf(ka, qa, NT)
        dp = dotf(v, doz, NT)
        ps, ds = [], []
        for first, rows in tiles_of(nk, LANES):
            col = (shift - first // LANES) * LANES
            t = t_scr[hh, 0:rows, col : col + nq]
            p = jnp.exp(raw[first : first + rows] + (g * t - lse))
            d = p * (dp[first : first + rows] - delta)
            gate += jnp.sum(d * t, axis=0, keepdims=True)
            c_scr[hh, 0:rows, col : col + nq] += d * g
            ps.append(p.astype(BF16))
            ds.append(d.astype(BF16))
        pb, db = jnp.concatenate(ps, axis=0), jnp.concatenate(ds, axis=0)
        dk_add, dv_add, dq_add = dotf(db, qz, NN), dotf(pb, doz, NN), dotf(db, kz, TN)
        dk = dk_add if dk is None else dk + dk_add
        dv = dv_add if dv is None else dv + dv_add
        dq = dq_add if dq is None else dq + dq_add
        gate_ref[head, :] = gate
        half = LANES // 2
        acc = c_scr[hh]
        while half >= 8:
            acc = acc[:half] + pltpu.roll(acc[half:], width - half, 1)
            half //= 2
        row = lax.broadcasted_iota(jnp.int32, (8, 1), 0)
        for bit in (1, 2, 4):
            acc = jnp.where((row & bit) != 0, pltpu.roll(acc, width - bit, 1), acc)
        diag_ref[head, :] += jnp.sum(acc, axis=0, keepdims=True)
    dq_ref[...] = (dq.astype(BF16) * (LANES // 2) ** -0.5).astype(BF16)
    dkv_ref[0] = dk.astype(BF16)
    dkv_ref[1] = dv.astype(BF16)
    col_ref[0:1, :] = jnp.sum(dq, axis=0, keepdims=True) * (LANES // 2) ** -0.5
    col_ref[1:2, :] = jnp.sum(dv, axis=0, keepdims=True)


def attend_backward(
    u, q, k, v, do, att, qa, ka, g, lse, gate, diag, cols, row_block, us,
    start=0, count=None, into=(), deps=(),
):
    nq, nk = qa.shape[0], ka.shape[0]
    heads, width = u.shape
    pairs = heads // 2
    count = count or pairs
    col = lambda c: (lambda p: (0, c + start + p))
    row = lambda p: (row_block, start + p)
    fix = lambda p: (0, 0)
    return pl.pallas_call(
        ignoring(functools.partial(backward_kernel, start), 12, len(into) + len(deps)),
        grid=(count,),
        in_specs=[
            pl.BlockSpec(u.shape, fix),
            pl.BlockSpec((nq, LANES), col(cols[0])),
            pl.BlockSpec((nk, LANES), col(cols[1])),
            pl.BlockSpec((nk, LANES), col(cols[2])),
            pl.BlockSpec((nq, LANES), row),
            pl.BlockSpec((nq, LANES), row),
            pl.BlockSpec((nq, LANES), fix),
            pl.BlockSpec((nk, LANES), fix),
            pl.BlockSpec(g.shape, fix),
            pl.BlockSpec(lse.shape, fix),
            pl.BlockSpec(gate.shape, fix),
            pl.BlockSpec(diag.shape, fix),
        ]
        + [ANY_SPEC] * (len(into) + len(deps)),
        out_specs=[
            pl.BlockSpec((nq, LANES), col(0)),
            pl.BlockSpec((2, nk, LANES), lambda p: (0, 0, start + p)),
            pl.BlockSpec((2, LANES), col(0)),
            pl.BlockSpec(gate.shape, fix),
            pl.BlockSpec(diag.shape, fix),
        ],
        out_shape=[
            jax.ShapeDtypeStruct((nq, pairs * LANES), BF16),
            jax.ShapeDtypeStruct((2, nk, pairs * LANES), BF16),
            jax.ShapeDtypeStruct((2, pairs * LANES), F32),
            jax.ShapeDtypeStruct(gate.shape, F32),
            jax.ShapeDtypeStruct(diag.shape, F32),
        ],
        input_output_aliases={12 + i: i for i in range(len(into))},
        scratch_shapes=[pltpu.VMEM((2, LANES, width), F32), pltpu.VMEM((2, LANES, width), F32)],
        compiler_params=pltpu.CompilerParams(vmem_limit_bytes=56 * 2**20),
        cost_estimate=cost(us),
        name="attention_backward",
    )(u, q, k, v, do, att, qa, ka, g, lse, gate, diag, *into, *deps)


def project_own_kernel(x_ref, mine_ref, other_ref, core_ref, out_ref, w_ref, small_ref):
    step = pl.program_id(0)
    width = x_ref.shape[1]
    cut = 3 * width // 2

    def unpack(first, second):
        w_ref[:, 0:cut] = first[:, 0:cut]
        w_ref[:, cut : 2 * cut] = second[:, 0:cut]
        small_ref[...] = first[:, cut : cut + SMALL].astype(F32).T[0 : small_ref.shape[0]]

    @pl.when((step == 0) & (core_ref[0] == 0))
    def _():
        unpack(mine_ref, other_ref)

    @pl.when((step == 0) & (core_ref[0] != 0))
    def _():
        unpack(other_ref, mine_ref)

    bias = jnp.where(step == 0, small_ref[0:1, :], jnp.where(step == 2, small_ref[1:2, :], 0.0))
    scale = jnp.where(step == 0, (LANES // 2) ** -0.5, 1.0)
    w = w_ref[:, pl.ds(pl.multiple_of(step * width, LANES), width)]
    out_ref[...] = ((dotf(x_ref[...], w, NN) + bias) * scale).astype(BF16)


def project_own(x, rows, mine, other, core):
    width = x.shape[1]
    fix = lambda c: (0, 0)
    return pl.pallas_call(
        project_own_kernel,
        grid=(3,),
        in_specs=[
            pl.BlockSpec((rows, width), fix),
            pl.BlockSpec(mine.shape, fix),
            pl.BlockSpec(other.shape, fix),
            SMEM_SPEC,
        ],
        out_specs=[
            pl.BlockSpec((rows, width), lambda c: (0, c)),
            pl.BlockSpec((width, 3 * width), fix),
            pl.BlockSpec((16, width), fix),
        ],
        out_shape=[
            jax.ShapeDtypeStruct((rows, 3 * width), BF16),
            jax.ShapeDtypeStruct((width, 3 * width), BF16),
            jax.ShapeDtypeStruct((16, width), F32),
        ],
        compiler_params=pltpu.CompilerParams(vmem_limit_bytes=48 * 2**20),
        cost_estimate=cost(8),
        name="projection_own",
    )(x, mine, other, core)


def project_shared_kernel(all_ref, loc_ref, w_ref, b_ref, q_out, kv_out):
    step = pl.program_id(0)

    @pl.when(step == 0)
    def _():
        q = dotf(loc_ref[...], w_ref[...], NN) + b_ref[0:1, :]
        q_out[...] = (q * (LANES // 2) ** -0.5).astype(BF16)

    @pl.when(step > 0)
    def _():
        bias = jnp.where(step == 2, b_ref[1:2, :], 0.0)
        kv_out[...] = (dotf(all_ref[...], w_ref[...], NN) + bias).astype(BF16)


def project_shared(x_all, x_loc, weight, small, deps=()):
    n_all, width = x_all.shape
    n_loc = x_loc.shape[0]
    fix = lambda c: (0, 0)
    return pl.pallas_call(
        ignoring(project_shared_kernel, 4, len(deps)),
        grid=(3,),
        in_specs=[
            pl.BlockSpec((n_all, width), fix),
            pl.BlockSpec((n_loc, width), fix),
            pl.BlockSpec((width, width), lambda c: (0, c)),
            pl.BlockSpec(small.shape, fix),
        ]
        + [ANY_SPEC] * len(deps),
        out_specs=[
            pl.BlockSpec((n_loc, width), fix),
            pl.BlockSpec((n_all, width), lambda c: (0, jnp.maximum(c - 1, 0))),
        ],
        out_shape=[
            jax.ShapeDtypeStruct((n_loc, width), BF16),
            jax.ShapeDtypeStruct((n_all, 2 * width), BF16),
        ],
        compiler_params=pltpu.CompilerParams(vmem_limit_bytes=48 * 2**20),
        cost_estimate=cost(5),
        name="projection_shared",
    )(x_all, x_loc, weight, small, *deps)


def gelu_parts(x):
    size = jnp.abs(x)
    t = 1.0 / (1.0 + (0.3275911 * 0.7071067811865476) * size)
    poly = t * (
        0.254829592
        + t * (-0.284496736 + t * (1.421413741 + t * (-1.453152027 + t * 1.061405429)))
    )
    bell = jnp.exp(-0.5 * x * x)
    tail = 0.5 * poly * bell
    phi = jnp.where(x >= 0, 1.0 - tail, tail)
    return x * phi, phi + x * bell * 0.3989422804014327


def mean_last(v):
    return jnp.sum(v, axis=-1, keepdims=True) * (1.0 / v.shape[-1])


def layer_kernel(
    chunks, tile,
    x_ref, a_ref, c_ref, wom_ref, woo_ref, mine_ref, other_ref, vec_ref, core_ref,
    h_ref, ga_ref, g1_ref, keep_ref, send_ref, sums_ref,
    z_scr, r_scr, nh_scr, acc_scr, di_scr, act_scr, der_scr, ih_scr, wo_ref, up_ref, down_ref,
):
    step = pl.program_id(0)
    total, width = x_ref.shape
    half = width // 2
    low_core = core_ref[0] == 0
    high_core = core_ref[0] != 0

    vec = lambda i: vec_ref[i : i + 1, :]

    def over_tiles(body):
        @pl.loop(0, total // tile)
        def _(i):
            body(pl.ds(pl.multiple_of(i * tile, tile), tile))

    def add_sum(row, value):
        sums_ref[row : row + 1, :] += jnp.sum(value, axis=0, keepdims=True)

    def load(ref, is_mine):
        @pl.when(is_mine)
        def _():
            ref[...] = mine_ref[...]

        @pl.when(jnp.logical_not(is_mine))
        def _():
            ref[...] = other_ref[...]

    def emit(is_mine, value, cols=slice(None)):
        @pl.when(is_mine)
        def _():
            keep_ref[:, cols] = value

        @pl.when(jnp.logical_not(is_mine))
        def _():
            send_ref[:, cols] = value

    back = jnp.maximum(step - chunks, 0)
    j = back // 2
    forth = step < chunks
    even = (step >= chunks) & (step < 3 * chunks) & (back % 2 == 0)
    odd = (step >= chunks) & (step < 3 * chunks) & (back % 2 == 1)

    @pl.when(step == 0)
    def _():
        sums_ref[...] = jnp.zeros_like(sums_ref)

        @pl.when(low_core)
        def _():
            wo_ref[:, 0:half] = wom_ref[...]
            wo_ref[:, half:width] = woo_ref[...]

        @pl.when(high_core)
        def _():
            wo_ref[:, 0:half] = woo_ref[...]
            wo_ref[:, half:width] = wom_ref[...]

        def body(here):
            y = dotf(a_ref[here, :], wo_ref[...], NN) + vec(2) + x_ref[here, :].astype(F32)
            y = y - mean_last(y)
            r = lax.rsqrt(mean_last(y * y) + EPS_NORM)
            z = y * r
            z_scr[here, :] = z
            r_scr[here, :] = r
            nh_scr[here, :] = (z * vec(6) + vec(4)).astype(BF16)
            acc_scr[here, :] = jnp.zeros_like(z)

        over_tiles(body)

    @pl.when(forth | odd)
    def _():
        load(up_ref, low_core)

    @pl.when(forth | even)
    def _():
        load(down_ref, high_core)

    @pl.when(forth)
    def _():
        def body(here):
            inner = dotf(nh_scr[here, :], up_ref[...], NN) + vec_ref[pl.ds(8 + step, 1), :]
            act, der = gelu_parts(inner)
            act = act.astype(BF16)
            act_scr[step, here, :] = act
            der_scr[step, here, :] = der.astype(BF16)
            acc_scr[here, :] += dotf(act, down_ref[...], NN)

        over_tiles(body)

    @pl.when(step == chunks)
    def _():
        def body(here):
            v = z_scr[here, :] * vec(6) + vec(4) + acc_scr[here, :] + vec(3)
            v = v - mean_last(v)
            r = lax.rsqrt(mean_last(v * v) + EPS_NORM)
            z = v * r
            h_ref[here, :] = (z * vec(7) + vec(5)).astype(BF16)
            c = c_ref[here, :].astype(F32)
            q = c * vec(7)
            gt = r * (q - mean_last(q) - z * mean_last(q * z))
            acc_scr[here, :] = gt
            di_scr[here, :] = gt.astype(BF16)
            add_sum(3, gt)
            add_sum(5, c)
            add_sum(7, c * z)

        over_tiles(body)

    @pl.when(even)
    def _():
        emit(high_core, dotf(act_scr[j], di_scr[...], TN).astype(BF16))

        def body(here):
            gi = dotf(di_scr[here, :], down_ref[...], NT) * der_scr[j, here, :].astype(F32)
            sums_ref[pl.ds(8 + j, 1), :] += jnp.sum(gi, axis=0, keepdims=True)
            ih_scr[here, :] = gi.astype(BF16)

        over_tiles(body)

    @pl.when(odd)
    def _():
        emit(low_core, dotf(nh_scr[...], ih_scr[...], TN).astype(BF16))

        def body(here):
            acc_scr[here, :] += dotf(ih_scr[here, :], up_ref[...], NT)

        over_tiles(body)

    @pl.when(step == 3 * chunks)
    def _():
        def body(here):
            gn = acc_scr[here, :]
            z = z_scr[here, :]
            q = gn * vec(6)
            g1 = r_scr[here, :] * (q - mean_last(q) - z * mean_last(q * z))
            g1_ref[here, :] = g1
            ah = g1.astype(BF16)
            di_scr[here, :] = ah
            ga_ref[here, :] = dotf(ah, wo_ref[...], NT).astype(BF16)
            add_sum(2, g1)
            add_sum(4, gn)
            add_sum(6, gn * z)

        over_tiles(body)
        out = dotf(a_ref[...], di_scr[...], TN).astype(BF16)
        emit(low_core, out[:, 0:half], slice(0, half))
        emit(high_core, out[:, half:width], slice(0, half))


def layer_rest(x, att, cot, mine, other, vec, core, chunks):
    total, width = x.shape
    fix = lambda s: (0, 0)
    once = pl.Buffered(buffer_count=1)

    def chunk_of(s):
        return jnp.where(s < chunks, s, jnp.clip((s - chunks) // 2, 0, chunks - 1))

    def const(shape):
        return pl.BlockSpec(shape, fix, pipeline_mode=once)

    rows = const((total, width))
    square = (width, width)
    out_half = pl.BlockSpec((width, width // 2), lambda s: (0, 2 * chunks), pipeline_mode=once)
    weight_spec = pl.BlockSpec(square, lambda s: (0, chunk_of(s)))
    grad_spec = pl.BlockSpec(square, lambda s: (0, jnp.maximum(s - chunks, 0) // 2))
    return pl.pallas_call(
        functools.partial(layer_kernel, chunks, 256),
        grid=(3 * chunks + 1,),
        in_specs=[
            rows, rows, rows, out_half, out_half, weight_spec, weight_spec, const(vec.shape), SMEM_SPEC,
        ],
        out_specs=[rows, rows, rows, grad_spec, grad_spec, const(vec.shape)],
        out_shape=[
            jax.ShapeDtypeStruct((total, width), BF16),
            jax.ShapeDtypeStruct((total, width), BF16),
            jax.ShapeDtypeStruct((total, width), F32),
            jax.ShapeDtypeStruct(mine.shape, BF16),
            jax.ShapeDtypeStruct(mine.shape, BF16),
            jax.ShapeDtypeStruct(vec.shape, F32),
        ],
        scratch_shapes=[
            pltpu.VMEM((total, width), F32),
            pltpu.VMEM((total, 1), F32),
            pltpu.VMEM((total, width), BF16),
            pltpu.VMEM((total, width), F32),
            pltpu.VMEM((total, width), BF16),
            pltpu.VMEM((chunks, total, width), BF16),
            pltpu.VMEM((chunks, total, width), BF16),
            pltpu.VMEM((total, width), BF16),
            pltpu.VMEM(square, BF16),
            pltpu.VMEM(square, BF16),
            pltpu.VMEM(square, BF16),
        ],
        compiler_params=pltpu.CompilerParams(vmem_limit_bytes=60 * 2**20),
        cost_estimate=cost(70),
        name="layer_rest",
    )(x, att, cot, mine, other, mine, other, vec, core)


def shared_input_kernel(dq_ref, dkv_ref, w_ref, part_ref, loc_ref, acc):
    step = pl.program_id(0)

    @pl.when(step == 0)
    def _():
        loc_ref[...] = dotf(dq_ref[...], w_ref[...], NT)

    @pl.when(step == 1)
    def _():
        acc[...] = dotf(dkv_ref[...], w_ref[...], NT)

    @pl.when(step == 2)
    def _():
        part_ref[...] = (acc[...] + dotf(dkv_ref[...], w_ref[...], NT)).astype(BF16)


def shared_input(dq, dkv, weight, deps=()):
    n_loc, width = dq.shape
    n_all = dkv.shape[1]
    fix = lambda c: (0, 0)
    return pl.pallas_call(
        ignoring(shared_input_kernel, 3, len(deps)),
        grid=(3,),
        in_specs=[
            pl.BlockSpec((n_loc, width), fix),
            pl.BlockSpec((None, n_all, width), lambda c: (jnp.maximum(c - 1, 0), 0, 0)),
            pl.BlockSpec((width, width), lambda c: (0, c)),
        ]
        + [ANY_SPEC] * len(deps),
        out_specs=[pl.BlockSpec((n_all, width), fix), pl.BlockSpec((n_loc, width), fix)],
        out_shape=[
            jax.ShapeDtypeStruct((n_all, width), BF16),
            jax.ShapeDtypeStruct((n_loc, width), F32),
        ],
        scratch_shapes=[pltpu.VMEM((n_all, width), F32)],
        compiler_params=pltpu.CompilerParams(vmem_limit_bytes=48 * 2**20),
        cost_estimate=cost(5),
        name="shared_input",
    )(dq, dkv, weight, *deps)


def weight_grad_kernel(
    x0_ref, x4_ref, loc_ref, dq_ref, dkv_ref, dq4_ref, dkv4_ref, core_ref, keep_ref, send_ref
):
    step = pl.program_id(0)
    width = x0_ref.shape[1]
    half = width // 2
    cut = 3 * half
    low_core = core_ref[0] == 0
    high_core = core_ref[0] != 0

    def emit(is_mine, cols, value):
        @pl.when(is_mine)
        def _():
            keep_ref[:, cols] = value

        @pl.when(jnp.logical_not(is_mine))
        def _():
            send_ref[:, cols] = value

    @pl.when(step == 0)
    def _():
        grad = dotf(x0_ref[...], dq_ref[...], TN) + dotf(loc_ref[...], dq4_ref[...], TN)
        emit(low_core, slice(0, width), grad.astype(BF16))

    @pl.when(step > 0)
    def _():
        grad = dotf(x0_ref[...], dkv_ref[...], TN) + dotf(x4_ref[...], dkv4_ref[...], TN)
        grad = grad.astype(BF16)

        @pl.when(step == 1)
        def _():
            emit(low_core, slice(width, cut), grad[:, 0:half])
            emit(high_core, slice(0, half), grad[:, half:width])

        @pl.when(step == 2)
        def _():
            emit(high_core, slice(half, cut), grad)


def weight_grad(x_cat, x_all, x_loc, dq, dkv, dq4, dkv4, core, deps=()):
    own, width = dq.shape
    n_all, n_loc = x_all.shape[0], x_loc.shape[0]
    fix = lambda c: (0, 0)
    half = lambda c: (jnp.maximum(c - 1, 0), 0, 0)
    shape = (width, 3 * width // 2)
    return pl.pallas_call(
        ignoring(weight_grad_kernel, 8, len(deps)),
        grid=(3,),
        in_specs=[
            pl.BlockSpec((own, width), fix),
            pl.BlockSpec((n_all, width), fix),
            pl.BlockSpec((n_loc, width), fix),
            pl.BlockSpec((own, width), fix),
            pl.BlockSpec((None, own, width), half),
            pl.BlockSpec((n_loc, width), fix),
            pl.BlockSpec((None, n_all, width), half),
            SMEM_SPEC,
        ]
        + [ANY_SPEC] * len(deps),
        out_specs=[pl.BlockSpec(shape, fix)] * 2,
        out_shape=[jax.ShapeDtypeStruct(shape, BF16)] * 2,
        compiler_params=pltpu.CompilerParams(vmem_limit_bytes=56 * 2**20),
        cost_estimate=cost(10),
        name="projection_weight_grad",
    )(x_cat, x_all, x_loc, dq, dkv, dq4, dkv4, core, *deps)


def own_input_kernel(dq_ref, dkv_ref, w_ref, base_ref, gate_ref, dirs_ref, dx_ref, acc):
    step = pl.program_id(0)

    @pl.when(step == 0)
    def _():
        gate = dotf(gate_ref[...], dirs_ref[...], TN)[0 : acc.shape[0]]
        acc[...] = base_ref[...] + gate + dotf(dq_ref[...], w_ref[...], NT)

    @pl.when(step == 1)
    def _():
        acc[...] += dotf(dkv_ref[...], w_ref[...], NT)

    @pl.when(step == 2)
    def _():
        dx_ref[...] = (acc[...] + dotf(dkv_ref[...], w_ref[...], NT)).astype(BF16)


def own_input(dq, dkv, weight, base, gate, dirs, deps=()):
    own, width = dq.shape
    fix = lambda c: (0, 0)
    return pl.pallas_call(
        ignoring(own_input_kernel, 6, len(deps)),
        grid=(3,),
        in_specs=[
            pl.BlockSpec((own, width), fix),
            pl.BlockSpec((None, own, width), lambda c: (jnp.maximum(c - 1, 0), 0, 0)),
            pl.BlockSpec((width, width), lambda c: (0, c)),
            pl.BlockSpec((own, width), fix),
            pl.BlockSpec(gate.shape, fix),
            pl.BlockSpec(dirs.shape, fix),
        ]
        + [ANY_SPEC] * len(deps),
        out_specs=pl.BlockSpec((own, width), fix),
        out_shape=jax.ShapeDtypeStruct((own, width), BF16),
        scratch_shapes=[pltpu.VMEM((own, width), F32)],
        compiler_params=pltpu.CompilerParams(vmem_limit_bytes=56 * 2**20),
        cost_estimate=cost(8),
        name="own_input",
    )(dq, dkv, weight, base, gate, dirs, *deps)


hold = lax.optimization_barrier


def after(value, *earlier):
    return lax.optimization_barrier((value,) + earlier)[0]


def thirds(v):
    high = v.astype(BF16)
    rest = v - high.astype(F32)
    middle = rest.astype(BF16)
    return high, middle, (rest - middle.astype(F32)).astype(BF16)


def swap(array, axis, bit):
    size = lax.axis_size(axis)
    return lax.ppermute(array, axis, [(i, i ^ (1 << bit)) for i in range(size)])


def swap_places(array, mask):
    return lax.ppermute(array, "blk", [(i, i ^ mask) for i in range(lax.axis_size("blk"))])


def by_place(arrays):
    place = lax.axis_index("blk")
    odd, upper = (place & 1) == 1, (place >> 1) == 1
    near = [jnp.where(odd, arrays[1 - i], arrays[i]) for i in range(2)]
    far = [jnp.where(odd, arrays[3 - i], arrays[2 + i]) for i in range(2)]
    return [jnp.where(upper, f, n) for f, n in zip(far, near)] + [
        jnp.where(upper, n, f) for f, n in zip(far, near)
    ]


def bit_of(axis, bit):
    return (lax.axis_index(axis) >> bit) & 1


def bit_count(axis):
    count = lax.axis_size(axis).bit_length() - 1
    assert 1 << count == lax.axis_size(axis)
    return count


def join(array, axis, bit, position):
    def finish(flight):
        mine, other = flight
        upper = bit_of(axis, bit) == 1
        return jnp.stack(
            [jnp.where(upper, other, mine), jnp.where(upper, mine, other)], axis=position
        )

    return (array, swap(array, axis, bit)), finish


def at_once(step):
    flight, finish = step
    return finish(flight)


def together(steps):
    flights, finishes = zip(*steps)
    return flights, lambda done: [finish(flight) for finish, flight in zip(finishes, done)]


def gather_begin(first, second):
    low = bit_of("rows", 0) == 0
    keep, send = jnp.where(low, first, second), jnp.where(low, second, first)

    def finish(flight):
        mine, got = flight
        return jnp.stack([jnp.where(low, mine, got), jnp.where(low, got, mine)], axis=0)

    return (keep, swap(send, "rows", 0)), finish


def blk_bits():
    return list(reversed(range(bit_count("blk"))))


def gather_blk(part, number):
    return join(part, "blk", blk_bits()[number], 1 + number)


def halves_of(array):
    array = array.reshape(-1, array.shape[-1])
    cut = array.shape[-1] // 2 // LANES * LANES
    return [array[:, :cut], array[:, cut:]]


def orders():
    high = list(range(1, bit_count("rows")))
    return high, high[::-1]


def gather_high(halves, step):
    steps = []
    for half, order in zip(halves, orders()):
        position = sum(1 for other in order[:step] if other > order[step])
        steps.append(join(half, "rows", order[step], position))
    return together(steps)


def whole(halves):
    return jnp.concatenate([h.reshape(-1, h.shape[-1]) for h in halves], axis=-1)


def halve(array, axis, bit, position):
    mine = bit_of(axis, bit)
    keep = lax.dynamic_index_in_dim(array, mine, position, keepdims=False)
    send = lax.dynamic_index_in_dim(array, 1 - mine, position, keepdims=False)

    def finish(flight):
        return (flight[0].astype(F32) + flight[1].astype(F32)).astype(BF16)

    return (keep, swap(send, axis, bit)), finish


def scatter_begin(keep, send):
    def finish(flight):
        return (flight[0].astype(F32) + flight[1].astype(F32)).astype(BF16)

    return (keep, swap(send, "rows", 0)), finish


def scatter_high(halves, step):
    steps = []
    for half, order in zip(halves, orders()):
        left = sorted(order[step:], reverse=True)
        view = half.reshape((2,) * len(left) + (-1, half.shape[-1]))
        steps.append(halve(view, "rows", order[step], left.index(order[step])))
    return together(steps)


def scatter_blk(part, bit):
    count = bit_count("blk")
    part = part.reshape((2,) * (1 + count - bit) + (-1, part.shape[-1]))
    return halve(part, "blk", bit, count - bit)


def scatter_end(part):
    core = bit_of("rows", 0)
    part = part.reshape((2, -1, part.shape[-1]))
    keep = lax.dynamic_index_in_dim(part, core, 0, keepdims=False)
    send = lax.dynamic_index_in_dim(part, 1 - core, 0, keepdims=False)

    def finish(flight):
        keep, got = flight
        low = core == 0
        first, second = jnp.where(low, keep, got), jnp.where(low, got, keep)
        return first.astype(F32), second.astype(F32)

    return (keep, swap(send, "rows", 0)), finish


def exchange_first(blocks):
    upper = bit_of("blk", 1)
    pairs = blocks.reshape((2, 2) + blocks.shape[1:])
    keep = lax.dynamic_index_in_dim(pairs, upper, 0, keepdims=False)
    send = lax.dynamic_index_in_dim(pairs, 1 - upper, 0, keepdims=False)
    return (keep, swap_places(send, 2))


def exchange_second(flight):
    odd = bit_of("blk", 0)
    keep, got = flight
    pick = lambda array, index: lax.dynamic_index_in_dim(array, index, 0, keepdims=False)
    send = jnp.stack([pick(keep, 1 - odd), pick(got, 1 - odd)])
    return (pick(keep, odd), pick(got, odd), swap_places(send, 1))


def exchange_end(flight):
    mine, far, other = flight
    return by_place([mine, other[0], far, other[1]])


def shards(
    hidden_in,
    segment_ids,
    bucket_map,
    qkv_weight,
    out_weight,
    up_weight,
    down_weight,
    bias_cols,
    norm_gains,
    up_bias,
    rel_table,
    gate_weight,
    gate_scale,
    cotangent,
):
    row_count, block_len, width = hidden_in.shape
    heads = gate_scale.shape[0]
    pairs = heads // 2
    head_dim = width // heads
    bucket_count = rel_table.shape[0]
    cycle = lax.axis_size("blk")
    place = lax.axis_index("blk")
    core = bit_of("rows", 0).reshape(1)
    frames = block_len * cycle
    shared = row_count - 1
    used = frames + block_len
    total = -(-used // 256) * 256
    inner_width = up_weight.shape[1]
    chunks = inner_width // width
    local_rows = qkv_weight.shape[0]
    half = width // 2
    cut = 3 * half
    high_steps = len(orders()[0])
    assert row_count == cycle + 1 and cycle == 4

    def take(array, index):
        return lax.dynamic_index_in_dim(array, index, 0, keepdims=False)

    def with_rest(blocks, last):
        return jnp.concatenate(blocks + [last, jnp.zeros((total - used, width), BF16)], axis=0)

    extras = jnp.concatenate(
        [bias_cols, norm_gains, up_bias.reshape(local_rows, chunks)], axis=1
    )
    extras = jnp.pad(extras, ((0, 0), (0, SMALL - extras.shape[1])))
    qkv_part = at_once(
        gather_begin(
            jnp.concatenate([qkv_weight[:, :cut], extras], axis=1),
            jnp.concatenate([qkv_weight[:, cut:], jnp.zeros_like(extras)], axis=1),
        )
    )
    up_turned = up_weight.reshape(local_rows, width, chunks).transpose(0, 2, 1)
    rest_flight, rest_finish = gather_begin(
        jnp.concatenate([up_turned.reshape(local_rows, inner_width), out_weight[:, :half]], axis=1),
        jnp.concatenate([down_weight.reshape(local_rows, inner_width), out_weight[:, half:]], axis=1),
    )
    hidden_in, segment_ids, rest_flight, qkv_part = hold(
        (hidden_in, segment_ids, rest_flight, qkv_part)
    )
    seg_rows = jnp.pad(segment_ids.astype(BF16), ((0, 0), (0, width - block_len)))

    def with_segment(index):
        tail_rows = jnp.pad(take(seg_rows, index)[None, :], ((0, 15), (0, 0)))
        return jnp.concatenate([take(hidden_in, index), tail_rows], axis=0)

    packs = [with_segment(place ^ s) for s in range(cycle)]
    qkv_flight, qkv_finish = gather_blk(qkv_part, 0)
    packs[1] = swap_places(packs[1], 1)
    qkv_flight, rest_flight = hold((qkv_flight, rest_flight))
    qkv_flight, qkv_finish = gather_blk(qkv_finish(qkv_flight), 1)
    rest_flight, rest_finish = gather_blk(rest_finish(rest_flight), 0)
    qkv_part = qkv_finish(qkv_flight)
    qkv_halves = halves_of(qkv_part)
    for step in range(high_steps - 2):
        qkv_halves = at_once(gather_high(qkv_halves, step))
    qkv_flight, qkv_finish = gather_high(qkv_halves, high_steps - 2)
    qkv_flight, rest_flight, packs = hold((qkv_flight, rest_flight, packs))
    packs[2], packs[3] = swap_places(packs[2], 2), swap_places(packs[3], 3)
    qkv_flight, qkv_finish = gather_high(qkv_finish(qkv_flight), high_steps - 1)
    rest_flight, rest_finish = gather_blk(rest_finish(rest_flight), 1)
    qkv_flight, rest_flight = hold((qkv_flight, rest_flight))
    qkv_mine = whole(qkv_finish(qkv_flight))
    qkv_other = swap(qkv_mine, "rows", 0)
    rest_halves = halves_of(rest_finish(rest_flight))
    for step in range(high_steps - 2):
        rest_halves = at_once(gather_high(rest_halves, step))
    rest_flight, rest_finish = gather_high(rest_halves, high_steps - 2)
    shared_pack = with_segment(shared)
    packs, qkv_mine, shared_pack = hold((packs, qkv_mine, shared_pack))
    shared_flight, shared_finish = join(shared_pack, "blk", 1, 0)
    x_loc = hidden_in[shared]
    x_cat = with_rest(by_place([p[:block_len] for p in packs]), x_loc)
    seg_own = jnp.concatenate(by_place([p[block_len, :block_len] for p in packs]))

    gate_weight, bucket_map, _ = hold((gate_weight, bucket_map, qkv_part))
    first_dir = jnp.sum(gate_weight[:, :4], axis=1)
    second_dir = jnp.sum(gate_weight[:, 4:], axis=1)
    picks = jnp.repeat(jnp.eye(heads, dtype=F32), head_dim, axis=0)
    dirs = jnp.concatenate(
        [picks * jnp.tile(first_dir, heads)[:, None], picks * jnp.tile(second_dir, heads)[:, None]],
        axis=1,
    ).T
    gate_count = 2 * heads
    dirs_high, dirs_middle, dirs_low = thirds(dirs)
    logits = dotf(jnp.concatenate([dirs_high, dirs_middle, dirs_low], axis=0), x_cat, NT)
    logits = logits[:gate_count] + (
        logits[gate_count : 2 * gate_count] + logits[2 * gate_count :]
    )
    sig = jax.nn.sigmoid(logits)
    gate_a, gate_b = sig[:heads], sig[heads:]
    gating = gate_a * (gate_b * gate_scale[:, None] - 1.0) + 2.0
    g_own, g_loc = gating[:, :frames], gating[:, frames:used]

    shift = -(-frames // LANES)
    span = 2 * frames - 1
    lead = shift * LANES - (frames - 1)
    table_width = 2 * shift * LANES
    slots = jnp.pad(bucket_map[::-1], (lead, table_width - lead - span), constant_values=-1)
    bucket_ids = jnp.arange(bucket_count, dtype=jnp.int32)
    hot = (bucket_ids[:, None] == slots[None, :]).astype(F32)
    u_own = lax.dot_general(rel_table, hot, (((0,), (0,)), ((), ())), precision=HIGHEST)
    narrow = -(-(shift * LANES + block_len) // LANES) * LANES
    u_loc = lax.dynamic_slice_in_dim(
        jnp.pad(u_own, ((0, 0), (0, frames))), place * block_len, narrow, 1
    )

    lane = jnp.arange(LANES) % (LANES // 2)

    def penalty(seg):
        seg = seg.astype(jnp.int32)
        return jnp.where((lane < 4)[None, :] & (lane[None, :] != seg[:, None]), -1e30, 0.0).astype(BF16)

    def member(seg):
        return (lane[None, :] == seg.astype(jnp.int32)[:, None]).astype(BF16)

    qa_own, ka_own = penalty(seg_own), member(seg_own)

    own_cols = (0, pairs, 2 * pairs)
    loc_cols = (0, 0, pairs)
    qkv_own, qkv_full, small = project_own(x_cat, frames, qkv_mine, qkv_other, core)
    rest_flight, shared_flight, qkv_own, small, cotangent = hold(
        (rest_flight, shared_flight, qkv_own, small, cotangent)
    )
    rest_flight, rest_finish = gather_high(rest_finish(rest_flight), high_steps - 1)
    shared_flight, shared_finish = join(shared_finish(shared_flight), "blk", 0, 1)
    cot_flight = exchange_first(cotangent[:cycle])
    into = (jnp.zeros((total, width), F32), jnp.zeros((total, width), BF16))
    att, att_half, lse_own = attend_forward(
        u_own, qkv_own, qkv_own, qkv_own, qa_own, ka_own, g_own, own_cols, frames, True, into, 0, 18,
    )
    shared_flight, cot_flight, rest_flight, att, att_half, lse_own = hold(
        (shared_flight, cot_flight, rest_flight, att, att_half, lse_own)
    )
    rest_mine = whole(rest_finish(rest_flight))
    rest_other = swap(rest_mine, "rows", 0)
    cot_flight = exchange_second(cot_flight)
    shared_pack = shared_finish(shared_flight).reshape((cycle, -1, width))
    x_all = shared_pack[:, :block_len].reshape(frames, width)
    seg_all = shared_pack[:, block_len, :block_len].reshape(frames)
    qa_loc, ka_all = penalty(segment_ids[shared]), member(seg_all)
    q_loc, kv_all = project_shared(x_all, x_loc, qkv_full, small, (rest_mine,))
    att, att_half, lse_loc = attend_forward(
        u_loc, q_loc, kv_all, kv_all, qa_loc, ka_all, g_loc, loc_cols, frames, False,
        (att, att_half), cycle, 8,
    )
    cot_flight, rest_other, att, att_half, lse_loc = hold(
        (cot_flight, rest_other, att, att_half, lse_loc)
    )
    c_cat = with_rest(exchange_end(cot_flight), cotangent[shared])
    h_cat, ga_cat, g1_cat, rest_keep, rest_send, sums = layer_rest(
        x_cat, att_half, c_cat, rest_mine, rest_other, small, core, chunks
    )

    def blocks_of(own):
        return own[:frames].reshape(cycle, block_len, width)

    rest_flight, rest_finish = scatter_begin(rest_keep, rest_send)
    hidden_flight = exchange_first(blocks_of(h_cat))
    dq_loc, dkv_all, col_loc, gate_loc, diag_loc = attend_backward(
        u_loc, q_loc, kv_all, kv_all, ga_cat, att, qa_loc, ka_all, g_loc, lse_loc,
        jnp.zeros((heads, block_len), F32), jnp.zeros((heads, narrow), F32), loc_cols, cycle, 16,
    )
    part_all, dx_loc = shared_input(dq_loc, dkv_all, qkv_full)
    rest_flight, part_all, dx_loc, diag_loc = hold((rest_flight, part_all, dx_loc, diag_loc))
    rest_halves = halves_of(rest_finish(rest_flight))
    rest_flight, rest_finish = scatter_high(rest_halves, 0)
    part_flight, part_finish = halve(part_all.reshape(2, 2, block_len, width), "blk", 0, 1)
    diag = lax.dynamic_slice_in_dim(
        jnp.pad(diag_loc, ((0, 0), (frames, table_width))), frames - place * block_len, table_width, 1
    )
    split = pairs - pairs // 3
    into = attend_backward(
        u_own, qkv_own, qkv_own, qkv_own, ga_cat, att, qa_own, ka_own, g_own, lse_own,
        jnp.zeros((heads, frames), F32), diag, own_cols, 0, 26, 0, split, (), (part_all,),
    )
    rest_flight, hidden_flight, part_flight, into = hold(
        (rest_flight, hidden_flight, part_flight, into)
    )
    rest_halves = rest_finish(rest_flight)
    for step in range(1, high_steps):
        rest_flight, rest_finish = scatter_high(rest_halves, step)
        rest_halves = rest_finish(rest_flight) if step < high_steps - 1 else rest_halves
    hidden_flight = exchange_second(hidden_flight)
    part_flight, part_finish = halve(part_finish(part_flight), "blk", 1, 0)
    dq_own, dkv_own, col_own, gate_own, diag = into
    into = attend_backward(
        u_own, qkv_own, qkv_own, qkv_own, ga_cat, att, qa_own, ka_own, g_own, lse_own,
        gate_own, diag, own_cols, 0, 13, split, pairs - split, (dq_own, dkv_own, col_own),
        tuple(rest_halves),
    )
    rest_flight, hidden_flight, part_flight, into = hold(
        (rest_flight, hidden_flight, part_flight, into)
    )
    dq_own, dkv_own, col_own, gate_own, diag = into
    rest_flight, rest_finish = scatter_blk(whole(rest_finish(rest_flight)), 0)

    gate_grad = jnp.concatenate(
        [gate_own, gate_loc, jnp.zeros((heads, total - used), F32)], axis=1
    )
    a, b, c = gate_a, gate_b, gate_scale[:, None]
    da = gate_grad * (b * c - 1.0) * a * (1.0 - a)
    db = gate_grad * a * c * b * (1.0 - b)
    d = jnp.concatenate([da, db], axis=0)
    d_high, d_middle, d_low = thirds(d)
    d_mix = jnp.concatenate([d_high, d_middle, d_high], axis=0)
    dirs_mix = jnp.concatenate([dirs_high, dirs_high, dirs_middle], axis=0)
    dx_own = own_input(dq_own, dkv_own, qkv_full, g1_cat, d_mix, dirs_mix)
    rest_flight, dx_own, hidden_flight, part_flight, sums = hold(
        (rest_flight, dx_own, hidden_flight, part_flight, sums)
    )
    input_flight = exchange_first(blocks_of(dx_own))
    rest_flight, rest_finish = scatter_blk(rest_finish(rest_flight), 1)
    qkv_keep, qkv_send = weight_grad(
        x_cat, x_all, x_loc, dq_own, dkv_own, dq_loc, dkv_all, core, (dx_own,)
    )
    back_flight, back_finish = scatter_begin(qkv_keep, qkv_send)
    diag, d_high, sums, back_flight = hold((diag, d_high, sums, back_flight))

    dw = dotf(jnp.concatenate([d_high, d_middle, d_low], axis=0), x_cat, NN)
    dw = dw[:gate_count] + (dw[gate_count : 2 * gate_count] + dw[2 * gate_count :])
    dw = jnp.einsum("sggd->sd", dw.reshape(2, heads, heads, head_dim))
    scale_grad = jnp.sum(gate_grad * a * b, axis=1)
    table_grad = lax.dot_general(diag, hot, NT, precision=HIGHEST)
    wide = lambda v: jnp.pad(v, ((0, 0), (0, width - v.shape[1])))
    flat = jnp.concatenate(
        [col_own + col_loc, sums[2 : 8 + chunks], wide(table_grad), wide(dw), wide(scale_grad[None])],
        axis=0,
    )
    flat_steps = [("rows", bit) for bit in range(bit_count("rows"))] + [("blk", 0), ("blk", 1)]
    back_halves = halves_of(back_finish(back_flight))
    for step in range(high_steps):
        back_flight, back_finish = scatter_high(back_halves, step)
        flat_other = swap(flat, *flat_steps[step])
        back_flight, flat, flat_other = hold((back_flight, flat, flat_other))
        back_halves, flat = back_finish(back_flight), flat + flat_other
    back_flight, back_finish = scatter_blk(whole(back_halves), 0)
    input_flight, rest_flight, flat = hold((input_flight, rest_flight, flat))
    input_flight = exchange_second(input_flight)
    rest_flight, rest_finish = scatter_end(rest_finish(rest_flight))
    flat_other = swap(flat, *flat_steps[high_steps])
    back_flight, flat, flat_other, rest_flight = hold((back_flight, flat, flat_other, rest_flight))
    flat = flat + flat_other
    back_flight, back_finish = scatter_blk(back_finish(back_flight), 1)
    flat_other = swap(flat, *flat_steps[high_steps + 1])
    back_flight, flat, flat_other = hold((back_flight, flat, flat_other))
    flat = flat + flat_other
    back_flight, back_finish = scatter_end(back_finish(back_flight))
    for step in flat_steps[high_steps + 2 :]:
        flat = flat + swap(flat, *step)
    gate_x = dotf(d_mix[:, frames:used], dirs_mix, TN)
    mine = dx_loc + part_finish(part_flight).astype(F32) + g1_cat[frames:used] + gate_x
    in_rows = lambda flight, last: jnp.stack(exchange_end(flight) + [last])
    hidden_out = in_rows(hidden_flight, h_cat[frames:used])
    grad_input = in_rows(input_flight, mine.astype(BF16))
    rest_first, rest_second = rest_finish(rest_flight)
    last_first, last_second = back_finish(back_flight)
    cols = 8 + chunks
    first_row = (lax.axis_index("rows") * cycle + place) * local_rows
    local_sums = lax.dynamic_slice(flat, (0, first_row), (cols, local_rows)).T
    table_sum = flat[cols : cols + heads, :bucket_count].T
    dw = flat[cols + heads : cols + heads + 2, :head_dim]
    gate_weight_sum = jnp.broadcast_to(dw[:, None, :], (2, 4, head_dim)).reshape(8, head_dim).T
    gate_scale_sum = flat[cols + heads + 2, :heads]

    grad_up = rest_first[:, :inner_width].reshape(local_rows, chunks, width).transpose(0, 2, 1)
    grad_down = rest_second[:, :inner_width].reshape(local_rows * chunks, width)
    return (
        hidden_out,
        grad_input,
        jnp.concatenate([last_first, last_second], axis=1),
        jnp.concatenate([rest_first[:, inner_width:], rest_second[:, inner_width:]], axis=1),
        grad_up.reshape(local_rows, inner_width),
        grad_down,
        local_sums[:, 0:6],
        local_sums[:, 6:8],
        local_sums[:, 8:cols].reshape(-1),
        table_sum,
        gate_weight_sum,
        gate_scale_sum,
    )


def solution(mesh):
    placed = (
        P("rows", "blk", None),
        P("rows", "blk"),
        P(),
        P(("rows", "blk"), None),
        P(("rows", "blk"), None),
        P(("rows", "blk"), None),
        P(("rows", "blk"), None),
        P(("rows", "blk"), None),
        P(("rows", "blk"), None),
        P(("rows", "blk")),
        P(),
        P(),
        P(),
        P("rows", "blk", None),
    )
    return jax.shard_map(
        shards,
        mesh=mesh,
        in_specs=placed,
        out_specs=(
            P("rows", "blk", None),
            P("rows", "blk", None),
            P(("rows", "blk"), None),
            P(("rows", "blk"), None),
            P(("rows", "blk"), None),
            P(("rows", "blk"), None),
            P(("rows", "blk"), None),
            P(("rows", "blk"), None),
            P(("rows", "blk")),
            P(),
            P(),
            P(),
        ),
        check_vma=False,
    )
```

```python
import functools

import jax
import jax.numpy as jnp
from jax import lax
from jax.experimental import pallas as pl
from jax.experimental.pallas import tpu as pltpu
from jax.sharding import PartitionSpec as P

EPS_NORM = 1e-05
LANES = 128
SMALL = 128
BUCKET_ROWS = 384
BF16 = jnp.bfloat16
F32 = jnp.float32
NN = (((1,), (0,)), ((), ()))
NT = (((1,), (1,)), ((), ()))
TN = (((0,), (0,)), ((), ()))
HIGHEST = lax.Precision.HIGHEST


def thirds(v):
    high = v.astype(BF16)
    rest = v - high.astype(F32)
    middle = rest.astype(BF16)
    return high, middle, (rest - middle.astype(F32)).astype(BF16)


def dotf(a, b, dims):
    return lax.dot_general(a, b, dims, preferred_element_type=F32)


def tiles_of(total, tile):
    return [(s, min(tile, total - s)) for s in range(0, total, tile)]


ANY_SPEC = pl.BlockSpec(memory_space=pl.ANY)


def ignoring(kernel, inputs, count):
    return lambda *refs: kernel(*refs[:inputs], *refs[inputs + count :])


def cost(us):
    return pl.CostEstimate(flops=1000, bytes_accessed=1000, transcendentals=0)


SMEM_SPEC = pl.BlockSpec(memory_space=pltpu.SMEM)


def table_rows_of(u, width):
    return pltpu.roll(jnp.broadcast_to(u, (LANES, width)), 0, 1, stride=1, stride_axis=0)


def forward_kernel(
    tile, flip, u_ref, q_ref, k_ref, v_ref, qa_ref, ka_ref, g_ref,
    ob_ref, o_ref, lse_ref, t_scr,
):
    nq, nk, width = q_ref.shape[0], k_ref.shape[0], u_ref.shape[-1]
    pair = pl.program_id(0)
    half = LANES // 2
    shift = -(-nk // LANES)
    low = lax.broadcasted_iota(jnp.int32, (1, LANES), 1) < half
    low_rows = lax.broadcasted_iota(jnp.int32, (LANES, 1), 0) < half
    k, v, q = k_ref[...], v_ref[...], q_ref[...]
    zero = jnp.zeros((), BF16)
    khs, qhs, vzs, gs = [], [], [], []
    for hh in range(2):
        head = pl.ds(2 * pair + hh, 1)
        t_scr[hh] = table_rows_of(u_ref[head, :], width)
        gs.append(g_ref[head, :])
        sel = low if hh == 0 else jnp.logical_not(low)
        khs.append(jnp.where(sel, k, ka_ref[...]))
        qhs.append(jnp.where(sel, q, qa_ref[...]))
        vzs.append(jnp.where(sel, v, zero))
    vt = v.T if flip else None
    for first, cols in tiles_of(nq, tile):
        total, scales, parts = None, [], []
        for hh in range(2):
            raw = dotf(khs[hh], qhs[hh][first : first + cols], NT)
            g = gs[hh][:, first : first + cols]
            scores, peak = [], None
            for f2, r2 in tiles_of(nk, LANES):
                col = (shift - f2 // LANES) * LANES + first
                s = raw[f2 : f2 + r2] + g * t_scr[hh, 0:r2, col : col + cols]
                top = jnp.max(s, axis=0, keepdims=True)
                peak = top if peak is None else jnp.maximum(peak, top)
                scores.append(s)
            probs, mass = [], None
            for s in scores:
                p = jnp.exp(s - peak)
                part = jnp.sum(p, axis=0, keepdims=True)
                mass = part if mass is None else mass + part
                probs.append(p.astype(BF16))
            lse_ref[pl.ds(2 * pair + hh, 1), first : first + cols] = peak + jnp.log(mass)
            pb = jnp.concatenate(probs, axis=0)
            if flip:
                parts.append(dotf(vt[hh * half : (hh + 1) * half], pb, NN) / mass)
            else:
                x = dotf(pb, vzs[hh], TN)
                total = x if total is None else total + x
                scales.append(1.0 / mass)
        if flip:
            o = jnp.concatenate(parts, axis=0).T
        else:
            o = total * jnp.where(low_rows, scales[0], scales[1]).T
        o_ref[first : first + cols, :] = o
        ob_ref[first : first + cols, :] = o.astype(BF16)


def attend_forward(
    u, q, k, v, qa, ka, g, cols, pairs, tile, flip, into, row_block, us, deps=()
):
    nq, nk = qa.shape[0], ka.shape[0]
    heads, width = u.shape
    col = lambda c: (lambda p: (0, c + p))
    fix = lambda p: (0, 0)
    out_spec = pl.BlockSpec((nq, LANES), lambda p: (row_block, p))
    return pl.pallas_call(
        ignoring(functools.partial(forward_kernel, tile, flip), 7, len(into) + len(deps)),
        grid=(pairs,),
        in_specs=[
            pl.BlockSpec(u.shape, fix),
            pl.BlockSpec((nq, LANES), col(cols[0])),
            pl.BlockSpec((nk, LANES), col(cols[1])),
            pl.BlockSpec((nk, LANES), col(cols[2])),
            pl.BlockSpec((nq, LANES), fix),
            pl.BlockSpec((nk, LANES), fix),
            pl.BlockSpec(g.shape, fix),
        ]
        + [ANY_SPEC] * (len(into) + len(deps)),
        out_specs=[out_spec, out_spec, pl.BlockSpec((heads, nq), fix)],
        out_shape=[
            jax.ShapeDtypeStruct(into[0].shape, BF16),
            jax.ShapeDtypeStruct(into[0].shape, F32),
            jax.ShapeDtypeStruct((heads, nq), F32),
        ],
        input_output_aliases={7 + i: i for i in range(len(into))},
        scratch_shapes=[pltpu.VMEM((2, LANES, width), F32)],
        compiler_params=pltpu.CompilerParams(vmem_limit_bytes=40 * 2**20),
        cost_estimate=cost(us),
        name="attention_forward",
    )(u, q, k, v, qa, ka, g, *into, *deps)


def backward_kernel(
    start, begin, u_ref, q_ref, k_ref, v_ref, do_ref, att_ref, qa_ref, ka_ref, g_ref, lse_ref,
    gate_in, diag_in, dq_ref, dkv_ref, col_ref, gate_ref, diag_ref, t_scr, c_scr,
):
    nq, nk, width = q_ref.shape[0], k_ref.shape[0], u_ref.shape[-1]
    step = pl.program_id(0)
    shift = -(-nk // LANES)

    @pl.when(step == 0)
    def _():
        gate_ref[...] = jnp.zeros_like(gate_ref) if begin else gate_in[...]
        diag_ref[...] = diag_in[...]

    low = lax.broadcasted_iota(jnp.int32, (1, LANES), 1) < LANES // 2
    k, v, q, do = k_ref[...], v_ref[...], q_ref[...], do_ref[...]
    prod = do.astype(F32) * att_ref[...]
    zero = jnp.zeros((), BF16)
    dq, dk, dv = None, None, None
    for hh in range(2):
        head = pl.ds(2 * (start + step) + hh, 1)
        t_scr[hh] = table_rows_of(u_ref[head, :], width)
        c_scr[hh] = jnp.zeros_like(c_scr[hh])
        sel = low if hh == 0 else jnp.logical_not(low)
        ones = jnp.broadcast_to(jnp.where(sel, 1.0, 0.0), (8, LANES))
        delta = lax.dot_general(ones, prod, NT, precision=HIGHEST, preferred_element_type=F32)[0:1]
        ka = jnp.where(sel, k, ka_ref[...])
        qa = jnp.where(sel, q, qa_ref[...])
        kz, qz, doz = jnp.where(sel, k, zero), jnp.where(sel, q, zero), jnp.where(sel, do, zero)
        lse = lse_ref[head, :]
        g = g_ref[head, :]
        gate = jnp.zeros((1, nq), F32)
        raw = dotf(ka, qa, NT)
        dp = dotf(v, doz, NT)
        ps, ds = [], []
        for first, rows in tiles_of(nk, LANES):
            col = (shift - first // LANES) * LANES
            t = t_scr[hh, 0:rows, col : col + nq]
            p = jnp.exp(raw[first : first + rows] + (g * t - lse))
            d = p * (dp[first : first + rows] - delta)
            gate += jnp.sum(d * t, axis=0, keepdims=True)
            c_scr[hh, 0:rows, col : col + nq] += d * g
            ps.append(p.astype(BF16))
            ds.append(d.astype(BF16))
        pb, db = jnp.concatenate(ps, axis=0), jnp.concatenate(ds, axis=0)
        dk_add, dv_add, dq_add = dotf(db, qz, NN), dotf(pb, doz, NN), dotf(db, kz, TN)
        dk = dk_add if dk is None else dk + dk_add
        dv = dv_add if dv is None else dv + dv_add
        dq = dq_add if dq is None else dq + dq_add
        gate_ref[head, :] = gate
        half = LANES // 2
        acc = c_scr[hh]
        while half >= 8:
            acc = acc[:half] + pltpu.roll(acc[half:], width - half, 1)
            half //= 2
        row = lax.broadcasted_iota(jnp.int32, (8, 1), 0)
        for bit in (1, 2, 4):
            acc = jnp.where((row & bit) != 0, pltpu.roll(acc, width - bit, 1), acc)
        diag_ref[head, :] += jnp.sum(acc, axis=0, keepdims=True)
    dq_ref[...] = (dq.astype(BF16) * (LANES // 2) ** -0.5).astype(BF16)
    dkv_ref[0] = dk.astype(BF16)
    dkv_ref[1] = dv.astype(BF16)
    col_ref[0:1, :] = jnp.sum(dq, axis=0, keepdims=True) * (LANES // 2) ** -0.5
    col_ref[1:2, :] = jnp.sum(dv, axis=0, keepdims=True)


def attend_backward(
    u, q, k, v, do, att, qa, ka, g, lse, gate, diag, cols, pairs, row_block, us,
    start, count, into=(), deps=(),
):
    nq, nk = qa.shape[0], ka.shape[0]
    heads, width = u.shape
    col = lambda c: (lambda p: (0, c + start + p))
    row = lambda p: (row_block, start + p)
    fix = lambda p: (0, 0)
    return pl.pallas_call(
        ignoring(functools.partial(backward_kernel, start, start == 0), 12, len(into) + len(deps)),
        grid=(count,),
        in_specs=[
            pl.BlockSpec(u.shape, fix),
            pl.BlockSpec((nq, LANES), col(cols[0])),
            pl.BlockSpec((nk, LANES), col(cols[1])),
            pl.BlockSpec((nk, LANES), col(cols[2])),
            pl.BlockSpec((nq, LANES), row),
            pl.BlockSpec((nq, LANES), row),
            pl.BlockSpec((nq, LANES), fix),
            pl.BlockSpec((nk, LANES), fix),
            pl.BlockSpec(g.shape, fix),
            pl.BlockSpec(lse.shape, fix),
            pl.BlockSpec(gate.shape, fix),
            pl.BlockSpec(diag.shape, fix),
        ]
        + [ANY_SPEC] * (len(into) + len(deps)),
        out_specs=[
            pl.BlockSpec((nq, LANES), col(0)),
            pl.BlockSpec((2, nk, LANES), lambda p: (0, 0, start + p)),
            pl.BlockSpec((2, LANES), col(0)),
            pl.BlockSpec(gate.shape, fix),
            pl.BlockSpec(diag.shape, fix),
        ],
        out_shape=[
            jax.ShapeDtypeStruct((nq, pairs * LANES), BF16),
            jax.ShapeDtypeStruct((2, nk, pairs * LANES), BF16),
            jax.ShapeDtypeStruct((2, pairs * LANES), F32),
            jax.ShapeDtypeStruct(gate.shape, F32),
            jax.ShapeDtypeStruct(diag.shape, F32),
        ],
        input_output_aliases={12 + i: i for i in range(len(into))},
        scratch_shapes=[pltpu.VMEM((2, LANES, width), F32), pltpu.VMEM((2, LANES, width), F32)],
        compiler_params=pltpu.CompilerParams(vmem_limit_bytes=60 * 2**20),
        cost_estimate=cost(us),
        name="attention_backward",
    )(u, q, k, v, do, att, qa, ka, g, lse, gate, diag, *into, *deps)


def own_kernel(
    p0_ref, p1_ref, p2_ref, p3_ref, loc_ref, mine_ref, other_ref, dirs_ref, scale_ref, core_ref, place_ref,
    out_ref, w_ref, small_ref, x_ref, qa_ref, ka_ref, ql_ref, kl_ref, ga_ref, gl_ref, g0_ref, g1_ref,
    x_scr, seg_scr, all_scr,
):
    step = pl.program_id(0)
    width = loc_ref.shape[1]
    block = loc_ref.shape[0]
    own = out_ref.shape[0]
    cut = 3 * width // 2
    rows = scale_ref.shape[0]

    lane = lax.broadcasted_iota(jnp.int32, (1, LANES), 1)
    lane = jnp.where(lane >= LANES // 2, lane - LANES // 2, lane).astype(F32)
    penalty = lambda seg: jnp.where((lane < 4.0) & (lane != seg), -1e30, 0.0).astype(BF16)

    def unpack(first, second):
        w_ref[:, 0:cut] = first[:, 0:cut]
        w_ref[:, cut : 2 * cut] = second[:, 0:cut]
        small_ref[...] = first[:, cut : cut + SMALL].astype(F32).T[0 : small_ref.shape[0]]

    def gates(x, ref, value_ref):
        logits = dotf(dirs_ref[...], x, NT)
        count = 2 * rows
        logits = logits[:count] + (logits[count : 2 * count] + logits[2 * count :])
        sig = 1.0 / (1.0 + jnp.exp(-logits))
        a, b = sig[:rows], sig[rows:]
        ref[0] = a
        ref[1] = b
        value_ref[...] = a * (b * scale_ref[...] - 1.0) + 2.0

    @pl.when((step == 0) & (core_ref[0] == 0))
    def _():
        unpack(mine_ref, other_ref)

    @pl.when((step == 0) & (core_ref[0] != 0))
    def _():
        unpack(other_ref, mine_ref)

    @pl.when(step == 0)
    def _():
        for s, ref in enumerate((p0_ref, p1_ref, p2_ref, p3_ref)):
            here = pl.ds(pl.multiple_of((place_ref[0] ^ s) * block, 8), block)
            x_scr[here, :] = ref[0:block, :].astype(F32)
            for row, scr in ((block, seg_scr), (block + 1, all_scr)):
                seg = ref[row : row + 1, 0 : 2 * LANES].astype(F32)
                seg = jnp.broadcast_to(seg, (LANES, 2 * LANES)).T[0:block]
                scr[here, :] = seg
                if s == 0 and row > block:
                    ql_ref[...] = penalty(seg)
        x_scr[own : own + block, :] = loc_ref[...].astype(F32)
        x_scr[own + block :, :] = jnp.zeros((x_scr.shape[0] - own - block, width), F32)
        x_ref[...] = x_scr[...].astype(BF16)
        qa_ref[...] = penalty(seg_scr[...])
        ka_ref[...] = jnp.where(lane == seg_scr[...], 1.0, 0.0).astype(BF16)
        kl_ref[...] = jnp.where(lane == all_scr[...], 1.0, 0.0).astype(BF16)
        gates(x_ref[0:own, :], ga_ref, g0_ref)
        gates(loc_ref[...], gl_ref, g1_ref)

    bias = jnp.where(step == 0, small_ref[0:1, :], jnp.where(step == 2, small_ref[1:2, :], 0.0))
    scale = jnp.where(step == 0, (LANES // 2) ** -0.5, 1.0)
    w = w_ref[:, pl.ds(pl.multiple_of(step * width, LANES), width)]
    out_ref[...] = ((dotf(x_ref[0:own, :], w, NN) + bias) * scale).astype(BF16)


def project_own(packs, loc, mine, other, dirs, scale, core, place, total):
    block, width = loc.shape
    own = len(packs) * block
    rows = scale.shape[0]
    fix = lambda c: (0, 0)
    full = lambda shape: pl.BlockSpec(shape, lambda c: (0,) * len(shape))
    shapes = [
        ((own, 3 * width), BF16),
        ((width, 3 * width), BF16),
        ((16, width), F32),
        ((total, width), BF16),
        ((own, LANES), BF16),
        ((own, LANES), BF16),
        ((block, LANES), BF16),
        ((own, LANES), BF16),
        ((2, rows, own), F32),
        ((2, rows, block), F32),
        ((rows, own), F32),
        ((rows, block), F32),
    ]
    return pl.pallas_call(
        own_kernel,
        grid=(3,),
        in_specs=[full(p.shape) for p in packs]
        + [full(v.shape) for v in (loc, mine, other, dirs, scale)]
        + [SMEM_SPEC, SMEM_SPEC],
        out_specs=[pl.BlockSpec((own, width), lambda c: (0, c))] + [full(s) for s, _ in shapes[1:]],
        out_shape=[jax.ShapeDtypeStruct(s, t) for s, t in shapes],
        scratch_shapes=[pltpu.VMEM((total, width), F32)] + [pltpu.VMEM((own, LANES), F32)] * 2,
        compiler_params=pltpu.CompilerParams(vmem_limit_bytes=40 * 2**20),
        cost_estimate=cost(10),
        name="projection_own",
    )(*packs, loc, mine, other, dirs, scale, core, place)


def project_shared_kernel(all_ref, loc_ref, w_ref, b_ref, q_out, kv_out):
    step = pl.program_id(0)

    @pl.when(step == 0)
    def _():
        q = dotf(loc_ref[...], w_ref[...], NN) + b_ref[0:1, :]
        q_out[...] = (q * (LANES // 2) ** -0.5).astype(BF16)

    @pl.when(step > 0)
    def _():
        bias = jnp.where(step == 2, b_ref[1:2, :], 0.0)
        kv_out[...] = (dotf(all_ref[...], w_ref[...], NN) + bias).astype(BF16)


def project_shared(x_all, x_loc, weight, small, deps=()):
    n_all, width = x_all.shape
    n_loc = x_loc.shape[0]
    fix = lambda c: (0, 0)
    return pl.pallas_call(
        ignoring(project_shared_kernel, 4, len(deps)),
        grid=(3,),
        in_specs=[
            pl.BlockSpec((n_all, width), fix),
            pl.BlockSpec((n_loc, width), fix),
            pl.BlockSpec((width, width), lambda c: (0, c)),
            pl.BlockSpec(small.shape, fix),
        ]
        + [ANY_SPEC] * len(deps),
        out_specs=[
            pl.BlockSpec((n_loc, width), fix),
            pl.BlockSpec((n_all, width), lambda c: (0, jnp.maximum(c - 1, 0))),
        ],
        out_shape=[
            jax.ShapeDtypeStruct((n_loc, width), BF16),
            jax.ShapeDtypeStruct((n_all, 2 * width), BF16),
        ],
        compiler_params=pltpu.CompilerParams(vmem_limit_bytes=16 * 2**20),
        cost_estimate=cost(5),
        name="projection_shared",
    )(x_all, x_loc, weight, small, *deps)


def gelu_parts(x):
    size = jnp.abs(x)
    t = 1.0 / (1.0 + (0.3275911 * 0.7071067811865476) * size)
    poly = t * (
        0.254829592
        + t * (-0.284496736 + t * (1.421413741 + t * (-1.453152027 + t * 1.061405429)))
    )
    bell = jnp.exp(-0.5 * x * x)
    tail = 0.5 * poly * bell
    phi = jnp.where(x >= 0, 1.0 - tail, tail)
    return x * phi, phi + x * bell * 0.3989422804014327


def mean_last(v):
    return jnp.sum(v, axis=-1, keepdims=True) * (1.0 / v.shape[-1])


def layer_kernel(
    chunks, tile,
    x_ref, a_ref, c0_ref, c1_ref, c2_ref, c3_ref, cl_ref, wom_ref, woo_ref, mine_ref, other_ref, vec_ref,
    core_ref, place_ref,
    h_ref, ga_ref, g1_ref, keep_ref, send_ref, sums_ref,
    c_scr, z_scr, r_scr, nh_scr, acc_scr, di_scr, act_scr, der_scr, ih_scr, wo_ref, up_ref, down_ref,
):
    step = pl.program_id(0)
    total, width = x_ref.shape
    half = width // 2
    low_core = core_ref[0] == 0
    high_core = core_ref[0] != 0

    vec = lambda i: vec_ref[i : i + 1, :]

    def over_tiles(body):
        @pl.loop(0, total // tile)
        def _(i):
            body(pl.ds(pl.multiple_of(i * tile, tile), tile))

    def add_sum(row, value):
        sums_ref[row : row + 1, :] += jnp.sum(value, axis=0, keepdims=True)

    def load(ref, is_mine):
        @pl.when(is_mine)
        def _():
            ref[...] = mine_ref[...]

        @pl.when(jnp.logical_not(is_mine))
        def _():
            ref[...] = other_ref[...]

    def emit(is_mine, value, cols=slice(None)):
        @pl.when(is_mine)
        def _():
            keep_ref[:, cols] = value

        @pl.when(jnp.logical_not(is_mine))
        def _():
            send_ref[:, cols] = value

    back = jnp.maximum(step - chunks, 0)
    j = back // 2
    forth = step < chunks
    even = (step >= chunks) & (step < 3 * chunks) & (back % 2 == 0)
    odd = (step >= chunks) & (step < 3 * chunks) & (back % 2 == 1)

    @pl.when(step == 0)
    def _():
        sums_ref[...] = jnp.zeros_like(sums_ref)

        @pl.when(low_core)
        def _():
            wo_ref[:, 0:half] = wom_ref[...]
            wo_ref[:, half:width] = woo_ref[...]

        @pl.when(high_core)
        def _():
            wo_ref[:, 0:half] = woo_ref[...]
            wo_ref[:, half:width] = wom_ref[...]

        def body(here):
            y = dotf(a_ref[here, :], wo_ref[...], NN) + vec(2) + x_ref[here, :].astype(F32)
            y = y - mean_last(y)
            r = lax.rsqrt(mean_last(y * y) + EPS_NORM)
            z = y * r
            z_scr[here, :] = z
            r_scr[here, :] = r
            nh_scr[here, :] = (z * vec(6) + vec(4)).astype(BF16)
            acc_scr[here, :] = jnp.zeros_like(z)

        over_tiles(body)

    @pl.when(forth | odd)
    def _():
        load(up_ref, low_core)

    @pl.when(forth | even)
    def _():
        load(down_ref, high_core)

    @pl.when(forth)
    def _():
        def body(here):
            inner = dotf(nh_scr[here, :], up_ref[...], NN) + vec_ref[pl.ds(8 + step, 1), :]
            act, der = gelu_parts(inner)
            act = act.astype(BF16)
            act_scr[step, here, :] = act
            der_scr[step, here, :] = der.astype(BF16)
            acc_scr[here, :] += dotf(act, down_ref[...], NN)

        over_tiles(body)

    @pl.when(step == chunks)
    def _():
        block = cl_ref.shape[0]
        for s, ref in enumerate((c0_ref, c1_ref, c2_ref, c3_ref)):
            there = pl.ds(pl.multiple_of((place_ref[0] ^ s) * block, 8), block)
            c_scr[there, :] = ref[...].astype(F32)
        c_scr[4 * block : 5 * block, :] = cl_ref[...].astype(F32)
        c_scr[5 * block :, :] = jnp.zeros((total - 5 * block, width), F32)

        def body(here):
            v = z_scr[here, :] * vec(6) + vec(4) + acc_scr[here, :] + vec(3)
            v = v - mean_last(v)
            r = lax.rsqrt(mean_last(v * v) + EPS_NORM)
            z = v * r
            h_ref[here, :] = (z * vec(7) + vec(5)).astype(BF16)
            c = c_scr[here, :]
            q = c * vec(7)
            gt = r * (q - mean_last(q) - z * mean_last(q * z))
            acc_scr[here, :] = gt
            di_scr[here, :] = gt.astype(BF16)
            add_sum(3, gt)
            add_sum(5, c)
            add_sum(7, c * z)

        over_tiles(body)

    @pl.when(even)
    def _():
        emit(high_core, dotf(act_scr[j], di_scr[...], TN).astype(BF16))

        def body(here):
            gi = dotf(di_scr[here, :], down_ref[...], NT) * der_scr[j, here, :].astype(F32)
            sums_ref[pl.ds(8 + j, 1), :] += jnp.sum(gi, axis=0, keepdims=True)
            ih_scr[here, :] = gi.astype(BF16)

        over_tiles(body)

    @pl.when(odd)
    def _():
        emit(low_core, dotf(nh_scr[...], ih_scr[...], TN).astype(BF16))

        def body(here):
            acc_scr[here, :] += dotf(ih_scr[here, :], up_ref[...], NT)

        over_tiles(body)

    @pl.when(step == 3 * chunks)
    def _():
        def body(here):
            gn = acc_scr[here, :]
            z = z_scr[here, :]
            q = gn * vec(6)
            g1 = r_scr[here, :] * (q - mean_last(q) - z * mean_last(q * z))
            g1_ref[here, :] = g1
            ah = g1.astype(BF16)
            di_scr[here, :] = ah
            ga_ref[here, :] = dotf(ah, wo_ref[...], NT).astype(BF16)
            add_sum(2, g1)
            add_sum(4, gn)
            add_sum(6, gn * z)

        over_tiles(body)
        out = dotf(a_ref[...], di_scr[...], TN).astype(BF16)
        emit(low_core, out[:, 0:half], slice(0, half))
        emit(high_core, out[:, half:width], slice(0, half))


def layer_rest(x, att, cot, mine, other, vec, core, place, chunks):
    total, width = x.shape
    fix = lambda s: (0, 0)
    once = pl.Buffered(buffer_count=1)

    def chunk_of(s):
        return jnp.where(s < chunks, s, jnp.clip((s - chunks) // 2, 0, chunks - 1))

    def const(shape):
        return pl.BlockSpec(shape, fix, pipeline_mode=once)

    rows = const((total, width))
    square = (width, width)
    out_half = pl.BlockSpec((width, width // 2), lambda s: (0, 2 * chunks), pipeline_mode=once)
    weight_spec = pl.BlockSpec(square, lambda s: (0, chunk_of(s)))
    grad_spec = pl.BlockSpec(square, lambda s: (0, jnp.maximum(s - chunks, 0) // 2))
    return pl.pallas_call(
        functools.partial(layer_kernel, chunks, 512),
        grid=(3 * chunks + 1,),
        in_specs=[
            rows, rows, *[const(v.shape) for v in cot],
            out_half, out_half, weight_spec, weight_spec, const(vec.shape), SMEM_SPEC, SMEM_SPEC,
        ],
        out_specs=[rows, rows, rows, grad_spec, grad_spec, const(vec.shape)],
        out_shape=[
            jax.ShapeDtypeStruct((total, width), BF16),
            jax.ShapeDtypeStruct((total, width), BF16),
            jax.ShapeDtypeStruct((total, width), F32),
            jax.ShapeDtypeStruct(mine.shape, BF16),
            jax.ShapeDtypeStruct(mine.shape, BF16),
            jax.ShapeDtypeStruct(vec.shape, F32),
        ],
        scratch_shapes=[
            pltpu.VMEM((total, width), F32),
            pltpu.VMEM((total, width), F32),
            pltpu.VMEM((total, 1), F32),
            pltpu.VMEM((total, width), BF16),
            pltpu.VMEM((total, width), F32),
            pltpu.VMEM((total, width), BF16),
            pltpu.VMEM((chunks, total, width), BF16),
            pltpu.VMEM((chunks, total, width), BF16),
            pltpu.VMEM((total, width), BF16),
            pltpu.VMEM(square, BF16),
            pltpu.VMEM(square, BF16),
            pltpu.VMEM(square, BF16),
        ],
        compiler_params=pltpu.CompilerParams(vmem_limit_bytes=60 * 2**20),
        cost_estimate=cost(70),
        name="layer_rest",
    )(x, att, *cot, mine, other, mine, other, vec, core, place)


def settle_kernel(b0_ref, b1_ref, b2_ref, b3_ref, *rest):
    place_ref, out_ref = rest[-2:]
    for s, ref in enumerate((b0_ref, b1_ref, b2_ref, b3_ref)):
        out_ref[place_ref[0] ^ s] = ref[...]
    total = rest[0][...]
    for ref in rest[1:-2]:
        total = total + ref[...].astype(F32)
    out_ref[4] = total.astype(out_ref.dtype)


def settle(blocks, last, last_block, place):
    block, width = blocks[1].shape
    one = pl.BlockSpec((block, width), lambda s: (0, 0))
    return pl.pallas_call(
        settle_kernel,
        grid=(1,),
        in_specs=[one] * 4
        + [pl.BlockSpec((block, width), lambda s: (last_block, 0))] * len(last)
        + [SMEM_SPEC],
        out_specs=pl.BlockSpec((5, block, width), lambda s: (0, 0, 0)),
        out_shape=jax.ShapeDtypeStruct((5, block, width), BF16),
        compiler_params=pltpu.CompilerParams(vmem_limit_bytes=16 * 2**20),
        cost_estimate=cost(2),
        name="settle",
    )(*blocks, *last, place)


def shared_input_kernel(
    dq_ref, dkv_ref, w_ref, base_ref, grad_ref, gate_ref, scale_ref, dirs_ref, part_ref, loc_ref, acc
):
    step = pl.program_id(0)

    @pl.when(step == 0)
    def _():
        mix = gate_mix(grad_ref[...], gate_ref, scale_ref[...])
        loc_ref[...] = base_ref[...] + dotf(mix, dirs_ref[...], TN) + dotf(dq_ref[...], w_ref[...], NT)

    @pl.when(step == 1)
    def _():
        acc[...] = dotf(dkv_ref[...], w_ref[...], NT)

    @pl.when(step == 2)
    def _():
        part_ref[...] = (acc[...] + dotf(dkv_ref[...], w_ref[...], NT)).astype(BF16)


def shared_input(dq, dkv, weight, base, base_block, grad, gate, scale, dirs):
    n_loc, width = dq.shape
    n_all = dkv.shape[1]
    fix = lambda c: (0, 0)
    return pl.pallas_call(
        shared_input_kernel,
        grid=(3,),
        in_specs=[
            pl.BlockSpec((n_loc, width), fix),
            pl.BlockSpec((None, n_all, width), lambda c: (jnp.maximum(c - 1, 0), 0, 0)),
            pl.BlockSpec((width, width), lambda c: (0, c)),
            pl.BlockSpec((n_loc, width), lambda c: (base_block, 0)),
            pl.BlockSpec(grad.shape, fix),
            pl.BlockSpec(gate.shape, lambda c: (0, 0, 0)),
            pl.BlockSpec(scale.shape, fix),
            pl.BlockSpec(dirs.shape, fix),
        ],
        out_specs=[pl.BlockSpec((n_all, width), fix), pl.BlockSpec((n_loc, width), fix)],
        out_shape=[
            jax.ShapeDtypeStruct((n_all, width), BF16),
            jax.ShapeDtypeStruct((n_loc, width), F32),
        ],
        scratch_shapes=[pltpu.VMEM((n_all, width), F32)],
        compiler_params=pltpu.CompilerParams(vmem_limit_bytes=60 * 2**20),
        cost_estimate=cost(5),
        name="shared_input",
    )(dq, dkv, weight, base, grad, gate, scale, dirs)


def weight_grad_kernel(
    x0_ref, x4_ref, loc_ref, dq_ref, dkv_ref, dq4_ref, dkv4_ref, core_ref, keep_ref, send_ref
):
    step = pl.program_id(0)
    width = x0_ref.shape[1]
    half = width // 2
    cut = 3 * half
    low_core = core_ref[0] == 0
    high_core = core_ref[0] != 0

    def emit(is_mine, cols, value):
        @pl.when(is_mine)
        def _():
            keep_ref[:, cols] = value

        @pl.when(jnp.logical_not(is_mine))
        def _():
            send_ref[:, cols] = value

    @pl.when(step == 0)
    def _():
        grad = dotf(x0_ref[...], dq_ref[...], TN) + dotf(loc_ref[...], dq4_ref[...], TN)
        emit(low_core, slice(0, width), grad.astype(BF16))

    @pl.when(step > 0)
    def _():
        grad = dotf(x0_ref[...], dkv_ref[...], TN) + dotf(x4_ref[...], dkv4_ref[...], TN)
        grad = grad.astype(BF16)

        @pl.when(step == 1)
        def _():
            emit(low_core, slice(width, cut), grad[:, 0:half])
            emit(high_core, slice(0, half), grad[:, half:width])

        @pl.when(step == 2)
        def _():
            emit(high_core, slice(half, cut), grad)


def weight_grad(x_cat, x_all, x_loc, dq, dkv, dq4, dkv4, core, deps=()):
    own, width = dq.shape
    n_all, n_loc = x_all.shape[0], x_loc.shape[0]
    fix = lambda c: (0, 0)
    half = lambda c: (jnp.maximum(c - 1, 0), 0, 0)
    shape = (width, 3 * width // 2)
    return pl.pallas_call(
        ignoring(weight_grad_kernel, 8, len(deps)),
        grid=(3,),
        in_specs=[
            pl.BlockSpec((own, width), fix),
            pl.BlockSpec((n_all, width), fix),
            pl.BlockSpec((n_loc, width), fix),
            pl.BlockSpec((own, width), fix),
            pl.BlockSpec((None, own, width), half),
            pl.BlockSpec((n_loc, width), fix),
            pl.BlockSpec((None, n_all, width), half),
            SMEM_SPEC,
        ]
        + [ANY_SPEC] * len(deps),
        out_specs=[pl.BlockSpec(shape, fix)] * 2,
        out_shape=[jax.ShapeDtypeStruct(shape, BF16)] * 2,
        compiler_params=pltpu.CompilerParams(vmem_limit_bytes=24 * 2**20),
        cost_estimate=cost(10),
        name="projection_weight_grad",
    )(x_cat, x_all, x_loc, dq, dkv, dq4, dkv4, core, *deps)


def gate_parts(grad, gate_ref, c):
    a, b = gate_ref[0], gate_ref[1]
    return thirds(grad * (b * c - 1.0) * a * (1.0 - a)), thirds(grad * a * c * b * (1.0 - b))


def gate_mix(grad, gate_ref, c):
    da, db = gate_parts(grad, gate_ref, c)
    return jnp.concatenate([da[0], db[0], da[1], db[1], da[0], db[0]], axis=0)


def gate_kernel(
    grad0_ref, grad1_ref, gate0_ref, gate1_ref, scale_ref, diag0_ref, diag1_ref, slots_ref, x_ref, loc_ref,
    col0_ref, col1_ref, sums_ref, turn_ref, flat_ref,
):
    c = scale_ref[...]
    rows = c.shape[0]
    head_dim = LANES // 2
    turned = diag1_ref[...]
    turned = jnp.concatenate(
        [turned, jnp.zeros((rows, diag0_ref.shape[1] - turned.shape[1]), F32)], axis=1
    )
    diag = diag0_ref[...] + pltpu.roll(turned, turn_ref[0], 1)

    def back(grad_ref, gate_ref, x):
        grad = grad_ref[...]
        da, db = gate_parts(grad, gate_ref, c)
        d = jnp.concatenate([part for pair in zip(da, db) for part in pair], axis=0)
        return dotf(d, x, NN), jnp.sum(grad * gate_ref[0] * gate_ref[1], axis=1, keepdims=True)

    dw0, scale0 = back(grad0_ref, gate0_ref, x_ref[...])
    dw1, scale1 = back(grad1_ref, gate1_ref, loc_ref[...])
    dw = dw0 + dw1
    dw = dw[: 2 * rows] + (dw[2 * rows : 4 * rows] + dw[4 * rows :])
    lane = lax.broadcasted_iota(jnp.int32, dw.shape, 1)
    row = lax.broadcasted_iota(jnp.int32, dw.shape, 0)
    row = jnp.where(row >= rows, row - rows, row) * head_dim
    dw = jnp.where((lane >= row) & (lane < row + head_dim), dw, 0.0)
    buckets = lax.broadcasted_iota(jnp.int32, (BUCKET_ROWS, diag.shape[1]), 0)
    hot = jnp.where(buckets == slots_ref[...], 1.0, 0.0).astype(BF16)
    table = dotf(jnp.concatenate(thirds(diag), axis=0), hot, NT)
    table = table[:rows] + (table[rows : 2 * rows] + table[2 * rows :])
    flat_ref[...] = jnp.zeros_like(flat_ref)
    flat_ref[0:rows, :] = sums_ref[...]
    flat_ref[0:2, :] = col0_ref[...] + col1_ref[...]
    flat_ref[rows : 2 * rows, 0:BUCKET_ROWS] = table
    flat_ref[rows : 2 * rows, BUCKET_ROWS : BUCKET_ROWS + LANES] = jnp.broadcast_to(
        scale0 + scale1, (rows, LANES)
    )
    flat_ref[2 * rows : 2 * rows + 1, :] = jnp.sum(dw[:rows], axis=0, keepdims=True)
    flat_ref[2 * rows + 1 : 2 * rows + 2, :] = jnp.sum(dw[rows:], axis=0, keepdims=True)


def gate_sums(grads, gates, scale, diags, slots, x, loc, cols, sums, turn):
    rows, own = grads[0].shape
    width = x.shape[1]
    full = lambda v: pl.BlockSpec(v.shape, lambda s: (0,) * v.ndim)
    args = [*grads, *gates, scale, *diags, slots, x, loc, *cols, sums, turn]
    specs = [full(v) for v in args[:-1]] + [SMEM_SPEC]
    specs[8] = pl.BlockSpec((own, width), lambda s: (0, 0))
    out = jax.ShapeDtypeStruct((2 * rows + 8, width), F32)
    return pl.pallas_call(
        gate_kernel,
        grid=(1,),
        in_specs=specs,
        out_specs=full(out),
        out_shape=out,
        compiler_params=pltpu.CompilerParams(vmem_limit_bytes=20 * 2**20),
        cost_estimate=cost(4),
        name="gate_sums",
    )(*args)


def own_input_kernel(
    dq_ref, dkv_ref, w_ref, base_ref, grad_ref, gate_ref, scale_ref, dirs_ref, dx_ref, acc
):
    step = pl.program_id(0)

    @pl.when(step == 0)
    def _():
        mix = gate_mix(grad_ref[...], gate_ref, scale_ref[...])
        acc[...] = base_ref[...] + dotf(mix, dirs_ref[...], TN) + dotf(dq_ref[...], w_ref[...], NT)

    @pl.when(step == 1)
    def _():
        acc[...] += dotf(dkv_ref[...], w_ref[...], NT)

    @pl.when(step == 2)
    def _():
        dx_ref[...] = (acc[...] + dotf(dkv_ref[...], w_ref[...], NT)).astype(BF16)


def own_input(dq, dkv, weight, base, grad, gate, scale, dirs, deps=()):
    own, width = dq.shape
    fix = lambda c: (0, 0)
    return pl.pallas_call(
        ignoring(own_input_kernel, 8, len(deps)),
        grid=(3,),
        in_specs=[
            pl.BlockSpec((own, width), fix),
            pl.BlockSpec((None, own, width), lambda c: (jnp.maximum(c - 1, 0), 0, 0)),
            pl.BlockSpec((width, width), lambda c: (0, c)),
            pl.BlockSpec((own, width), fix),
            pl.BlockSpec(grad.shape, fix),
            pl.BlockSpec(gate.shape, lambda c: (0, 0, 0)),
            pl.BlockSpec(scale.shape, fix),
            pl.BlockSpec(dirs.shape, fix),
        ]
        + [ANY_SPEC] * len(deps),
        out_specs=pl.BlockSpec((own, width), fix),
        out_shape=jax.ShapeDtypeStruct((own, width), BF16),
        scratch_shapes=[pltpu.VMEM((own, width), F32)],
        compiler_params=pltpu.CompilerParams(vmem_limit_bytes=20 * 2**20),
        cost_estimate=cost(8),
        name="own_input",
    )(dq, dkv, weight, base, grad, gate, scale, dirs, *deps)


def split_sum_kernel(_bits, keep_ref, got_ref, *outs):
    step = pl.program_id(0)
    cut = outs[0].shape[1]
    total = keep_ref[...] + got_ref[...]
    first, second = total[:, :cut], total[:, cut:]

    def put(here, ref, value):
        @pl.when(here)
        def _():
            ref[...] = value

    put(step // 2 == 0, outs[0], first)
    put(step // 2 == 1, outs[1], first)
    put(step % 2 == 0, outs[2], second)
    put(step % 2 == 1, outs[3], second)


def split_sum(keep, got, bits, cut, parts):
    rows, cols = keep.shape
    block = rows // 4 // parts
    low = lambda s, bits: (s // 2) ^ bits[0]
    high = lambda s, bits: (s % 2) ^ bits[1]
    wide = pl.BlockSpec(
        (block, cols), lambda s, t, bits: ((2 * high(s, bits) + low(s, bits)) * parts + t, 0)
    )
    at = lambda index, s, t, first, last: (
        index * parts + jnp.where(s < first, 0, jnp.where(s > last, parts - 1, t)), 0
    )
    stay = lambda s, t, bits: at(jnp.where(s < 2, s, 1) ^ bits[1], s, t, 0, 1)
    go = lambda s, t, bits: at(jnp.where(s < 2, 0, s - 2) ^ bits[1], s, t, 2, 3)
    stay_other = lambda s, t, bits: (
        jnp.where(s % 2 == 0, low(s, bits) * parts + t, low(s, bits) * parts + parts - 1), 0
    )
    go_other = lambda s, t, bits: (
        jnp.where(s % 2 == 1, low(s, bits) * parts + t, low(s, bits) * parts), 0
    )
    return pl.pallas_call(
        split_sum_kernel,
        grid_spec=pltpu.PrefetchScalarGridSpec(
            num_scalar_prefetch=1,
            grid=(4, parts),
            in_specs=[wide, wide],
            out_specs=[
                pl.BlockSpec((block, cut), stay),
                pl.BlockSpec((block, cut), go),
                pl.BlockSpec((block, cols - cut), stay_other),
                pl.BlockSpec((block, cols - cut), go_other),
            ],
        ),
        out_shape=[jax.ShapeDtypeStruct((rows // 2, cut), BF16)] * 2
        + [jax.ShapeDtypeStruct((rows // 2, cols - cut), BF16)] * 2,
        compiler_params=pltpu.CompilerParams(vmem_limit_bytes=16 * 2**20),
        cost_estimate=cost(3),
        name="split_sum",
    )(bits, keep, got)


def merge_kernel(_bits, a0_ref, a1_ref, b0_ref, b1_ref, out_ref):
    step = pl.program_id(0)
    cut = a0_ref.shape[1]

    def put(here, cols, ref):
        @pl.when(here)
        def _():
            out_ref[:, cols] = ref[...]

    put(step // 2 == 0, slice(0, cut), a0_ref)
    put(step // 2 == 1, slice(0, cut), a1_ref)
    put(step % 2 == 0, slice(cut, None), b0_ref)
    put(step % 2 == 1, slice(cut, None), b1_ref)


def merge(first, second, bits):
    rows, cut = first[0].shape
    rest = second[0].shape[1]
    block = rows // 2
    low = lambda s, bits: (s % 2) ^ bits[0]
    high = lambda s, bits: (s // 2) ^ bits[1]
    own = lambda s, bits: (jnp.where(s < 2, s % 2, 1) ^ bits[0], 0)
    other = lambda s, bits: (jnp.where(s < 2, 0, s % 2) ^ bits[0], 0)
    beside = lambda s, bits: (high(s, bits), 0)
    return pl.pallas_call(
        merge_kernel,
        grid_spec=pltpu.PrefetchScalarGridSpec(
            num_scalar_prefetch=1,
            grid=(4,),
            in_specs=[
                pl.BlockSpec((block, cut), own),
                pl.BlockSpec((block, cut), other),
                pl.BlockSpec((block, rest), beside),
                pl.BlockSpec((block, rest), beside),
            ],
            out_specs=pl.BlockSpec(
                (block, cut + rest), lambda s, bits: (2 * high(s, bits) + low(s, bits), 0)
            ),
        ),
        out_shape=jax.ShapeDtypeStruct((2 * rows, cut + rest), BF16),
        compiler_params=pltpu.CompilerParams(vmem_limit_bytes=16 * 2**20),
        cost_estimate=cost(3),
        name="merge",
    )(bits, *first, *second)


def split_four_kernel(_own, keep_ref, got_ref, *outs):
    total = keep_ref[...] + got_ref[...]
    for s, ref in enumerate(outs):
        @pl.when(pl.program_id(0) == s)
        def _():
            ref[...] = total


def split_four(keep, got, own):
    rows, cols = keep.shape
    block = rows // 4
    there = pl.BlockSpec((block, cols), lambda s, own: (s ^ own[0], 0))
    return pl.pallas_call(
        split_four_kernel,
        grid_spec=pltpu.PrefetchScalarGridSpec(
            num_scalar_prefetch=1,
            grid=(4,),
            in_specs=[there, there],
            out_specs=[pl.BlockSpec((block, cols), lambda s, own: (0, 0))] * 4,
        ),
        out_shape=[jax.ShapeDtypeStruct((block, cols), BF16)] * 4,
        compiler_params=pltpu.CompilerParams(vmem_limit_bytes=16 * 2**20),
        cost_estimate=cost(2),
        name="split_four",
    )(own, keep, got)


hold = lax.optimization_barrier


def after(value, *earlier):
    return lax.optimization_barrier((value,) + earlier)[0]


def swap(array, axis, bit):
    size = lax.axis_size(axis)
    return lax.ppermute(array, axis, [(i, i ^ (1 << bit)) for i in range(size)])


def swap_places(array, mask):
    return lax.ppermute(array, "blk", [(i, i ^ mask) for i in range(lax.axis_size("blk"))])


def by_place(arrays):
    place = lax.axis_index("blk")
    odd, upper = (place & 1) == 1, (place >> 1) == 1
    near = [jnp.where(odd, arrays[1 - i], arrays[i]) for i in range(2)]
    far = [jnp.where(odd, arrays[3 - i], arrays[2 + i]) for i in range(2)]
    return [jnp.where(upper, f, n) for f, n in zip(far, near)] + [
        jnp.where(upper, n, f) for f, n in zip(far, near)
    ]


def bit_of(axis, bit):
    return (lax.axis_index(axis) >> bit) & 1


def bit_count(axis):
    count = lax.axis_size(axis).bit_length() - 1
    assert 1 << count == lax.axis_size(axis)
    return count


def join(array, axis, bit, position):
    def finish(flight):
        mine, other = flight
        upper = bit_of(axis, bit) == 1
        return jnp.stack(
            [jnp.where(upper, other, mine), jnp.where(upper, mine, other)], axis=position
        )

    return (array, swap(array, axis, bit)), finish


def at_once(step):
    flight, finish = step
    return finish(flight)


def together(steps):
    flights, finishes = zip(*steps)
    return flights, lambda done: [finish(flight) for finish, flight in zip(finishes, done)]


def gather_begin(first, second):
    low = bit_of("rows", 0) == 0
    keep, send = jnp.where(low, first, second), jnp.where(low, second, first)

    def finish(flight):
        mine, got = flight
        return jnp.stack([jnp.where(low, mine, got), jnp.where(low, got, mine)], axis=0)

    return (keep, swap(send, "rows", 0)), finish


def blk_bits():
    return list(reversed(range(bit_count("blk"))))


def gather_blk(part, number):
    return join(part, "blk", blk_bits()[number], 1 + number)


def halves_of(array):
    array = array.reshape(-1, array.shape[-1])
    cut = array.shape[-1] // 2 // LANES * LANES
    return [array[:, :cut], array[:, cut:]]


def orders():
    high = list(range(1, bit_count("rows")))
    return high, high[::-1]


def gather_high(halves, step):
    steps = []
    for half, order in zip(halves, orders()):
        position = sum(1 for other in order[:step] if other > order[step])
        steps.append(join(half, "rows", order[step], position))
    return together(steps)


def gather_last(halves):
    first, second = orders()
    rows = halves[0].reshape(-1, halves[0].shape[-1]).shape[0]
    if len(first) == 2 and rows % 32 == 0:
        flat = [v.reshape(-1, v.shape[-1]) for v in halves]
        flights = [(v, swap(v, "rows", order[1])) for v, order in zip(flat, (first, second))]
        bits = jnp.stack([bit_of("rows", bit) for bit in first])
        return flights, lambda flights: merge(flights[0], flights[1], bits)
    flights, finish = gather_high(halves, len(first) - 1)
    return flights, lambda flights: whole(finish(flights))


def whole(halves):
    return jnp.concatenate([h.reshape(-1, h.shape[-1]) for h in halves], axis=-1)


def added(pair):
    if len(pair) == 1:
        return pair[0]
    return pair[0] + pair[1]


def part_of(pair, index, axis):
    return added([lax.dynamic_index_in_dim(v, index, axis, keepdims=False) for v in pair])


def halve(pair, shape, axis, bit, position):
    pair = [v.reshape(shape + (-1, v.shape[-1])) for v in pair]
    mine = bit_of(axis, bit)
    return part_of(pair, mine, position), swap(part_of(pair, 1 - mine, position), axis, bit)


def scatter_begin(keep, send):
    return keep, swap(send, "rows", 0)


def scatter_first(pair):
    first, second = orders()
    rows, cols = pair[0].shape
    if len(first) == 2 and rows % 128 == 0:
        cut = halves_of(pair[0])[0].shape[1]
        bits = jnp.stack([bit_of("rows", bit) for bit in first])
        keep_a, send_a, keep_b, send_b = split_sum(pair[0], pair[1], bits, cut, 1)
        return [(keep_a, swap(send_a, "rows", first[0])), (keep_b, swap(send_b, "rows", second[0]))]
    return scatter_high([(half,) for half in halves_of(added(pair))], 0)


def scatter_high(halves, step):
    out = []
    for half, order in zip(halves, orders()):
        left = sorted(order[step:], reverse=True)
        out.append(halve(half, (2,) * len(left), "rows", order[step], left.index(order[step])))
    return out


def scatter_whole(halves):
    whole_sum = jnp.concatenate([added([v.reshape(-1, v.shape[-1]) for v in h]) for h in halves], axis=-1)
    return whole_sum


def exchange_first(blocks):
    upper = bit_of("blk", 1)
    pairs = blocks.reshape((2, 2) + blocks.shape[1:])
    keep = lax.dynamic_index_in_dim(pairs, upper, 0, keepdims=False)
    send = lax.dynamic_index_in_dim(pairs, 1 - upper, 0, keepdims=False)
    return (keep, swap_places(send, 2))


def exchange_second(flight):
    odd = bit_of("blk", 0)
    pick = lambda array, index: lax.dynamic_index_in_dim(array, index, 0, keepdims=False)
    send = jnp.stack([pick(array, 1 - odd) for array in flight])
    return (pick(flight[0], odd), pick(flight[1], odd), swap_places(send, 1))


def exchange_end(flight):
    mine, far, other = flight
    return [mine, other[0], far, other[1]]


def total_of(parts):
    return sum(v.astype(F32) for v in parts).astype(BF16)


def scatter_four(pair):
    own = bit_of("rows", 1) + 2 * bit_of("rows", 2)
    blocks = split_four(pair[0], pair[1], own.reshape(1))
    size = lax.axis_size("rows")
    return [blocks[0]] + [
        lax.ppermute(blocks[s], "rows", [(i, i ^ (2 * s)) for i in range(size)]) for s in (1, 2, 3)
    ]


def scatter_places(parts):
    place = lax.axis_index("blk")
    views = [v.reshape((2, 4, -1, v.shape[-1])) for v in parts]
    blocks = [
        total_of([lax.dynamic_index_in_dim(v, place ^ s, 1, keepdims=False) for v in views]) for s in range(4)
    ]
    return [blocks[0]] + [swap_places(blocks[s], s) for s in (1, 2, 3)]


def scatter_blk(pair, bit):
    count = bit_count("blk")
    return halve(pair, (2,) * (1 + count - bit), "blk", bit, count - bit)


def scatter_end(pair):
    core = bit_of("rows", 0)
    pair = [v.reshape((2, -1, v.shape[-1])) for v in pair]
    half = lambda index: total_of([lax.dynamic_index_in_dim(v, index, 0, keepdims=False) for v in pair])
    return half(core), swap(half(1 - core), "rows", 0)


def scatter_done(flight):
    keep, got = flight
    low = bit_of("rows", 0) == 0
    return jnp.where(low, keep, got).astype(F32), jnp.where(low, got, keep).astype(F32)


def shards(
    hidden_in,
    segment_ids,
    bucket_map,
    qkv_weight,
    out_weight,
    up_weight,
    down_weight,
    bias_cols,
    norm_gains,
    up_bias,
    rel_table,
    gate_weight,
    gate_scale,
    cotangent,
):
    row_count, block_len, width = hidden_in.shape
    heads = gate_scale.shape[0]
    pairs = heads // 2
    head_dim = width // heads
    bucket_count = rel_table.shape[0]
    cycle = lax.axis_size("blk")
    place = lax.axis_index("blk")
    core = bit_of("rows", 0).reshape(1)
    frames = block_len * cycle
    shared = row_count - 1
    used = frames + block_len
    total = -(-used // 256) * 256
    inner_width = up_weight.shape[1]
    chunks = inner_width // width
    local_rows = qkv_weight.shape[0]
    half = width // 2
    cut = 3 * half
    high_steps = len(orders()[0])
    assert row_count == cycle + 1 and cycle == 4

    def take(array, index):
        return lax.dynamic_index_in_dim(array, index, 0, keepdims=False)

    def with_rest(blocks, last):
        return jnp.concatenate(blocks + [last, jnp.zeros((total - used, width), BF16)], axis=0)

    extras = jnp.concatenate(
        [bias_cols, norm_gains, up_bias.reshape(local_rows, chunks)], axis=1
    )
    extras = jnp.pad(extras, ((0, 0), (0, SMALL - extras.shape[1])))
    qkv_part = at_once(
        gather_begin(
            jnp.concatenate([qkv_weight[:, :cut], extras], axis=1),
            jnp.concatenate([qkv_weight[:, cut:], jnp.zeros_like(extras)], axis=1),
        )
    )
    up_turned = up_weight.reshape(local_rows, width, chunks).transpose(0, 2, 1)
    rest_flight, rest_finish = gather_begin(
        jnp.concatenate([up_turned.reshape(local_rows, inner_width), out_weight[:, :half]], axis=1),
        jnp.concatenate([down_weight.reshape(local_rows, inner_width), out_weight[:, half:]], axis=1),
    )
    head_rows = -(-heads // 16) * 16
    picks = jnp.repeat(jnp.eye(heads, head_rows, dtype=F32), head_dim, axis=0)
    dirs = [
        picks * jnp.tile(jnp.sum(gate_weight[:, part], axis=1), heads)[:, None]
        for part in (slice(0, 4), slice(4, 8))
    ]
    dirs_high, dirs_middle, dirs_low = thirds(jnp.concatenate(dirs, axis=1).T)
    dirs_all = jnp.concatenate([dirs_high, dirs_middle, dirs_low], axis=0)
    dirs_mix = jnp.concatenate([dirs_high, dirs_high, dirs_middle], axis=0)
    scale_rows = jnp.pad(gate_scale, (0, head_rows - heads))[:, None]

    shift = -(-frames // LANES)
    span = 2 * frames - 1
    lead = shift * LANES - (frames - 1)
    table_width = 2 * shift * LANES
    narrow = -(-(shift * LANES + block_len) // LANES) * LANES
    slots = jnp.pad(bucket_map[::-1], (lead, table_width - lead - span), constant_values=-1)
    hot = (jnp.arange(bucket_count, dtype=jnp.int32)[:, None] == slots[None, :]).astype(F32)

    hidden_in, segment_ids, rest_flight, qkv_part = hold(
        (hidden_in, segment_ids, rest_flight, qkv_part)
    )
    seg_rows = jnp.pad(segment_ids.astype(BF16), ((0, 0), (0, width - block_len)))

    def with_segments(index):
        tail_rows = jnp.pad(jnp.stack([take(seg_rows, index), seg_rows[shared]]), ((0, 14), (0, 0)))
        return jnp.concatenate([take(hidden_in, index), tail_rows], axis=0)

    packs = [with_segments(place ^ s) for s in range(cycle)]
    qkv_flight, qkv_finish = gather_blk(qkv_part, 0)
    qkv_flight, rest_flight = hold((qkv_flight, rest_flight))
    qkv_flight, qkv_finish = gather_blk(qkv_finish(qkv_flight), 1)
    rest_flight, rest_finish = gather_blk(rest_finish(rest_flight), 0)
    qkv_flight, packs, rel_table, hot, cotangent = hold(
        (qkv_flight, packs, rel_table, hot, cotangent)
    )
    cot = [take(cotangent, place ^ s) for s in range(cycle)] + [cotangent[shared]]
    blank = jnp.zeros((total, width), BF16)
    packs[1] = swap_places(packs[1], 1)
    qkv_part = qkv_finish(qkv_flight)
    qkv_halves = halves_of(qkv_part)
    for step in range(high_steps - 2):
        qkv_halves = at_once(gather_high(qkv_halves, step))
    qkv_flight, qkv_finish = gather_high(qkv_halves, high_steps - 2)
    table = jnp.pad(rel_table, ((0, 0), (0, head_rows - heads)))
    u_own = lax.dot_general(table, hot, (((0,), (0,)), ((), ())), precision=HIGHEST)
    u_loc = lax.dynamic_slice_in_dim(
        jnp.pad(u_own, ((0, 0), (0, frames))), place * block_len, narrow, 1
    )
    qkv_flight, rest_flight, packs, cot, blank, u_own, u_loc, dirs_all, x_loc = hold(
        (qkv_flight, rest_flight, packs, cot, blank, u_own, u_loc, dirs_all, hidden_in[shared])
    )
    packs[2], packs[3] = swap_places(packs[2], 2), swap_places(packs[3], 3)
    qkv_flight, qkv_finish = gather_last(qkv_finish(qkv_flight))
    rest_flight, rest_finish = gather_blk(rest_finish(rest_flight), 1)
    qkv_flight, rest_flight, packs = hold((qkv_flight, rest_flight, packs))
    qkv_mine = qkv_finish(qkv_flight)
    qkv_other = swap(qkv_mine, "rows", 0)
    rest_halves = halves_of(rest_finish(rest_flight))
    for step in range(high_steps - 2):
        rest_halves = at_once(gather_high(rest_halves, step))
    rest_flight, rest_finish = gather_high(rest_halves, high_steps - 2)
    shared_flight, shared_finish = join(x_loc, "blk", 1, 0)
    own_cols = (0, pairs, 2 * pairs)
    loc_cols = (0, 0, pairs)
    place_of = place.reshape(1)
    (
        qkv_own, qkv_full, small, x_cat, qa_own, ka_own, qa_loc, ka_all, gate_own, gate_loc, g_own, g_loc,
    ) = project_own(packs, x_loc, qkv_mine, qkv_other, dirs_all, scale_rows, core, place_of, total)
    rest_flight, shared_flight, qkv_own, small, cot = hold(
        (rest_flight, shared_flight, qkv_own, small, cot)
    )
    rest_flight, rest_finish = gather_last(rest_finish(rest_flight))
    shared_flight, shared_finish = join(shared_finish(shared_flight), "blk", 0, 1)
    cot[2], cot[3] = swap_places(cot[2], 2), swap_places(cot[3], 3)
    att_half, att, lse_own = attend_forward(
        u_own, qkv_own, qkv_own, qkv_own, qa_own, ka_own, g_own, own_cols, pairs, frames, True,
        (blank,), 0, 18,
    )
    shared_flight, rest_flight, cot, att, att_half, lse_own = hold(
        (shared_flight, rest_flight, cot, att, att_half, lse_own)
    )
    rest_mine = rest_finish(rest_flight)
    rest_other = swap(rest_mine, "rows", 0)
    x_all = shared_finish(shared_flight).reshape(frames, width)
    q_loc, kv_all = project_shared(x_all, x_loc, qkv_full, small, (rest_mine,))
    cot[1] = swap_places(cot[1], 1)
    att_half, att, lse_loc = attend_forward(
        u_loc, q_loc, kv_all, kv_all, qa_loc, ka_all, g_loc, loc_cols, pairs, frames, False,
        (att_half, att), cycle, 8,
    )
    cot, rest_other, att, att_half, lse_loc = hold((cot, rest_other, att, att_half, lse_loc))
    h_cat, ga_cat, g1_cat, rest_keep, rest_send, sums = layer_rest(
        x_cat, att_half, cot, rest_mine, rest_other, small, core, place_of, chunks
    )

    def blocks_of(own):
        return own[:frames].reshape(cycle, block_len, width)

    rest_flight = scatter_begin(rest_keep, rest_send)
    hidden = [take(blocks_of(h_cat), place ^ s) for s in range(cycle)]
    hidden = [hidden[0]] + [swap_places(hidden[s], s) for s in range(1, cycle)]
    dq_loc, dkv_all, col_loc, grad_loc, diag_loc = attend_backward(
        u_loc, q_loc, kv_all, kv_all, ga_cat, att, qa_loc, ka_all, g_loc, lse_loc,
        g_loc, jnp.zeros((head_rows, narrow), F32), loc_cols, pairs, cycle, 16, 0, pairs,
    )
    part_all, mine = shared_input(
        dq_loc, dkv_all, qkv_full, g1_cat, cycle, grad_loc, gate_loc, scale_rows, dirs_mix
    )
    rest_flight, hidden, part_all = hold((rest_flight, hidden, part_all))
    rest_flight = scatter_first(rest_flight)
    part_flight = halve((part_all,), (2, 2), "blk", 0, 1)
    third = pairs // 3
    into = attend_backward(
        u_own, qkv_own, qkv_own, qkv_own, ga_cat, att, qa_own, ka_own, g_own, lse_own,
        g_own, jnp.zeros((head_rows, table_width), F32), own_cols, pairs, 0, 26, 0, pairs - third, (),
        (rest_flight[0][0], rest_flight[1][0], part_flight[0]),
    )
    rest_flight, part_flight, into = hold((rest_flight, part_flight, into))
    for step in range(1, high_steps):
        rest_flight = scatter_high(rest_flight, step)
    part_flight = halve(part_flight, (2,), "blk", 1, 0)
    dq_own, dkv_own, col_own, grad_own, diag = into
    into = attend_backward(
        u_own, qkv_own, qkv_own, qkv_own, ga_cat, att, qa_own, ka_own, g_own, lse_own,
        grad_own, diag, own_cols, pairs, 0, 13, pairs - third, third, (dq_own, dkv_own, col_own),
        (rest_flight[0][0], rest_flight[1][0]),
    )
    rest_flight, part_flight, into = hold((rest_flight, part_flight, into))
    dq_own, dkv_own, col_own, grad_own, diag = into
    rest_flight = scatter_blk((scatter_whole(rest_flight),), 0)
    flat = gate_sums(
        (grad_own, grad_loc), (gate_own, gate_loc), scale_rows, (diag, diag_loc), slots[None, :], x_cat, x_loc,
        (col_own, col_loc), sums, (place * block_len).reshape(1),
    )
    direct = high_steps == 2 and width % 64 == 0
    upper = [2 * s for s in (1, 2, 3)] if direct else []
    swap_rows = lambda array, mask: lax.ppermute(
        array, "rows", [(i, i ^ mask) for i in range(lax.axis_size("rows"))]
    )
    add_up = lambda arrays: sum(arrays[1:], arrays[0])
    flat_flight = [flat] + [swap_rows(flat, mask) for mask in upper]
    dx_own = own_input(
        dq_own, dkv_own, qkv_full, g1_cat, grad_own, gate_own, scale_rows, dirs_mix, (rest_flight[0], flat)
    )
    flat_flight, dx_own = hold((flat_flight, dx_own))
    flat = add_up(flat_flight)
    flat_flight = (flat, swap(flat, "rows", 0))
    inputs = [take(blocks_of(dx_own), place ^ s) for s in range(cycle)]
    inputs[2] = swap_places(inputs[2], 2)
    qkv_keep, qkv_send = weight_grad(
        x_cat, x_all, x_loc, dq_own, dkv_own, dq_loc, dkv_all, core, (dx_own,)
    )
    rest_flight, flat_flight, qkv_keep, qkv_send, inputs = hold(
        (rest_flight, flat_flight, qkv_keep, qkv_send, inputs)
    )
    back_flight = scatter_begin(qkv_keep, qkv_send)
    flat = add_up(flat_flight)
    flat_flight = (flat, swap_places(flat, 1))
    rest_flight = scatter_blk(rest_flight, 1)
    back_flight, flat_flight = hold((back_flight, flat_flight))
    flat = add_up(flat_flight)
    if direct:
        back_flight = scatter_four(back_flight)
    else:
        back_flight = scatter_first(back_flight)
        for step in range(1, high_steps):
            back_flight = scatter_high(back_flight, step)
    inputs[3], hidden = hold((inputs[3], hidden, back_flight[0]))[:2]
    inputs[3] = swap_places(inputs[3], 3)
    hidden_out = settle(hidden, (h_cat,), cycle, place_of)
    back_flight, rest_flight, inputs, flat, hidden_out = hold(
        (back_flight, rest_flight, inputs, flat, hidden_out)
    )
    if direct:
        back_flight = scatter_places(back_flight)
    else:
        back_flight = scatter_blk(scatter_blk((scatter_whole(back_flight),), 0), 1)
        for bit in range(1, bit_count("rows")):
            flat = flat + swap(flat, "rows", bit)
    inputs[1], flat, rest_flight = hold((inputs[1], flat, rest_flight, back_flight[0]))[:3]
    inputs[1] = swap_places(inputs[1], 1)
    flat_flight = (flat, swap_places(flat, 2))
    back_flight, flat_flight, inputs = hold((back_flight, flat_flight, inputs))
    back_flight = scatter_end(back_flight)
    flat_flight, rest_flight, inputs = hold((flat_flight, rest_flight, inputs, back_flight[0]))[:3]
    rest_flight = scatter_end(rest_flight)
    flat = add_up(flat_flight)
    grad_input = settle(inputs, (mine,) + tuple(part_flight), 0, place_of)
    rest_first, rest_second = scatter_done(rest_flight)
    last_first, last_second = scatter_done(back_flight)
    first_row = (lax.axis_index("rows") * cycle + place) * local_rows
    local_sums = lax.dynamic_slice(flat, (0, first_row), (8 + chunks, local_rows)).T
    table_sum = flat[head_rows : head_rows + heads, :bucket_count].T
    dw = flat[2 * head_rows : 2 * head_rows + 2].reshape(2, heads, head_dim).sum(axis=1)
    gate_weight_sum = jnp.broadcast_to(dw[:, None, :], (2, 4, head_dim)).reshape(8, head_dim).T
    gate_scale_sum = flat[head_rows : head_rows + heads, BUCKET_ROWS]

    grad_up = rest_first[:, :inner_width].reshape(local_rows, chunks, width).transpose(0, 2, 1)
    grad_down = rest_second[:, :inner_width].reshape(local_rows * chunks, width)
    return (
        hidden_out,
        grad_input,
        jnp.concatenate([last_first, last_second], axis=1),
        jnp.concatenate([rest_first[:, inner_width:], rest_second[:, inner_width:]], axis=1),
        grad_up.reshape(local_rows, inner_width),
        grad_down,
        local_sums[:, 0:6],
        local_sums[:, 6:8],
        local_sums[:, 8 : 8 + chunks].reshape(-1),
        table_sum,
        gate_weight_sum,
        gate_scale_sum,
    )


def solution(mesh):
    placed = (
        P("rows", "blk", None),
        P("rows", "blk"),
        P(),
        P(("rows", "blk"), None),
        P(("rows", "blk"), None),
        P(("rows", "blk"), None),
        P(("rows", "blk"), None),
        P(("rows", "blk"), None),
        P(("rows", "blk"), None),
        P(("rows", "blk")),
        P(),
        P(),
        P(),
        P("rows", "blk", None),
    )
    return jax.shard_map(
        shards,
        mesh=mesh,
        in_specs=placed,
        out_specs=(
            P("rows", "blk", None),
            P("rows", "blk", None),
            P(("rows", "blk"), None),
            P(("rows", "blk"), None),
            P(("rows", "blk"), None),
            P(("rows", "blk"), None),
            P(("rows", "blk"), None),
            P(("rows", "blk"), None),
            P(("rows", "blk")),
            P(),
            P(),
            P(),
        ),
        check_vma=False,
    )
```

```python
import functools

import jax
import jax.numpy as jnp
from jax import lax
from jax.experimental import pallas as pl
from jax.experimental.pallas import tpu as pltpu
from jax.sharding import PartitionSpec as P

EPS_NORM = 1e-05
LANES = 128
SMALL = 128
BUCKET_ROWS = 384
BF16 = jnp.bfloat16
F32 = jnp.float32
NN = (((1,), (0,)), ((), ()))
NT = (((1,), (1,)), ((), ()))
TN = (((0,), (0,)), ((), ()))
HIGHEST = lax.Precision.HIGHEST


def thirds(v):
    high = v.astype(BF16)
    rest = v - high.astype(F32)
    middle = rest.astype(BF16)
    return high, middle, (rest - middle.astype(F32)).astype(BF16)


def dotf(a, b, dims):
    return lax.dot_general(a, b, dims, preferred_element_type=F32)


def tiles_of(total, tile):
    return [(s, min(tile, total - s)) for s in range(0, total, tile)]


ANY_SPEC = pl.BlockSpec(memory_space=pl.ANY)


def ignoring(kernel, inputs, count):
    return lambda *refs: kernel(*refs[:inputs], *refs[inputs + count :])


def cost(us):
    return pl.CostEstimate(flops=1000, bytes_accessed=1000, transcendentals=0)


SMEM_SPEC = pl.BlockSpec(memory_space=pltpu.SMEM)


def table_rows_of(u, width):
    return pltpu.roll(jnp.broadcast_to(u, (LANES, width)), 0, 1, stride=1, stride_axis=0)


def forward_kernel(
    tile, flip, u_ref, q_ref, k_ref, v_ref, qa_ref, ka_ref, g_ref,
    ob_ref, o_ref, lse_ref, t_scr,
):
    nq, nk, width = q_ref.shape[0], k_ref.shape[0], u_ref.shape[-1]
    pair = pl.program_id(0)
    half = LANES // 2
    shift = -(-nk // LANES)
    low = lax.broadcasted_iota(jnp.int32, (1, LANES), 1) < half
    low_rows = lax.broadcasted_iota(jnp.int32, (LANES, 1), 0) < half
    k, v, q = k_ref[...], v_ref[...], q_ref[...]
    zero = jnp.zeros((), BF16)
    khs, qhs, vzs, gs = [], [], [], []
    for hh in range(2):
        head = pl.ds(2 * pair + hh, 1)
        t_scr[hh] = table_rows_of(u_ref[head, :], width)
        gs.append(g_ref[head, :])
        sel = low if hh == 0 else jnp.logical_not(low)
        khs.append(jnp.where(sel, k, ka_ref[...]))
        qhs.append(jnp.where(sel, q, qa_ref[...]))
        vzs.append(jnp.where(sel, v, zero))
    vt = v.T if flip else None
    for first, cols in tiles_of(nq, tile):
        total, scales, parts = None, [], []
        for hh in range(2):
            raw = dotf(khs[hh], qhs[hh][first : first + cols], NT)
            g = gs[hh][:, first : first + cols]
            scores, peak = [], None
            for f2, r2 in tiles_of(nk, LANES):
                col = (shift - f2 // LANES) * LANES + first
                s = raw[f2 : f2 + r2] + g * t_scr[hh, 0:r2, col : col + cols]
                top = jnp.max(s, axis=0, keepdims=True)
                peak = top if peak is None else jnp.maximum(peak, top)
                scores.append(s)
            probs, mass = [], None
            for s in scores:
                p = jnp.exp(s - peak)
                part = jnp.sum(p, axis=0, keepdims=True)
                mass = part if mass is None else mass + part
                probs.append(p.astype(BF16))
            lse_ref[pl.ds(2 * pair + hh, 1), first : first + cols] = peak + jnp.log(mass)
            pb = jnp.concatenate(probs, axis=0)
            if flip:
                parts.append(dotf(vt[hh * half : (hh + 1) * half], pb, NN) / mass)
            else:
                x = dotf(pb, vzs[hh], TN)
                total = x if total is None else total + x
                scales.append(1.0 / mass)
        if flip:
            o = jnp.concatenate(parts, axis=0).T
        else:
            o = total * jnp.where(low_rows, scales[0], scales[1]).T
        o_ref[first : first + cols, :] = o
        ob_ref[first : first + cols, :] = o.astype(BF16)


def attend_forward(
    u, q, k, v, qa, ka, g, cols, pairs, tile, flip, into, row_block, us, deps=()
):
    nq, nk = qa.shape[0], ka.shape[0]
    heads, width = u.shape
    col = lambda c: (lambda p: (0, c + p))
    fix = lambda p: (0, 0)
    out_spec = pl.BlockSpec((nq, LANES), lambda p: (row_block, p))
    return pl.pallas_call(
        ignoring(functools.partial(forward_kernel, tile, flip), 7, len(into) + len(deps)),
        grid=(pairs,),
        in_specs=[
            pl.BlockSpec(u.shape, fix),
            pl.BlockSpec((nq, LANES), col(cols[0])),
            pl.BlockSpec((nk, LANES), col(cols[1])),
            pl.BlockSpec((nk, LANES), col(cols[2])),
            pl.BlockSpec((nq, LANES), fix),
            pl.BlockSpec((nk, LANES), fix),
            pl.BlockSpec(g.shape, fix),
        ]
        + [ANY_SPEC] * (len(into) + len(deps)),
        out_specs=[out_spec, out_spec, pl.BlockSpec((heads, nq), fix)],
        out_shape=[
            jax.ShapeDtypeStruct(into[0].shape, BF16),
            jax.ShapeDtypeStruct(into[0].shape, F32),
            jax.ShapeDtypeStruct((heads, nq), F32),
        ],
        input_output_aliases={7 + i: i for i in range(len(into))},
        scratch_shapes=[pltpu.VMEM((2, LANES, width), F32)],
        compiler_params=pltpu.CompilerParams(vmem_limit_bytes=40 * 2**20),
        cost_estimate=cost(us),
        name="attention_forward",
    )(u, q, k, v, qa, ka, g, *into, *deps)


def backward_kernel(
    start, begin, u_ref, q_ref, k_ref, v_ref, do_ref, att_ref, qa_ref, ka_ref, g_ref, lse_ref,
    gate_in, diag_in, dq_ref, dkv_ref, col_ref, gate_ref, diag_ref, t_scr, c_scr,
):
    nq, nk, width = q_ref.shape[0], k_ref.shape[0], u_ref.shape[-1]
    step = pl.program_id(0)
    shift = -(-nk // LANES)

    @pl.when(step == 0)
    def _():
        gate_ref[...] = jnp.zeros_like(gate_ref) if begin else gate_in[...]
        diag_ref[...] = diag_in[...]

    low = lax.broadcasted_iota(jnp.int32, (1, LANES), 1) < LANES // 2
    k, v, q, do = k_ref[...], v_ref[...], q_ref[...], do_ref[...]
    prod = (do.astype(F32) * att_ref[...]).T
    zero = jnp.zeros((), BF16)
    dq, dk, dv = None, None, None
    for hh in range(2):
        head = pl.ds(2 * (start + step) + hh, 1)
        t_scr[hh] = table_rows_of(u_ref[head, :], width)
        c_scr[hh] = jnp.zeros_like(c_scr[hh])
        sel = low if hh == 0 else jnp.logical_not(low)
        delta = jnp.sum(prod[hh * (LANES // 2) : (hh + 1) * (LANES // 2)], axis=0, keepdims=True)
        ka = jnp.where(sel, k, ka_ref[...])
        qa = jnp.where(sel, q, qa_ref[...])
        kz, qz, doz = jnp.where(sel, k, zero), jnp.where(sel, q, zero), jnp.where(sel, do, zero)
        lse = lse_ref[head, :]
        g = g_ref[head, :]
        gate = jnp.zeros((1, nq), F32)
        raw = dotf(ka, qa, NT)
        dp = dotf(v, doz, NT)
        ps, ds = [], []
        for first, rows in tiles_of(nk, LANES):
            col = (shift - first // LANES) * LANES
            t = t_scr[hh, 0:rows, col : col + nq]
            p = jnp.exp(raw[first : first + rows] + (g * t - lse))
            d = p * (dp[first : first + rows] - delta)
            gate += jnp.sum(d * t, axis=0, keepdims=True)
            c_scr[hh, 0:rows, col : col + nq] += d * g
            ps.append(p.astype(BF16))
            ds.append(d.astype(BF16))
        pb, db = jnp.concatenate(ps, axis=0), jnp.concatenate(ds, axis=0)
        dk_add, dv_add, dq_add = dotf(db, qz, NN), dotf(pb, doz, NN), dotf(db, kz, TN)
        dk = dk_add if dk is None else dk + dk_add
        dv = dv_add if dv is None else dv + dv_add
        dq = dq_add if dq is None else dq + dq_add
        gate_ref[head, :] = gate
        half = LANES // 2
        acc = c_scr[hh]
        while half >= 8:
            acc = acc[:half] + pltpu.roll(acc[half:], width - half, 1)
            half //= 2
        row = lax.broadcasted_iota(jnp.int32, (8, 1), 0)
        for bit in (1, 2, 4):
            acc = jnp.where((row & bit) != 0, pltpu.roll(acc, width - bit, 1), acc)
        diag_ref[head, :] += jnp.sum(acc, axis=0, keepdims=True)
    dq_ref[...] = (dq.astype(BF16) * (LANES // 2) ** -0.5).astype(BF16)
    dkv_ref[0] = dk.astype(BF16)
    dkv_ref[1] = dv.astype(BF16)
    col_ref[0:1, :] = jnp.sum(dq, axis=0, keepdims=True) * (LANES // 2) ** -0.5
    col_ref[1:2, :] = jnp.sum(dv, axis=0, keepdims=True)


def attend_backward(
    u, q, k, v, do, att, qa, ka, g, lse, gate, diag, cols, pairs, row_block, us,
    start, count, into=(), deps=(),
):
    nq, nk = qa.shape[0], ka.shape[0]
    heads, width = u.shape
    col = lambda c: (lambda p: (0, c + start + p))
    row = lambda p: (row_block, start + p)
    fix = lambda p: (0, 0)
    return pl.pallas_call(
        ignoring(functools.partial(backward_kernel, start, start == 0), 12, len(into) + len(deps)),
        grid=(count,),
        in_specs=[
            pl.BlockSpec(u.shape, fix),
            pl.BlockSpec((nq, LANES), col(cols[0])),
            pl.BlockSpec((nk, LANES), col(cols[1])),
            pl.BlockSpec((nk, LANES), col(cols[2])),
            pl.BlockSpec((nq, LANES), row),
            pl.BlockSpec((nq, LANES), row),
            pl.BlockSpec((nq, LANES), fix),
            pl.BlockSpec((nk, LANES), fix),
            pl.BlockSpec(g.shape, fix),
            pl.BlockSpec(lse.shape, fix),
            pl.BlockSpec(gate.shape, fix),
            pl.BlockSpec(diag.shape, fix),
        ]
        + [ANY_SPEC] * (len(into) + len(deps)),
        out_specs=[
            pl.BlockSpec((nq, LANES), col(0)),
            pl.BlockSpec((2, nk, LANES), lambda p: (0, 0, start + p)),
            pl.BlockSpec((2, LANES), col(0)),
            pl.BlockSpec(gate.shape, fix),
            pl.BlockSpec(diag.shape, fix),
        ],
        out_shape=[
            jax.ShapeDtypeStruct((nq, pairs * LANES), BF16),
            jax.ShapeDtypeStruct((2, nk, pairs * LANES), BF16),
            jax.ShapeDtypeStruct((2, pairs * LANES), F32),
            jax.ShapeDtypeStruct(gate.shape, F32),
            jax.ShapeDtypeStruct(diag.shape, F32),
        ],
        input_output_aliases={12 + i: i for i in range(len(into))},
        scratch_shapes=[pltpu.VMEM((2, LANES, width), F32), pltpu.VMEM((2, LANES, width), F32)],
        compiler_params=pltpu.CompilerParams(vmem_limit_bytes=60 * 2**20),
        cost_estimate=cost(us),
        name="attention_backward",
    )(u, q, k, v, do, att, qa, ka, g, lse, gate, diag, *into, *deps)


def own_kernel(
    p0_ref, p1_ref, p2_ref, p3_ref, loc_ref, mine_ref, other_ref, dirs_ref, scale_ref, core_ref, place_ref,
    out_ref, w_ref, small_ref, x_ref, qa_ref, ka_ref, ql_ref, kl_ref, ga_ref, gl_ref, g0_ref, g1_ref,
    x_scr, seg_scr, all_scr,
):
    step = pl.program_id(0)
    width = loc_ref.shape[1]
    block = loc_ref.shape[0]
    own = out_ref.shape[0]
    cut = 3 * width // 2
    rows = scale_ref.shape[0]

    lane = lax.broadcasted_iota(jnp.int32, (1, LANES), 1)
    lane = jnp.where(lane >= LANES // 2, lane - LANES // 2, lane).astype(F32)
    penalty = lambda seg: jnp.where((lane < 4.0) & (lane != seg), -1e30, 0.0).astype(BF16)

    def unpack(first, second):
        w_ref[:, 0:cut] = first[:, 0:cut]
        w_ref[:, cut : 2 * cut] = second[:, 0:cut]
        small_ref[...] = first[:, cut : cut + SMALL].astype(F32).T[0 : small_ref.shape[0]]

    def gates(x, ref, value_ref):
        logits = dotf(dirs_ref[...], x, NT)
        count = 2 * rows
        logits = logits[:count] + (logits[count : 2 * count] + logits[2 * count :])
        sig = 1.0 / (1.0 + jnp.exp(-logits))
        a, b = sig[:rows], sig[rows:]
        ref[0] = a
        ref[1] = b
        value_ref[...] = a * (b * scale_ref[...] - 1.0) + 2.0

    @pl.when((step == 0) & (core_ref[0] == 0))
    def _():
        unpack(mine_ref, other_ref)

    @pl.when((step == 0) & (core_ref[0] != 0))
    def _():
        unpack(other_ref, mine_ref)

    @pl.when(step == 0)
    def _():
        for s, ref in enumerate((p0_ref, p1_ref, p2_ref, p3_ref)):
            here = pl.ds(pl.multiple_of((place_ref[0] ^ s) * block, 8), block)
            x_scr[here, :] = ref[0:block, :].astype(F32)
            for row, scr in ((block, seg_scr), (block + 1, all_scr)):
                seg = ref[row : row + 1, 0 : 2 * LANES].astype(F32)
                seg = jnp.broadcast_to(seg, (LANES, 2 * LANES)).T[0:block]
                scr[here, :] = seg
                if s == 0 and row > block:
                    ql_ref[...] = penalty(seg)
        x_scr[own : own + block, :] = loc_ref[...].astype(F32)
        x_scr[own + block :, :] = jnp.zeros((x_scr.shape[0] - own - block, width), F32)
        x_ref[...] = x_scr[...].astype(BF16)
        qa_ref[...] = penalty(seg_scr[...])
        ka_ref[...] = jnp.where(lane == seg_scr[...], 1.0, 0.0).astype(BF16)
        kl_ref[...] = jnp.where(lane == all_scr[...], 1.0, 0.0).astype(BF16)
        gates(x_ref[0:own, :], ga_ref, g0_ref)
        gates(loc_ref[...], gl_ref, g1_ref)

    bias = jnp.where(step == 0, small_ref[0:1, :], jnp.where(step == 2, small_ref[1:2, :], 0.0))
    scale = jnp.where(step == 0, (LANES // 2) ** -0.5, 1.0)
    w = w_ref[:, pl.ds(pl.multiple_of(step * width, LANES), width)]
    out_ref[...] = ((dotf(x_ref[0:own, :], w, NN) + bias) * scale).astype(BF16)


def project_own(packs, loc, mine, other, dirs, scale, core, place, total):
    block, width = loc.shape
    own = len(packs) * block
    rows = scale.shape[0]
    fix = lambda c: (0, 0)
    full = lambda shape: pl.BlockSpec(shape, lambda c: (0,) * len(shape))
    shapes = [
        ((own, 3 * width), BF16),
        ((width, 3 * width), BF16),
        ((16, width), F32),
        ((total, width), BF16),
        ((own, LANES), BF16),
        ((own, LANES), BF16),
        ((block, LANES), BF16),
        ((own, LANES), BF16),
        ((2, rows, own), F32),
        ((2, rows, block), F32),
        ((rows, own), F32),
        ((rows, block), F32),
    ]
    return pl.pallas_call(
        own_kernel,
        grid=(3,),
        in_specs=[full(p.shape) for p in packs]
        + [full(v.shape) for v in (loc, mine, other, dirs, scale)]
        + [SMEM_SPEC, SMEM_SPEC],
        out_specs=[pl.BlockSpec((own, width), lambda c: (0, c))] + [full(s) for s, _ in shapes[1:]],
        out_shape=[jax.ShapeDtypeStruct(s, t) for s, t in shapes],
        scratch_shapes=[pltpu.VMEM((total, width), F32)] + [pltpu.VMEM((own, LANES), F32)] * 2,
        compiler_params=pltpu.CompilerParams(vmem_limit_bytes=40 * 2**20),
        cost_estimate=cost(10),
        name="projection_own",
    )(*packs, loc, mine, other, dirs, scale, core, place)


def project_shared_kernel(all_ref, loc_ref, w_ref, b_ref, q_out, kv_out):
    step = pl.program_id(0)

    @pl.when(step == 0)
    def _():
        q = dotf(loc_ref[...], w_ref[...], NN) + b_ref[0:1, :]
        q_out[...] = (q * (LANES // 2) ** -0.5).astype(BF16)

    @pl.when(step > 0)
    def _():
        bias = jnp.where(step == 2, b_ref[1:2, :], 0.0)
        kv_out[...] = (dotf(all_ref[...], w_ref[...], NN) + bias).astype(BF16)


def project_shared(x_all, x_loc, weight, small, deps=()):
    n_all, width = x_all.shape
    n_loc = x_loc.shape[0]
    fix = lambda c: (0, 0)
    return pl.pallas_call(
        ignoring(project_shared_kernel, 4, len(deps)),
        grid=(3,),
        in_specs=[
            pl.BlockSpec((n_all, width), fix),
            pl.BlockSpec((n_loc, width), fix),
            pl.BlockSpec((width, width), lambda c: (0, c)),
            pl.BlockSpec(small.shape, fix),
        ]
        + [ANY_SPEC] * len(deps),
        out_specs=[
            pl.BlockSpec((n_loc, width), fix),
            pl.BlockSpec((n_all, width), lambda c: (0, jnp.maximum(c - 1, 0))),
        ],
        out_shape=[
            jax.ShapeDtypeStruct((n_loc, width), BF16),
            jax.ShapeDtypeStruct((n_all, 2 * width), BF16),
        ],
        compiler_params=pltpu.CompilerParams(vmem_limit_bytes=16 * 2**20),
        cost_estimate=cost(5),
        name="projection_shared",
    )(x_all, x_loc, weight, small, *deps)


def gelu_parts(x):
    size = jnp.abs(x)
    t = 1.0 / (1.0 + (0.3275911 * 0.7071067811865476) * size)
    poly = t * (
        0.254829592
        + t * (-0.284496736 + t * (1.421413741 + t * (-1.453152027 + t * 1.061405429)))
    )
    bell = jnp.exp(-0.5 * x * x)
    tail = 0.5 * poly * bell
    phi = jnp.where(x >= 0, 1.0 - tail, tail)
    return x * phi, phi + x * bell * 0.3989422804014327


def mean_last(v):
    return jnp.sum(v, axis=-1, keepdims=True) * (1.0 / v.shape[-1])


def layer_kernel(
    chunks, tile,
    x_ref, a_ref, c0_ref, c1_ref, c2_ref, c3_ref, cl_ref, wom_ref, woo_ref, mine_ref, other_ref, vec_ref,
    core_ref, place_ref,
    h_ref, ga_ref, g1_ref, keep_ref, send_ref, sums_ref,
    c_scr, z_scr, r_scr, nh_scr, acc_scr, di_scr, act_scr, der_scr, ih_scr, wo_ref, up_ref, down_ref,
):
    step = pl.program_id(0)
    total, width = x_ref.shape
    half = width // 2
    low_core = core_ref[0] == 0
    high_core = core_ref[0] != 0

    vec = lambda i: vec_ref[i : i + 1, :]

    def over_tiles(body):
        @pl.loop(0, total // tile)
        def _(i):
            body(pl.ds(pl.multiple_of(i * tile, tile), tile))

    def add_sum(row, value):
        sums_ref[row : row + 1, :] += jnp.sum(value, axis=0, keepdims=True)

    def load(ref, is_mine):
        @pl.when(is_mine)
        def _():
            ref[...] = mine_ref[...]

        @pl.when(jnp.logical_not(is_mine))
        def _():
            ref[...] = other_ref[...]

    def emit(is_mine, value, cols=slice(None)):
        @pl.when(is_mine)
        def _():
            keep_ref[:, cols] = value

        @pl.when(jnp.logical_not(is_mine))
        def _():
            send_ref[:, cols] = value

    back = jnp.maximum(step - chunks, 0)
    j = back // 2
    forth = step < chunks
    even = (step >= chunks) & (step < 3 * chunks) & (back % 2 == 0)
    odd = (step >= chunks) & (step < 3 * chunks) & (back % 2 == 1)

    @pl.when(step == 0)
    def _():
        sums_ref[...] = jnp.zeros_like(sums_ref)

        @pl.when(low_core)
        def _():
            wo_ref[:, 0:half] = wom_ref[...]
            wo_ref[:, half:width] = woo_ref[...]

        @pl.when(high_core)
        def _():
            wo_ref[:, 0:half] = woo_ref[...]
            wo_ref[:, half:width] = wom_ref[...]

        def body(here):
            y = dotf(a_ref[here, :], wo_ref[...], NN) + vec(2) + x_ref[here, :].astype(F32)
            y = y - mean_last(y)
            r = lax.rsqrt(mean_last(y * y) + EPS_NORM)
            z = y * r
            z_scr[here, :] = z
            r_scr[here, :] = r
            nh_scr[here, :] = (z * vec(6) + vec(4)).astype(BF16)
            acc_scr[here, :] = jnp.zeros_like(z)

        for first, rows in tiles_of(total, tile):
            body(slice(first, first + rows))

    @pl.when(forth | odd)
    def _():
        load(up_ref, low_core)

    @pl.when(forth | even)
    def _():
        load(down_ref, high_core)

    @pl.when(forth)
    def _():
        bias = vec_ref[pl.ds(8 + step, 1), :]
        parts = [slice(first, first + rows) for first, rows in tiles_of(total, 256)]
        ahead = dotf(nh_scr[parts[0], :], up_ref[...], NN) + bias
        for i, here in enumerate(parts):
            inner = ahead
            if i + 1 < len(parts):
                ahead = dotf(nh_scr[parts[i + 1], :], up_ref[...], NN) + bias
            act, der = gelu_parts(inner)
            act = act.astype(BF16)
            act_scr[step, here, :] = act
            der_scr[step, here, :] = der.astype(BF16)
            acc_scr[here, :] += dotf(act, down_ref[...], NN)

    @pl.when(step == chunks)
    def _():
        block = cl_ref.shape[0]
        for s, ref in enumerate((c0_ref, c1_ref, c2_ref, c3_ref)):
            there = pl.ds(pl.multiple_of((place_ref[0] ^ s) * block, 8), block)
            c_scr[there, :] = ref[...].astype(F32)
        c_scr[4 * block : 5 * block, :] = cl_ref[...].astype(F32)
        c_scr[5 * block :, :] = jnp.zeros((total - 5 * block, width), F32)

        def body(here):
            v = z_scr[here, :] * vec(6) + vec(4) + acc_scr[here, :] + vec(3)
            v = v - mean_last(v)
            r = lax.rsqrt(mean_last(v * v) + EPS_NORM)
            z = v * r
            h_ref[here, :] = (z * vec(7) + vec(5)).astype(BF16)
            c = c_scr[here, :]
            q = c * vec(7)
            gt = r * (q - mean_last(q) - z * mean_last(q * z))
            acc_scr[here, :] = gt
            di_scr[here, :] = gt.astype(BF16)
            add_sum(3, gt)
            add_sum(5, c)
            add_sum(7, c * z)

        over_tiles(body)

    @pl.when(even)
    def _():
        emit(high_core, dotf(act_scr[j], di_scr[...], TN).astype(BF16))

        def body(here):
            gi = dotf(di_scr[here, :], down_ref[...], NT) * der_scr[j, here, :].astype(F32)
            sums_ref[pl.ds(8 + j, 1), :] += jnp.sum(gi, axis=0, keepdims=True)
            ih_scr[here, :] = gi.astype(BF16)

        over_tiles(body)

    @pl.when(odd)
    def _():
        emit(low_core, dotf(nh_scr[...], ih_scr[...], TN).astype(BF16))

        def body(here):
            acc_scr[here, :] += dotf(ih_scr[here, :], up_ref[...], NT)

        over_tiles(body)

    @pl.when(step == 3 * chunks)
    def _():
        def body(here):
            gn = acc_scr[here, :]
            z = z_scr[here, :]
            q = gn * vec(6)
            g1 = r_scr[here, :] * (q - mean_last(q) - z * mean_last(q * z))
            g1_ref[here, :] = g1
            ah = g1.astype(BF16)
            di_scr[here, :] = ah
            ga_ref[here, :] = dotf(ah, wo_ref[...], NT).astype(BF16)
            add_sum(2, g1)
            add_sum(4, gn)
            add_sum(6, gn * z)

        for first, rows in tiles_of(total, tile):
            body(slice(first, first + rows))
        out = dotf(a_ref[...], di_scr[...], TN).astype(BF16)
        emit(low_core, out[:, 0:half], slice(0, half))
        emit(high_core, out[:, half:width], slice(0, half))


def layer_rest(x, att, cot, mine, other, vec, core, place, chunks):
    total, width = x.shape
    fix = lambda s: (0, 0)
    once = pl.Buffered(buffer_count=1)

    def chunk_of(s):
        return jnp.where(s < chunks, s, jnp.clip((s - chunks) // 2, 0, chunks - 1))

    def const(shape):
        return pl.BlockSpec(shape, fix, pipeline_mode=once)

    rows = const((total, width))
    square = (width, width)
    out_half = pl.BlockSpec((width, width // 2), lambda s: (0, 2 * chunks), pipeline_mode=once)
    weight_spec = pl.BlockSpec(square, lambda s: (0, chunk_of(s)))
    grad_spec = pl.BlockSpec(square, lambda s: (0, jnp.maximum(s - chunks, 0) // 2))
    return pl.pallas_call(
        functools.partial(layer_kernel, chunks, 512),
        grid=(3 * chunks + 1,),
        in_specs=[
            rows, rows, *[const(v.shape) for v in cot],
            out_half, out_half, weight_spec, weight_spec, const(vec.shape), SMEM_SPEC, SMEM_SPEC,
        ],
        out_specs=[rows, rows, rows, grad_spec, grad_spec, const(vec.shape)],
        out_shape=[
            jax.ShapeDtypeStruct((total, width), BF16),
            jax.ShapeDtypeStruct((total, width), BF16),
            jax.ShapeDtypeStruct((total, width), F32),
            jax.ShapeDtypeStruct(mine.shape, BF16),
            jax.ShapeDtypeStruct(mine.shape, BF16),
            jax.ShapeDtypeStruct(vec.shape, F32),
        ],
        scratch_shapes=[
            pltpu.VMEM((total, width), F32),
            pltpu.VMEM((total, width), F32),
            pltpu.VMEM((total, 1), F32),
            pltpu.VMEM((total, width), BF16),
            pltpu.VMEM((total, width), F32),
            pltpu.VMEM((total, width), BF16),
            pltpu.VMEM((chunks, total, width), BF16),
            pltpu.VMEM((chunks, total, width), BF16),
            pltpu.VMEM((total, width), BF16),
            pltpu.VMEM(square, BF16),
            pltpu.VMEM(square, BF16),
            pltpu.VMEM(square, BF16),
        ],
        compiler_params=pltpu.CompilerParams(vmem_limit_bytes=60 * 2**20),
        cost_estimate=cost(70),
        name="layer_rest",
    )(x, att, *cot, mine, other, mine, other, vec, core, place)


def settle_kernel(b0_ref, b1_ref, b2_ref, b3_ref, *rest):
    place_ref, out_ref = rest[-2:]
    for s, ref in enumerate((b0_ref, b1_ref, b2_ref, b3_ref)):
        out_ref[place_ref[0] ^ s] = ref[...]
    total = rest[0][...]
    for ref in rest[1:-2]:
        total = total + ref[...].astype(F32)
    out_ref[4] = total.astype(out_ref.dtype)


def settle(blocks, last, last_block, place):
    block, width = blocks[1].shape
    one = pl.BlockSpec((block, width), lambda s: (0, 0))
    return pl.pallas_call(
        settle_kernel,
        grid=(1,),
        in_specs=[one] * 4
        + [pl.BlockSpec((block, width), lambda s: (last_block, 0))] * len(last)
        + [SMEM_SPEC],
        out_specs=pl.BlockSpec((5, block, width), lambda s: (0, 0, 0)),
        out_shape=jax.ShapeDtypeStruct((5, block, width), BF16),
        compiler_params=pltpu.CompilerParams(vmem_limit_bytes=16 * 2**20),
        cost_estimate=cost(2),
        name="settle",
    )(*blocks, *last, place)


def shared_input_kernel(
    dq_ref, dkv_ref, w_ref, base_ref, grad_ref, gate_ref, scale_ref, dirs_ref, part_ref, loc_ref, acc
):
    step = pl.program_id(0)

    @pl.when(step == 0)
    def _():
        mix = gate_mix(grad_ref[...], gate_ref, scale_ref[...])
        loc_ref[...] = base_ref[...] + dotf(mix, dirs_ref[...], TN) + dotf(dq_ref[...], w_ref[...], NT)

    @pl.when(step == 1)
    def _():
        acc[...] = dotf(dkv_ref[...], w_ref[...], NT)

    @pl.when(step == 2)
    def _():
        part_ref[...] = (acc[...] + dotf(dkv_ref[...], w_ref[...], NT)).astype(BF16)


def shared_input(dq, dkv, weight, base, base_block, grad, gate, scale, dirs):
    n_loc, width = dq.shape
    n_all = dkv.shape[1]
    fix = lambda c: (0, 0)
    return pl.pallas_call(
        shared_input_kernel,
        grid=(3,),
        in_specs=[
            pl.BlockSpec((n_loc, width), fix),
            pl.BlockSpec((None, n_all, width), lambda c: (jnp.maximum(c - 1, 0), 0, 0)),
            pl.BlockSpec((width, width), lambda c: (0, c)),
            pl.BlockSpec((n_loc, width), lambda c: (base_block, 0)),
            pl.BlockSpec(grad.shape, fix),
            pl.BlockSpec(gate.shape, lambda c: (0, 0, 0)),
            pl.BlockSpec(scale.shape, fix),
            pl.BlockSpec(dirs.shape, fix),
        ],
        out_specs=[pl.BlockSpec((n_all, width), fix), pl.BlockSpec((n_loc, width), fix)],
        out_shape=[
            jax.ShapeDtypeStruct((n_all, width), BF16),
            jax.ShapeDtypeStruct((n_loc, width), F32),
        ],
        scratch_shapes=[pltpu.VMEM((n_all, width), F32)],
        compiler_params=pltpu.CompilerParams(vmem_limit_bytes=60 * 2**20),
        cost_estimate=cost(5),
        name="shared_input",
    )(dq, dkv, weight, base, grad, gate, scale, dirs)


def weight_grad_kernel(
    x0_ref, x4_ref, loc_ref, dq_ref, dkv_ref, dq4_ref, dkv4_ref, core_ref, keep_ref, send_ref
):
    step = pl.program_id(0)
    width = x0_ref.shape[1]
    half = width // 2
    cut = 3 * half
    low_core = core_ref[0] == 0
    high_core = core_ref[0] != 0

    def emit(is_mine, cols, value):
        @pl.when(is_mine)
        def _():
            keep_ref[:, cols] = value

        @pl.when(jnp.logical_not(is_mine))
        def _():
            send_ref[:, cols] = value

    @pl.when(step == 0)
    def _():
        grad = dotf(x0_ref[...], dq_ref[...], TN) + dotf(loc_ref[...], dq4_ref[...], TN)
        emit(low_core, slice(0, width), grad.astype(BF16))

    @pl.when(step > 0)
    def _():
        grad = dotf(x0_ref[...], dkv_ref[...], TN) + dotf(x4_ref[...], dkv4_ref[...], TN)
        grad = grad.astype(BF16)

        @pl.when(step == 1)
        def _():
            emit(low_core, slice(width, cut), grad[:, 0:half])
            emit(high_core, slice(0, half), grad[:, half:width])

        @pl.when(step == 2)
        def _():
            emit(high_core, slice(half, cut), grad)


def weight_grad(x_cat, x_all, x_loc, dq, dkv, dq4, dkv4, core, deps=()):
    own, width = dq.shape
    n_all, n_loc = x_all.shape[0], x_loc.shape[0]
    fix = lambda c: (0, 0)
    half = lambda c: (jnp.maximum(c - 1, 0), 0, 0)
    shape = (width, 3 * width // 2)
    return pl.pallas_call(
        ignoring(weight_grad_kernel, 8, len(deps)),
        grid=(3,),
        in_specs=[
            pl.BlockSpec((own, width), fix),
            pl.BlockSpec((n_all, width), fix),
            pl.BlockSpec((n_loc, width), fix),
            pl.BlockSpec((own, width), fix),
            pl.BlockSpec((None, own, width), half),
            pl.BlockSpec((n_loc, width), fix),
            pl.BlockSpec((None, n_all, width), half),
            SMEM_SPEC,
        ]
        + [ANY_SPEC] * len(deps),
        out_specs=[pl.BlockSpec(shape, fix)] * 2,
        out_shape=[jax.ShapeDtypeStruct(shape, BF16)] * 2,
        compiler_params=pltpu.CompilerParams(vmem_limit_bytes=24 * 2**20),
        cost_estimate=cost(10),
        name="projection_weight_grad",
    )(x_cat, x_all, x_loc, dq, dkv, dq4, dkv4, core, *deps)


def gate_parts(grad, gate_ref, c):
    a, b = gate_ref[0], gate_ref[1]
    return thirds(grad * (b * c - 1.0) * a * (1.0 - a)), thirds(grad * a * c * b * (1.0 - b))


def gate_mix(grad, gate_ref, c):
    da, db = gate_parts(grad, gate_ref, c)
    return jnp.concatenate([da[0], db[0], da[1], db[1], da[0], db[0]], axis=0)


def gate_kernel(
    buckets_used, grad0_ref, grad1_ref, gate0_ref, gate1_ref, scale_ref, diag0_ref, diag1_ref, slots_ref, x_ref, loc_ref,
    col0_ref, col1_ref, sums_ref, turn_ref, flat_ref,
):
    c = scale_ref[...]
    rows = c.shape[0]
    head_dim = LANES // 2
    turned = diag1_ref[...]
    turned = jnp.concatenate(
        [turned, jnp.zeros((rows, diag0_ref.shape[1] - turned.shape[1]), F32)], axis=1
    )
    diag = diag0_ref[...] + pltpu.roll(turned, turn_ref[0], 1)

    def back(grad_ref, gate_ref, x):
        grad = grad_ref[...]
        da, db = gate_parts(grad, gate_ref, c)
        d = jnp.concatenate([part for pair in zip(da, db) for part in pair], axis=0)
        return dotf(d, x, NN), jnp.sum(grad * gate_ref[0] * gate_ref[1], axis=1, keepdims=True)

    dw0, scale0 = back(grad0_ref, gate0_ref, x_ref[...])
    dw1, scale1 = back(grad1_ref, gate1_ref, loc_ref[...])
    dw = dw0 + dw1
    dw = dw[: 2 * rows] + (dw[2 * rows : 4 * rows] + dw[4 * rows :])
    lane = lax.broadcasted_iota(jnp.int32, dw.shape, 1)
    row = lax.broadcasted_iota(jnp.int32, dw.shape, 0)
    row = jnp.where(row >= rows, row - rows, row) * head_dim
    dw = jnp.where((lane >= row) & (lane < row + head_dim), dw, 0.0)
    buckets = lax.broadcasted_iota(jnp.int32, (BUCKET_ROWS, diag.shape[1]), 0)
    hot = jnp.where(buckets == slots_ref[...], 1.0, 0.0).astype(BF16)
    table = dotf(jnp.concatenate(thirds(diag), axis=0), hot, NT)
    table = table[:rows] + (table[rows : 2 * rows] + table[2 * rows :])
    half = rows // 2
    flat_ref[...] = jnp.zeros_like(flat_ref)
    flat_ref[0:rows, :] = sums_ref[...]
    flat_ref[0:2, :] = col0_ref[...] + col1_ref[...]
    flat_ref[12:13, :] = jnp.sum(dw[:rows], axis=0, keepdims=True)
    flat_ref[13:14, :] = jnp.sum(dw[rows:], axis=0, keepdims=True)
    scales = jnp.broadcast_to(scale0 + scale1, (rows, LANES))
    lane = lax.broadcasted_iota(jnp.int32, table.shape, 1)
    table = jnp.where(lane < buckets_used, table, jnp.concatenate([scales] * (BUCKET_ROWS // LANES), axis=1))
    flat_ref[rows : rows + half, 0:BUCKET_ROWS] = table[0:half]
    flat_ref[rows : rows + half, BUCKET_ROWS : 2 * BUCKET_ROWS] = table[half:]


def gate_sums(grads, gates, scale, diags, slots, x, loc, cols, sums, turn, buckets_used):
    rows, own = grads[0].shape
    width = x.shape[1]
    full = lambda v: pl.BlockSpec(v.shape, lambda s: (0,) * v.ndim)
    args = [*grads, *gates, scale, *diags, slots, x, loc, *cols, sums, turn]
    specs = [full(v) for v in args[:-1]] + [SMEM_SPEC]
    specs[8] = pl.BlockSpec((own, width), lambda s: (0, 0))
    out = jax.ShapeDtypeStruct((rows + rows // 2, width), F32)
    return pl.pallas_call(
        functools.partial(gate_kernel, buckets_used),
        grid=(1,),
        in_specs=specs,
        out_specs=full(out),
        out_shape=out,
        compiler_params=pltpu.CompilerParams(vmem_limit_bytes=20 * 2**20),
        cost_estimate=cost(4),
        name="gate_sums",
    )(*args)


def own_input_kernel(
    dq_ref, dkv_ref, w_ref, base_ref, grad_ref, gate_ref, scale_ref, dirs_ref, dx_ref, acc
):
    step = pl.program_id(0)

    @pl.when(step == 0)
    def _():
        mix = gate_mix(grad_ref[...], gate_ref, scale_ref[...])
        acc[...] = base_ref[...] + dotf(mix, dirs_ref[...], TN) + dotf(dq_ref[...], w_ref[...], NT)

    @pl.when(step == 1)
    def _():
        acc[...] += dotf(dkv_ref[...], w_ref[...], NT)

    @pl.when(step == 2)
    def _():
        dx_ref[...] = (acc[...] + dotf(dkv_ref[...], w_ref[...], NT)).astype(BF16)


def own_input(dq, dkv, weight, base, grad, gate, scale, dirs, deps=()):
    own, width = dq.shape
    fix = lambda c: (0, 0)
    return pl.pallas_call(
        ignoring(own_input_kernel, 8, len(deps)),
        grid=(3,),
        in_specs=[
            pl.BlockSpec((own, width), fix),
            pl.BlockSpec((None, own, width), lambda c: (jnp.maximum(c - 1, 0), 0, 0)),
            pl.BlockSpec((width, width), lambda c: (0, c)),
            pl.BlockSpec((own, width), fix),
            pl.BlockSpec(grad.shape, fix),
            pl.BlockSpec(gate.shape, lambda c: (0, 0, 0)),
            pl.BlockSpec(scale.shape, fix),
            pl.BlockSpec(dirs.shape, fix),
        ]
        + [ANY_SPEC] * len(deps),
        out_specs=pl.BlockSpec((own, width), fix),
        out_shape=jax.ShapeDtypeStruct((own, width), BF16),
        scratch_shapes=[pltpu.VMEM((own, width), F32)],
        compiler_params=pltpu.CompilerParams(vmem_limit_bytes=20 * 2**20),
        cost_estimate=cost(8),
        name="own_input",
    )(dq, dkv, weight, base, grad, gate, scale, dirs, *deps)


def split_sum_kernel(_bits, keep_ref, got_ref, *outs):
    step = pl.program_id(0)
    cut = outs[0].shape[1]
    total = keep_ref[...] + got_ref[...]
    first, second = total[:, :cut], total[:, cut:]

    def put(here, ref, value):
        @pl.when(here)
        def _():
            ref[...] = value

    put(step // 2 == 0, outs[0], first)
    put(step // 2 == 1, outs[1], first)
    put(step % 2 == 0, outs[2], second)
    put(step % 2 == 1, outs[3], second)


def split_sum(keep, got, bits, cut, parts):
    rows, cols = keep.shape
    block = rows // 4 // parts
    low = lambda s, bits: (s // 2) ^ bits[0]
    high = lambda s, bits: (s % 2) ^ bits[1]
    wide = pl.BlockSpec(
        (block, cols), lambda s, t, bits: ((2 * high(s, bits) + low(s, bits)) * parts + t, 0)
    )
    at = lambda index, s, t, first, last: (
        index * parts + jnp.where(s < first, 0, jnp.where(s > last, parts - 1, t)), 0
    )
    stay = lambda s, t, bits: at(jnp.where(s < 2, s, 1) ^ bits[1], s, t, 0, 1)
    go = lambda s, t, bits: at(jnp.where(s < 2, 0, s - 2) ^ bits[1], s, t, 2, 3)
    stay_other = lambda s, t, bits: (
        jnp.where(s % 2 == 0, low(s, bits) * parts + t, low(s, bits) * parts + parts - 1), 0
    )
    go_other = lambda s, t, bits: (
        jnp.where(s % 2 == 1, low(s, bits) * parts + t, low(s, bits) * parts), 0
    )
    return pl.pallas_call(
        split_sum_kernel,
        grid_spec=pltpu.PrefetchScalarGridSpec(
            num_scalar_prefetch=1,
            grid=(4, parts),
            in_specs=[wide, wide],
            out_specs=[
                pl.BlockSpec((block, cut), stay),
                pl.BlockSpec((block, cut), go),
                pl.BlockSpec((block, cols - cut), stay_other),
                pl.BlockSpec((block, cols - cut), go_other),
            ],
        ),
        out_shape=[jax.ShapeDtypeStruct((rows // 2, cut), BF16)] * 2
        + [jax.ShapeDtypeStruct((rows // 2, cols - cut), BF16)] * 2,
        compiler_params=pltpu.CompilerParams(vmem_limit_bytes=60 * 2**20),
        cost_estimate=cost(3),
        name="split_sum",
    )(bits, keep, got)


def merge_kernel(_bits, a0_ref, a1_ref, b0_ref, b1_ref, out_ref):
    step = pl.program_id(0)
    cut = a0_ref.shape[1]

    def put(here, cols, ref):
        @pl.when(here)
        def _():
            out_ref[:, cols] = ref[...]

    put(step // 2 == 0, slice(0, cut), a0_ref)
    put(step // 2 == 1, slice(0, cut), a1_ref)
    put(step % 2 == 0, slice(cut, None), b0_ref)
    put(step % 2 == 1, slice(cut, None), b1_ref)


def merge(first, second, bits):
    rows, cut = first[0].shape
    rest = second[0].shape[1]
    block = rows // 2
    low = lambda s, bits: (s % 2) ^ bits[0]
    high = lambda s, bits: (s // 2) ^ bits[1]
    own = lambda s, bits: (jnp.where(s < 2, s % 2, 1) ^ bits[0], 0)
    other = lambda s, bits: (jnp.where(s < 2, 0, s % 2) ^ bits[0], 0)
    beside = lambda s, bits: (high(s, bits), 0)
    return pl.pallas_call(
        merge_kernel,
        grid_spec=pltpu.PrefetchScalarGridSpec(
            num_scalar_prefetch=1,
            grid=(4,),
            in_specs=[
                pl.BlockSpec((block, cut), own),
                pl.BlockSpec((block, cut), other),
                pl.BlockSpec((block, rest), beside),
                pl.BlockSpec((block, rest), beside),
            ],
            out_specs=pl.BlockSpec(
                (block, cut + rest), lambda s, bits: (2 * high(s, bits) + low(s, bits), 0)
            ),
        ),
        out_shape=jax.ShapeDtypeStruct((2 * rows, cut + rest), BF16),
        compiler_params=pltpu.CompilerParams(vmem_limit_bytes=16 * 2**20),
        cost_estimate=cost(3),
        name="merge",
    )(bits, *first, *second)


def split_four_kernel(_own, keep_ref, got_ref, *outs):
    total = keep_ref[...] + got_ref[...]
    for s, ref in enumerate(outs):
        @pl.when(pl.program_id(0) == s)
        def _():
            ref[...] = total


def split_four(keep, got, own):
    rows, cols = keep.shape
    block = rows // 4
    there = pl.BlockSpec((block, cols), lambda s, own: (s ^ own[0], 0))
    return pl.pallas_call(
        split_four_kernel,
        grid_spec=pltpu.PrefetchScalarGridSpec(
            num_scalar_prefetch=1,
            grid=(4,),
            in_specs=[there, there],
            out_specs=[pl.BlockSpec((block, cols), lambda s, own: (0, 0))] * 4,
        ),
        out_shape=[jax.ShapeDtypeStruct((block, cols), BF16)] * 4,
        compiler_params=pltpu.CompilerParams(vmem_limit_bytes=16 * 2**20),
        cost_estimate=cost(2),
        name="split_four",
    )(own, keep, got)


def finish_kernel(a_ref, b_ref, first_ref, bias_ref, gain_ref, up_ref, table_ref, gate_ref, scale_ref):
    flat = a_ref[...] + b_ref[...]
    width = flat.shape[1]
    rows = flat.shape[0] * 2 // 3
    heads, count = table_ref.shape
    local_rows = bias_ref.shape[1]
    local = pltpu.roll(flat[:rows], width - first_ref[0], 1)[:, 0:LANES]
    bias_ref[...] = local[0:6, 0:local_rows]
    gain_ref[...] = local[6:8, 0:local_rows]
    up_ref[...] = local[8 : 8 + up_ref.shape[0], 0:local_rows]
    table = jnp.concatenate(
        [flat[rows:, 0:BUCKET_ROWS], flat[rows:, BUCKET_ROWS : 2 * BUCKET_ROWS]], axis=0
    )
    table_ref[...] = table[0:heads, 0:count]
    scale_ref[...] = table.T[count : count + 1, 0:heads]
    folded = flat[8:16, 0:LANES]
    for k in range(1, width // LANES):
        folded = folded + flat[8:16, k * LANES : (k + 1) * LANES]
    folded = (folded + pltpu.roll(folded, LANES // 2, 1))[:, 0 : LANES // 2]
    row = lax.broadcasted_iota(jnp.int32, gate_ref.shape, 0)
    gate_ref[...] = jnp.where(row < gate_ref.shape[0] // 2, folded[4:5], folded[5:6])


def finish(flat, other, first_row, local_rows, chunks, table_shape, gate_shape):
    shapes = [
        (6, local_rows), (2, local_rows), (chunks, local_rows), table_shape[::-1], gate_shape[::-1],
        (1, table_shape[1]),
    ]
    full = lambda s: pl.BlockSpec(s, lambda i: (0, 0))
    return pl.pallas_call(
        finish_kernel,
        grid=(1,),
        in_specs=[full(flat.shape), full(flat.shape), SMEM_SPEC],
        out_specs=[full(s) for s in shapes],
        out_shape=[jax.ShapeDtypeStruct(s, F32) for s in shapes],
        cost_estimate=cost(1),
        name="finish",
    )(flat, other, first_row)


hold = lax.optimization_barrier


def after(value, *earlier):
    return lax.optimization_barrier((value,) + earlier)[0]


def swap(array, axis, bit):
    size = lax.axis_size(axis)
    return lax.ppermute(array, axis, [(i, i ^ (1 << bit)) for i in range(size)])


def swap_places(array, mask):
    return lax.ppermute(array, "blk", [(i, i ^ mask) for i in range(lax.axis_size("blk"))])


def by_place(arrays):
    place = lax.axis_index("blk")
    odd, upper = (place & 1) == 1, (place >> 1) == 1
    near = [jnp.where(odd, arrays[1 - i], arrays[i]) for i in range(2)]
    far = [jnp.where(odd, arrays[3 - i], arrays[2 + i]) for i in range(2)]
    return [jnp.where(upper, f, n) for f, n in zip(far, near)] + [
        jnp.where(upper, n, f) for f, n in zip(far, near)
    ]


def bit_of(axis, bit):
    return (lax.axis_index(axis) >> bit) & 1


def bit_count(axis):
    count = lax.axis_size(axis).bit_length() - 1
    assert 1 << count == lax.axis_size(axis)
    return count


def join(array, axis, bit, position):
    def finish(flight):
        mine, other = flight
        upper = bit_of(axis, bit) == 1
        return jnp.stack(
            [jnp.where(upper, other, mine), jnp.where(upper, mine, other)], axis=position
        )

    return (array, swap(array, axis, bit)), finish


def at_once(step):
    flight, finish = step
    return finish(flight)


def together(steps):
    flights, finishes = zip(*steps)
    return flights, lambda done: [finish(flight) for finish, flight in zip(finishes, done)]


def gather_begin(first, second):
    low = bit_of("rows", 0) == 0
    keep, send = jnp.where(low, first, second), jnp.where(low, second, first)

    def finish(flight):
        mine, got = flight
        return jnp.stack([jnp.where(low, mine, got), jnp.where(low, got, mine)], axis=0)

    return (keep, swap(send, "rows", 0)), finish


def blk_bits():
    return list(reversed(range(bit_count("blk"))))


def gather_blk(part, number):
    return join(part, "blk", blk_bits()[number], 1 + number)


def halves_of(array):
    array = array.reshape(-1, array.shape[-1])
    cut = array.shape[-1] // 2 // LANES * LANES
    return [array[:, :cut], array[:, cut:]]


def orders():
    high = list(range(1, bit_count("rows")))
    return high, high[::-1]


def gather_high(halves, step):
    steps = []
    for half, order in zip(halves, orders()):
        position = sum(1 for other in order[:step] if other > order[step])
        steps.append(join(half, "rows", order[step], position))
    return together(steps)


def gather_last(halves):
    first, second = orders()
    rows = halves[0].reshape(-1, halves[0].shape[-1]).shape[0]
    if len(first) == 2 and rows % 32 == 0:
        flat = [v.reshape(-1, v.shape[-1]) for v in halves]
        flights = [(v, swap(v, "rows", order[1])) for v, order in zip(flat, (first, second))]
        bits = jnp.stack([bit_of("rows", bit) for bit in first])
        return flights, lambda flights: merge(flights[0], flights[1], bits)
    flights, finish = gather_high(halves, len(first) - 1)
    return flights, lambda flights: whole(finish(flights))


def whole(halves):
    return jnp.concatenate([h.reshape(-1, h.shape[-1]) for h in halves], axis=-1)


def added(pair):
    if len(pair) == 1:
        return pair[0]
    return pair[0] + pair[1]


def part_of(pair, index, axis):
    return added([lax.dynamic_index_in_dim(v, index, axis, keepdims=False) for v in pair])


def halve(pair, shape, axis, bit, position):
    pair = [v.reshape(shape + (-1, v.shape[-1])) for v in pair]
    mine = bit_of(axis, bit)
    return part_of(pair, mine, position), swap(part_of(pair, 1 - mine, position), axis, bit)


def scatter_begin(keep, send):
    return keep, swap(send, "rows", 0)


def scatter_first(pair):
    first, second = orders()
    rows, cols = pair[0].shape
    if len(first) == 2 and rows % 128 == 0:
        cut = halves_of(pair[0])[0].shape[1]
        bits = jnp.stack([bit_of("rows", bit) for bit in first])
        keep_a, send_a, keep_b, send_b = split_sum(pair[0], pair[1], bits, cut, 1)
        return [(keep_a, swap(send_a, "rows", first[0])), (keep_b, swap(send_b, "rows", second[0]))]
    return scatter_high([(half,) for half in halves_of(added(pair))], 0)


def scatter_high(halves, step):
    out = []
    for half, order in zip(halves, orders()):
        left = sorted(order[step:], reverse=True)
        out.append(halve(half, (2,) * len(left), "rows", order[step], left.index(order[step])))
    return out


def scatter_whole(halves):
    whole_sum = jnp.concatenate([added([v.reshape(-1, v.shape[-1]) for v in h]) for h in halves], axis=-1)
    return whole_sum


def exchange_first(blocks):
    upper = bit_of("blk", 1)
    pairs = blocks.reshape((2, 2) + blocks.shape[1:])
    keep = lax.dynamic_index_in_dim(pairs, upper, 0, keepdims=False)
    send = lax.dynamic_index_in_dim(pairs, 1 - upper, 0, keepdims=False)
    return (keep, swap_places(send, 2))


def exchange_second(flight):
    odd = bit_of("blk", 0)
    pick = lambda array, index: lax.dynamic_index_in_dim(array, index, 0, keepdims=False)
    send = jnp.stack([pick(array, 1 - odd) for array in flight])
    return (pick(flight[0], odd), pick(flight[1], odd), swap_places(send, 1))


def exchange_end(flight):
    mine, far, other = flight
    return [mine, other[0], far, other[1]]


def total_of(parts):
    return sum(v.astype(F32) for v in parts).astype(BF16)


def scatter_four(pair):
    own = bit_of("rows", 1) + 2 * bit_of("rows", 2)
    blocks = split_four(pair[0], pair[1], own.reshape(1))
    size = lax.axis_size("rows")
    return [blocks[0]] + [
        lax.ppermute(blocks[s], "rows", [(i, i ^ (2 * s)) for i in range(size)]) for s in (1, 2, 3)
    ]


def scatter_places(parts):
    place = lax.axis_index("blk")
    views = [v.reshape((2, 4, -1, v.shape[-1])) for v in parts]
    blocks = [
        total_of([lax.dynamic_index_in_dim(v, place ^ s, 1, keepdims=False) for v in views]) for s in range(4)
    ]
    return [blocks[0]] + [swap_places(blocks[s], s) for s in (1, 2, 3)]


def scatter_blk(pair, bit):
    count = bit_count("blk")
    return halve(pair, (2,) * (1 + count - bit), "blk", bit, count - bit)


def scatter_end(pair):
    core = bit_of("rows", 0)
    pair = [v.reshape((2, -1, v.shape[-1])) for v in pair]
    half = lambda index: total_of([lax.dynamic_index_in_dim(v, index, 0, keepdims=False) for v in pair])
    return half(core), swap(half(1 - core), "rows", 0)


def scatter_done(flight):
    keep, got = flight
    low = bit_of("rows", 0) == 0
    return jnp.where(low, keep, got).astype(F32), jnp.where(low, got, keep).astype(F32)


def shards(
    hidden_in,
    segment_ids,
    bucket_map,
    qkv_weight,
    out_weight,
    up_weight,
    down_weight,
    bias_cols,
    norm_gains,
    up_bias,
    rel_table,
    gate_weight,
    gate_scale,
    cotangent,
):
    row_count, block_len, width = hidden_in.shape
    heads = gate_scale.shape[0]
    pairs = heads // 2
    head_dim = width // heads
    bucket_count = rel_table.shape[0]
    cycle = lax.axis_size("blk")
    place = lax.axis_index("blk")
    core = bit_of("rows", 0).reshape(1)
    frames = block_len * cycle
    shared = row_count - 1
    used = frames + block_len
    total = -(-used // 256) * 256
    inner_width = up_weight.shape[1]
    chunks = inner_width // width
    local_rows = qkv_weight.shape[0]
    half = width // 2
    cut = 3 * half
    high_steps = len(orders()[0])
    assert row_count == cycle + 1 and cycle == 4 and bucket_count < BUCKET_ROWS

    def take(array, index):
        return lax.dynamic_index_in_dim(array, index, 0, keepdims=False)

    def with_rest(blocks, last):
        return jnp.concatenate(blocks + [last, jnp.zeros((total - used, width), BF16)], axis=0)

    extras = jnp.concatenate(
        [bias_cols, norm_gains, up_bias.reshape(local_rows, chunks)], axis=1
    )
    extras = jnp.pad(extras, ((0, 0), (0, SMALL - extras.shape[1])))
    qkv_part = at_once(
        gather_begin(
            jnp.concatenate([qkv_weight[:, :cut], extras], axis=1),
            jnp.concatenate([qkv_weight[:, cut:], jnp.zeros_like(extras)], axis=1),
        )
    )
    up_turned = up_weight.reshape(local_rows, width, chunks).transpose(0, 2, 1)
    rest_flight, rest_finish = gather_begin(
        jnp.concatenate([up_turned.reshape(local_rows, inner_width), out_weight[:, :half]], axis=1),
        jnp.concatenate([down_weight.reshape(local_rows, inner_width), out_weight[:, half:]], axis=1),
    )
    head_rows = -(-heads // 16) * 16
    picks = jnp.repeat(jnp.eye(heads, head_rows, dtype=F32), head_dim, axis=0)
    dirs = [
        picks * jnp.tile(jnp.sum(gate_weight[:, part], axis=1), heads)[:, None]
        for part in (slice(0, 4), slice(4, 8))
    ]
    dirs_high, dirs_middle, dirs_low = thirds(jnp.concatenate(dirs, axis=1).T)
    dirs_all = jnp.concatenate([dirs_high, dirs_middle, dirs_low], axis=0)
    dirs_mix = jnp.concatenate([dirs_high, dirs_high, dirs_middle], axis=0)
    scale_rows = jnp.pad(gate_scale, (0, head_rows - heads))[:, None]

    shift = -(-frames // LANES)
    span = 2 * frames - 1
    lead = shift * LANES - (frames - 1)
    table_width = 2 * shift * LANES
    narrow = -(-(shift * LANES + block_len) // LANES) * LANES
    slots = jnp.pad(bucket_map[::-1], (lead, table_width - lead - span), constant_values=-1)
    hot = (jnp.arange(bucket_count, dtype=jnp.int32)[:, None] == slots[None, :]).astype(F32)

    hidden_in, segment_ids, rest_flight, qkv_part = hold(
        (hidden_in, segment_ids, rest_flight, qkv_part)
    )
    seg_rows = jnp.pad(segment_ids.astype(BF16), ((0, 0), (0, width - block_len)))

    def with_segments(index):
        tail_rows = jnp.pad(jnp.stack([take(seg_rows, index), seg_rows[shared]]), ((0, 14), (0, 0)))
        return jnp.concatenate([take(hidden_in, index), tail_rows], axis=0)

    packs = [with_segments(place ^ s) for s in range(cycle)]
    qkv_flight, qkv_finish = gather_blk(qkv_part, 0)
    qkv_flight, rest_flight = hold((qkv_flight, rest_flight))
    qkv_flight, qkv_finish = gather_blk(qkv_finish(qkv_flight), 1)
    rest_flight, rest_finish = gather_blk(rest_finish(rest_flight), 0)
    qkv_flight, packs, rel_table, hot, cotangent = hold(
        (qkv_flight, packs, rel_table, hot, cotangent)
    )
    cot = [take(cotangent, place ^ s) for s in range(cycle)] + [cotangent[shared]]
    blank = jnp.zeros((total, width), BF16)
    packs[1] = swap_places(packs[1], 1)
    qkv_part = qkv_finish(qkv_flight)
    qkv_halves = halves_of(qkv_part)
    for step in range(high_steps - 2):
        qkv_halves = at_once(gather_high(qkv_halves, step))
    qkv_flight, qkv_finish = gather_high(qkv_halves, high_steps - 2)
    table = jnp.pad(rel_table, ((0, 0), (0, head_rows - heads)))
    u_own = lax.dot_general(table, hot, (((0,), (0,)), ((), ())), precision=HIGHEST)
    u_loc = lax.dynamic_slice_in_dim(
        jnp.pad(u_own, ((0, 0), (0, frames))), place * block_len, narrow, 1
    )
    qkv_flight, rest_flight, packs, cot, blank, u_own, u_loc, dirs_all, x_loc = hold(
        (qkv_flight, rest_flight, packs, cot, blank, u_own, u_loc, dirs_all, hidden_in[shared])
    )
    packs[2], packs[3] = swap_places(packs[2], 2), swap_places(packs[3], 3)
    qkv_flight, qkv_finish = gather_last(qkv_finish(qkv_flight))
    rest_flight, rest_finish = gather_blk(rest_finish(rest_flight), 1)
    qkv_flight, rest_flight, packs = hold((qkv_flight, rest_flight, packs))
    qkv_mine = qkv_finish(qkv_flight)
    qkv_other = swap(qkv_mine, "rows", 0)
    rest_halves = halves_of(rest_finish(rest_flight))
    for step in range(high_steps - 2):
        rest_halves = at_once(gather_high(rest_halves, step))
    rest_flight, rest_finish = gather_high(rest_halves, high_steps - 2)
    shared_flight, shared_finish = join(x_loc, "blk", 1, 0)
    own_cols = (0, pairs, 2 * pairs)
    loc_cols = (0, 0, pairs)
    place_of = place.reshape(1)
    (
        qkv_own, qkv_full, small, x_cat, qa_own, ka_own, qa_loc, ka_all, gate_own, gate_loc, g_own, g_loc,
    ) = project_own(packs, x_loc, qkv_mine, qkv_other, dirs_all, scale_rows, core, place_of, total)
    rest_flight, shared_flight, qkv_own, small, cot = hold(
        (rest_flight, shared_flight, qkv_own, small, cot)
    )
    rest_flight, rest_finish = gather_last(rest_finish(rest_flight))
    shared_flight, shared_finish = join(shared_finish(shared_flight), "blk", 0, 1)
    cot[2] = swap_places(cot[2], 2)
    att_half, att, lse_own = attend_forward(
        u_own, qkv_own, qkv_own, qkv_own, qa_own, ka_own, g_own, own_cols, pairs, frames, True,
        (blank,), 0, 18,
    )
    shared_flight, rest_flight, cot, att, att_half, lse_own = hold(
        (shared_flight, rest_flight, cot, att, att_half, lse_own)
    )
    rest_mine = rest_finish(rest_flight)
    rest_other = swap(rest_mine, "rows", 0)
    x_all = shared_finish(shared_flight).reshape(frames, width)
    q_loc, kv_all = project_shared(x_all, x_loc, qkv_full, small, (rest_mine,))
    cot[1], cot[3] = swap_places(cot[1], 1), swap_places(cot[3], 3)
    att_half, att, lse_loc = attend_forward(
        u_loc, q_loc, kv_all, kv_all, qa_loc, ka_all, g_loc, loc_cols, pairs, frames, False,
        (att_half, att), cycle, 8,
    )
    cot, rest_other, att, att_half, lse_loc = hold((cot, rest_other, att, att_half, lse_loc))
    h_cat, ga_cat, g1_cat, rest_keep, rest_send, sums = layer_rest(
        x_cat, att_half, cot, rest_mine, rest_other, small, core, place_of, chunks
    )

    def blocks_of(own):
        return own[:frames].reshape(cycle, block_len, width)

    rest_flight = scatter_begin(rest_keep, rest_send)
    hidden = [take(blocks_of(h_cat), place ^ s) for s in range(cycle)]
    hidden[1], hidden[2] = swap_places(hidden[1], 1), swap_places(hidden[2], 2)
    dq_loc, dkv_all, col_loc, grad_loc, diag_loc = attend_backward(
        u_loc, q_loc, kv_all, kv_all, ga_cat, att, qa_loc, ka_all, g_loc, lse_loc,
        g_loc, jnp.zeros((head_rows, narrow), F32), loc_cols, pairs, cycle, 16, 0, pairs,
    )
    part_all, mine = shared_input(
        dq_loc, dkv_all, qkv_full, g1_cat, cycle, grad_loc, gate_loc, scale_rows, dirs_mix
    )
    rest_flight, hidden[:3], part_all = hold((rest_flight, hidden[:3], part_all))
    hidden[3] = swap_places(hidden[3], 3)
    rest_flight = scatter_first(rest_flight)
    part_flight = halve((part_all,), (2, 2), "blk", 0, 1)
    third = pairs // 3
    into = attend_backward(
        u_own, qkv_own, qkv_own, qkv_own, ga_cat, att, qa_own, ka_own, g_own, lse_own,
        g_own, jnp.zeros((head_rows, table_width), F32), own_cols, pairs, 0, 26, 0, pairs - third, (),
        (rest_flight[0][0], rest_flight[1][0], part_flight[0]),
    )
    rest_flight, part_flight, into, hidden[3] = hold((rest_flight, part_flight, into, hidden[3]))
    for step in range(1, high_steps):
        rest_flight = scatter_high(rest_flight, step)
    part_flight = halve(part_flight, (2,), "blk", 1, 0)
    dq_own, dkv_own, col_own, grad_own, diag = into
    into = attend_backward(
        u_own, qkv_own, qkv_own, qkv_own, ga_cat, att, qa_own, ka_own, g_own, lse_own,
        grad_own, diag, own_cols, pairs, 0, 13, pairs - third, third, (dq_own, dkv_own, col_own),
        (rest_flight[0][0], rest_flight[1][0]),
    )
    rest_flight, part_flight, into = hold((rest_flight, part_flight, into))
    dq_own, dkv_own, col_own, grad_own, diag = into
    rest_flight = scatter_blk((scatter_whole(rest_flight),), 0)
    flat = gate_sums(
        (grad_own, grad_loc), (gate_own, gate_loc), scale_rows, (diag, diag_loc), slots[None, :], x_cat, x_loc,
        (col_own, col_loc), sums, (place * block_len).reshape(1), bucket_count,
    )
    direct = high_steps == 2 and width % 64 == 0
    upper = [2 * s for s in (1, 2, 3)] if direct else []
    swap_rows = lambda array, mask: lax.ppermute(
        array, "rows", [(i, i ^ mask) for i in range(lax.axis_size("rows"))]
    )
    add_up = lambda arrays: sum(arrays[1:], arrays[0])
    flat_flight = [flat] + [swap_rows(flat, mask) for mask in upper]
    dx_own = own_input(
        dq_own, dkv_own, qkv_full, g1_cat, grad_own, gate_own, scale_rows, dirs_mix, (rest_flight[0], flat)
    )
    flat_flight, dx_own = hold((flat_flight, dx_own))
    flat = add_up(flat_flight)
    flat_flight = (flat, swap(flat, "rows", 0))
    inputs = [take(blocks_of(dx_own), place ^ s) for s in range(cycle)]
    inputs[1], inputs[2] = swap_places(inputs[1], 1), swap_places(inputs[2], 2)
    qkv_keep, qkv_send = weight_grad(
        x_cat, x_all, x_loc, dq_own, dkv_own, dq_loc, dkv_all, core, (dx_own,)
    )
    rest_flight, flat_flight, qkv_keep, qkv_send, inputs = hold(
        (rest_flight, flat_flight, qkv_keep, qkv_send, inputs)
    )
    back_flight = scatter_begin(qkv_keep, qkv_send)
    flat = add_up(flat_flight)
    rest_flight = scatter_blk(rest_flight, 1)
    back_flight = hold(back_flight)
    if direct:
        back_flight = scatter_four(back_flight)
    else:
        back_flight = scatter_first(back_flight)
        for step in range(1, high_steps):
            back_flight = scatter_high(back_flight, step)
    inputs[3], hidden = hold((inputs[3], hidden, back_flight[0]))[:2]
    inputs[3] = swap_places(inputs[3], 3)
    hidden_out = settle(hidden, (h_cat,), cycle, place_of)
    rest_flight = scatter_end(rest_flight)
    back_flight, rest_flight, inputs, flat, hidden_out = hold(
        (back_flight, rest_flight, inputs, flat, hidden_out)
    )
    if direct:
        back_flight = scatter_places(back_flight)
    else:
        back_flight = scatter_blk(scatter_blk((scatter_whole(back_flight),), 0), 1)
        for bit in range(1, bit_count("rows")):
            flat = flat + swap(flat, "rows", bit)
    flat, rest_flight, inputs = hold((flat, rest_flight, inputs, back_flight[0]))[:3]
    flat_flight = (flat, swap_places(flat, 1))
    rest_first, rest_second = scatter_done(rest_flight)
    grad_up = rest_first[:, :inner_width].reshape(local_rows, chunks, width).transpose(0, 2, 1)
    grad_up = grad_up.reshape(local_rows, inner_width)
    grad_down = rest_second[:, :inner_width].reshape(local_rows * chunks, width)
    grad_out = jnp.concatenate([rest_first[:, inner_width:], rest_second[:, inner_width:]], axis=1)
    grad_input = settle(inputs, (mine,) + tuple(part_flight), 0, place_of)
    back_flight, flat_flight, grad_input, grad_up, grad_down, grad_out = hold(
        (back_flight, flat_flight, grad_input, grad_up, grad_down, grad_out)
    )
    back_flight = scatter_end(back_flight)
    flat = add_up(flat_flight)
    flat_flight = (flat, swap_places(flat, 2))
    last_first, last_second = scatter_done(back_flight)
    first_row = (lax.axis_index("rows") * cycle + place) * local_rows
    bias_sum, gain_sum, up_bias_sum, table_sum, gate_weight_sum, gate_scale_sum = finish(
        *flat_flight, first_row.reshape(1), local_rows, chunks, rel_table.shape, gate_weight.shape
    )
    return (
        hidden_out,
        grad_input,
        jnp.concatenate([last_first, last_second], axis=1),
        grad_out,
        grad_up,
        grad_down,
        bias_sum.T,
        gain_sum.T,
        up_bias_sum.T.reshape(-1),
        table_sum.T,
        gate_weight_sum.T,
        gate_scale_sum.reshape(-1),
    )


def solution(mesh):
    placed = (
        P("rows", "blk", None),
        P("rows", "blk"),
        P(),
        P(("rows", "blk"), None),
        P(("rows", "blk"), None),
        P(("rows", "blk"), None),
        P(("rows", "blk"), None),
        P(("rows", "blk"), None),
        P(("rows", "blk"), None),
        P(("rows", "blk")),
        P(),
        P(),
        P(),
        P("rows", "blk", None),
    )
    return jax.shard_map(
        shards,
        mesh=mesh,
        in_specs=placed,
        out_specs=(
            P("rows", "blk", None),
            P("rows", "blk", None),
            P(("rows", "blk"), None),
            P(("rows", "blk"), None),
            P(("rows", "blk"), None),
            P(("rows", "blk"), None),
            P(("rows", "blk"), None),
            P(("rows", "blk"), None),
            P(("rows", "blk")),
            P(),
            P(),
            P(),
        ),
        check_vma=False,
    )
```

```python
import functools

import jax
import jax.numpy as jnp
from jax import lax
from jax.experimental import pallas as pl
from jax.experimental.pallas import tpu as pltpu
from jax.sharding import PartitionSpec as P

EPS_NORM = 1e-05
LANES = 128
SMALL = 128
BUCKET_ROWS = 384
BF16 = jnp.bfloat16
F32 = jnp.float32
NN = (((1,), (0,)), ((), ()))
NT = (((1,), (1,)), ((), ()))
TN = (((0,), (0,)), ((), ()))
HIGHEST = lax.Precision.HIGHEST


def thirds(v):
    high = v.astype(BF16)
    rest = v - high.astype(F32)
    middle = rest.astype(BF16)
    return high, middle, (rest - middle.astype(F32)).astype(BF16)


def dotf(a, b, dims):
    return lax.dot_general(a, b, dims, preferred_element_type=F32)


def tiles_of(total, tile):
    return [(s, min(tile, total - s)) for s in range(0, total, tile)]


ANY_SPEC = pl.BlockSpec(memory_space=pl.ANY)


def ignoring(kernel, inputs, count):
    return lambda *refs: kernel(*refs[:inputs], *refs[inputs + count :])


def cost(us):
    return pl.CostEstimate(flops=1000, bytes_accessed=1000, transcendentals=0)


SMEM_SPEC = pl.BlockSpec(memory_space=pltpu.SMEM)


def table_rows_of(u, width):
    return pltpu.roll(jnp.broadcast_to(u, (LANES, width)), 0, 1, stride=1, stride_axis=0)


def forward_kernel(
    tile, flip, u_ref, q_ref, k_ref, v_ref, qa_ref, ka_ref, g_ref,
    ob_ref, o_ref, lse_ref, t_scr,
):
    nq, nk, width = q_ref.shape[0], k_ref.shape[0], u_ref.shape[-1]
    pair = pl.program_id(0)
    half = LANES // 2
    shift = -(-nk // LANES)
    low = lax.broadcasted_iota(jnp.int32, (1, LANES), 1) < half
    low_rows = lax.broadcasted_iota(jnp.int32, (LANES, 1), 0) < half
    k, v, q = k_ref[...], v_ref[...], q_ref[...]
    zero = jnp.zeros((), BF16)
    khs, qhs, vzs, gs = [], [], [], []
    for hh in range(2):
        head = pl.ds(2 * pair + hh, 1)
        t_scr[hh] = table_rows_of(u_ref[head, :], width)
        gs.append(g_ref[head, :])
        sel = low if hh == 0 else jnp.logical_not(low)
        khs.append(jnp.where(sel, k, ka_ref[...]))
        qhs.append(jnp.where(sel, q, qa_ref[...]))
        vzs.append(jnp.where(sel, v, zero))
    vt = v.T if flip else None
    for first, cols in tiles_of(nq, tile):
        total, scales, parts = None, [], []
        for hh in range(2):
            raw = dotf(khs[hh], qhs[hh][first : first + cols], NT)
            g = gs[hh][:, first : first + cols]
            scores, peak = [], None
            for f2, r2 in tiles_of(nk, LANES):
                col = (shift - f2 // LANES) * LANES + first
                s = raw[f2 : f2 + r2] + g * t_scr[hh, 0:r2, col : col + cols]
                top = jnp.max(s, axis=0, keepdims=True)
                peak = top if peak is None else jnp.maximum(peak, top)
                scores.append(s)
            probs, mass = [], None
            for s in scores:
                p = jnp.exp(s - peak)
                part = jnp.sum(p, axis=0, keepdims=True)
                mass = part if mass is None else mass + part
                probs.append(p.astype(BF16))
            lse_ref[pl.ds(2 * pair + hh, 1), first : first + cols] = peak + jnp.log(mass)
            pb = jnp.concatenate(probs, axis=0)
            if flip:
                parts.append(dotf(vt[hh * half : (hh + 1) * half], pb, NN) / mass)
            else:
                x = dotf(pb, vzs[hh], TN)
                total = x if total is None else total + x
                scales.append(1.0 / mass)
        if flip:
            o = jnp.concatenate(parts, axis=0).T
        else:
            o = total * jnp.where(low_rows, scales[0], scales[1]).T
        o_ref[first : first + cols, :] = o
        ob_ref[first : first + cols, :] = o.astype(BF16)


def attend_forward(
    u, q, k, v, qa, ka, g, cols, pairs, tile, flip, into, row_block, us, deps=()
):
    nq, nk = qa.shape[0], ka.shape[0]
    heads, width = u.shape
    col = lambda c: (lambda p: (0, c + p))
    fix = lambda p: (0, 0)
    out_spec = pl.BlockSpec((nq, LANES), lambda p: (row_block, p))
    return pl.pallas_call(
        ignoring(functools.partial(forward_kernel, tile, flip), 7, len(into) + len(deps)),
        grid=(pairs,),
        in_specs=[
            pl.BlockSpec(u.shape, fix),
            pl.BlockSpec((nq, LANES), col(cols[0])),
            pl.BlockSpec((nk, LANES), col(cols[1])),
            pl.BlockSpec((nk, LANES), col(cols[2])),
            pl.BlockSpec((nq, LANES), fix),
            pl.BlockSpec((nk, LANES), fix),
            pl.BlockSpec(g.shape, fix),
        ]
        + [ANY_SPEC] * (len(into) + len(deps)),
        out_specs=[out_spec, out_spec, pl.BlockSpec((heads, nq), fix)],
        out_shape=[
            jax.ShapeDtypeStruct(into[0].shape, BF16),
            jax.ShapeDtypeStruct(into[0].shape, F32),
            jax.ShapeDtypeStruct((heads, nq), F32),
        ],
        input_output_aliases={7 + i: i for i in range(len(into))},
        scratch_shapes=[pltpu.VMEM((2, LANES, width), F32)],
        compiler_params=pltpu.CompilerParams(vmem_limit_bytes=40 * 2**20),
        cost_estimate=cost(us),
        name="attention_forward",
    )(u, q, k, v, qa, ka, g, *into, *deps)


def backward_kernel(
    start, begin, u_ref, q_ref, k_ref, v_ref, do_ref, att_ref, qa_ref, ka_ref, g_ref, lse_ref,
    gate_in, diag_in, dq_ref, dkv_ref, col_ref, gate_ref, diag_ref, t_scr, c_scr,
):
    nq, nk, width = q_ref.shape[0], k_ref.shape[0], u_ref.shape[-1]
    step = pl.program_id(0)
    shift = -(-nk // LANES)

    @pl.when(step == 0)
    def _():
        gate_ref[...] = jnp.zeros_like(gate_ref) if begin else gate_in[...]
        diag_ref[...] = jnp.zeros_like(diag_ref) if begin else diag_in[...]

    low = lax.broadcasted_iota(jnp.int32, (1, LANES), 1) < LANES // 2
    k, v, q, do = k_ref[...], v_ref[...], q_ref[...], do_ref[...]
    prod = (do.astype(F32) * att_ref[...]).T
    zero = jnp.zeros((), BF16)
    dq, dk, dv = None, None, None
    for hh in range(2):
        head = pl.ds(2 * (start + step) + hh, 1)
        t_scr[hh] = table_rows_of(u_ref[head, :], width)
        c_scr[hh] = jnp.zeros_like(c_scr[hh])
        sel = low if hh == 0 else jnp.logical_not(low)
        delta = jnp.sum(prod[hh * (LANES // 2) : (hh + 1) * (LANES // 2)], axis=0, keepdims=True)
        ka = jnp.where(sel, k, ka_ref[...])
        qa = jnp.where(sel, q, qa_ref[...])
        kz, qz, doz = jnp.where(sel, k, zero), jnp.where(sel, q, zero), jnp.where(sel, do, zero)
        lse = lse_ref[head, :]
        g = g_ref[head, :]
        gate = jnp.zeros((1, nq), F32)
        raw = dotf(ka, qa, NT)
        dp = dotf(v, doz, NT)
        ps, ds = [], []
        for first, rows in tiles_of(nk, LANES):
            col = (shift - first // LANES) * LANES
            t = t_scr[hh, 0:rows, col : col + nq]
            p = jnp.exp(raw[first : first + rows] + (g * t - lse))
            d = p * (dp[first : first + rows] - delta)
            gate += jnp.sum(d * t, axis=0, keepdims=True)
            c_scr[hh, 0:rows, col : col + nq] += d * g
            ps.append(p.astype(BF16))
            ds.append(d.astype(BF16))
        pb, db = jnp.concatenate(ps, axis=0), jnp.concatenate(ds, axis=0)
        dk_add, dv_add, dq_add = dotf(db, qz, NN), dotf(pb, doz, NN), dotf(db, kz, TN)
        dk = dk_add if dk is None else dk + dk_add
        dv = dv_add if dv is None else dv + dv_add
        dq = dq_add if dq is None else dq + dq_add
        gate_ref[head, :] = gate
        half = LANES // 2
        acc = c_scr[hh]
        while half >= 8:
            acc = acc[:half] + pltpu.roll(acc[half:], width - half, 1)
            half //= 2
        row = lax.broadcasted_iota(jnp.int32, (8, 1), 0)
        for bit in (1, 2, 4):
            acc = jnp.where((row & bit) != 0, pltpu.roll(acc, width - bit, 1), acc)
        diag_ref[head, :] += jnp.sum(acc, axis=0, keepdims=True)
    dq_ref[...] = (dq.astype(BF16) * (LANES // 2) ** -0.5).astype(BF16)
    dkv_ref[0] = dk.astype(BF16)
    dkv_ref[1] = dv.astype(BF16)
    col_ref[0:1, :] = jnp.sum(dq, axis=0, keepdims=True) * (LANES // 2) ** -0.5
    col_ref[1:2, :] = jnp.sum(dv, axis=0, keepdims=True)


def attend_backward(
    u, q, k, v, do, att, qa, ka, g, lse, gate, diag, cols, pairs, row_block, us,
    start, count, into=(), deps=(),
):
    nq, nk = qa.shape[0], ka.shape[0]
    heads, width = u.shape
    col = lambda c: (lambda p: (0, c + start + p))
    row = lambda p: (row_block, start + p)
    fix = lambda p: (0, 0)
    return pl.pallas_call(
        ignoring(functools.partial(backward_kernel, start, start == 0), 12, len(into) + len(deps)),
        grid=(count,),
        in_specs=[
            pl.BlockSpec(u.shape, fix),
            pl.BlockSpec((nq, LANES), col(cols[0])),
            pl.BlockSpec((nk, LANES), col(cols[1])),
            pl.BlockSpec((nk, LANES), col(cols[2])),
            pl.BlockSpec((nq, LANES), row),
            pl.BlockSpec((nq, LANES), row),
            pl.BlockSpec((nq, LANES), fix),
            pl.BlockSpec((nk, LANES), fix),
            pl.BlockSpec(g.shape, fix),
            pl.BlockSpec(lse.shape, fix),
            pl.BlockSpec(gate.shape, fix),
            pl.BlockSpec(diag.shape, fix),
        ]
        + [ANY_SPEC] * (len(into) + len(deps)),
        out_specs=[
            pl.BlockSpec((nq, LANES), col(0)),
            pl.BlockSpec((2, nk, LANES), lambda p: (0, 0, start + p)),
            pl.BlockSpec((2, LANES), col(0)),
            pl.BlockSpec(gate.shape, fix),
            pl.BlockSpec(diag.shape, fix),
        ],
        out_shape=[
            jax.ShapeDtypeStruct((nq, pairs * LANES), BF16),
            jax.ShapeDtypeStruct((2, nk, pairs * LANES), BF16),
            jax.ShapeDtypeStruct((2, pairs * LANES), F32),
            jax.ShapeDtypeStruct(gate.shape, F32),
            jax.ShapeDtypeStruct(diag.shape, F32),
        ],
        input_output_aliases={12 + i: i for i in range(len(into))},
        scratch_shapes=[pltpu.VMEM((2, LANES, width), F32), pltpu.VMEM((2, LANES, width), F32)],
        compiler_params=pltpu.CompilerParams(vmem_limit_bytes=60 * 2**20),
        cost_estimate=cost(us),
        name="attention_backward",
    )(u, q, k, v, do, att, qa, ka, g, lse, gate, diag, *into, *deps)


def own_kernel(
    p0_ref, p1_ref, p2_ref, p3_ref, loc_ref, mine_ref, other_ref, dirs_ref, scale_ref, core_ref, place_ref,
    out_ref, w_ref, small_ref, x_ref, qa_ref, ka_ref, ql_ref, kl_ref, ga_ref, gl_ref, g0_ref, g1_ref,
    x_scr, seg_scr, all_scr,
):
    step = pl.program_id(0)
    width = loc_ref.shape[1]
    block = loc_ref.shape[0]
    own = out_ref.shape[0]
    cut = 3 * width // 2
    rows = scale_ref.shape[0]

    lane = lax.broadcasted_iota(jnp.int32, (1, LANES), 1)
    lane = jnp.where(lane >= LANES // 2, lane - LANES // 2, lane).astype(F32)
    penalty = lambda seg: jnp.where((lane < 4.0) & (lane != seg), -1e30, 0.0).astype(BF16)

    def unpack(first, second):
        w_ref[:, 0:cut] = first[:, 0:cut]
        w_ref[:, cut : 2 * cut] = second[:, 0:cut]
        small_ref[...] = first[:, cut : cut + SMALL].astype(F32).T[0 : small_ref.shape[0]]

    def gates(x, ref, value_ref):
        logits = dotf(dirs_ref[...], x, NT)
        count = 2 * rows
        logits = logits[:count] + (logits[count : 2 * count] + logits[2 * count :])
        sig = 1.0 / (1.0 + jnp.exp(-logits))
        a, b = sig[:rows], sig[rows:]
        ref[0] = a
        ref[1] = b
        value_ref[...] = a * (b * scale_ref[...] - 1.0) + 2.0

    @pl.when((step == 0) & (core_ref[0] == 0))
    def _():
        unpack(mine_ref, other_ref)

    @pl.when((step == 0) & (core_ref[0] != 0))
    def _():
        unpack(other_ref, mine_ref)

    @pl.when(step == 0)
    def _():
        for s, ref in enumerate((p0_ref, p1_ref, p2_ref, p3_ref)):
            here = pl.ds(pl.multiple_of((place_ref[0] ^ s) * block, 8), block)
            x_scr[here, :] = ref[0:block, :].astype(F32)
            for row, scr in ((block, seg_scr), (block + 1, all_scr)):
                seg = ref[row : row + 1, 0 : 2 * LANES].astype(F32)
                seg = jnp.broadcast_to(seg, (LANES, 2 * LANES)).T[0:block]
                scr[here, :] = seg
                if s == 0 and row > block:
                    ql_ref[...] = penalty(seg)
        x_scr[own : own + block, :] = loc_ref[...].astype(F32)
        x_scr[own + block :, :] = jnp.zeros((x_scr.shape[0] - own - block, width), F32)
        x_ref[...] = x_scr[...].astype(BF16)
        qa_ref[...] = penalty(seg_scr[...])
        ka_ref[...] = jnp.where(lane == seg_scr[...], 1.0, 0.0).astype(BF16)
        kl_ref[...] = jnp.where(lane == all_scr[...], 1.0, 0.0).astype(BF16)
        gates(x_ref[0:own, :], ga_ref, g0_ref)
        gates(loc_ref[...], gl_ref, g1_ref)

    bias = jnp.where(step == 0, small_ref[0:1, :], jnp.where(step == 2, small_ref[1:2, :], 0.0))
    scale = jnp.where(step == 0, (LANES // 2) ** -0.5, 1.0)
    w = w_ref[:, pl.ds(pl.multiple_of(step * width, LANES), width)]
    out_ref[...] = ((dotf(x_ref[0:own, :], w, NN) + bias) * scale).astype(BF16)


def project_own(packs, loc, mine, other, dirs, scale, core, place, total):
    block, width = loc.shape
    own = len(packs) * block
    rows = scale.shape[0]
    fix = lambda c: (0, 0)
    full = lambda shape: pl.BlockSpec(shape, lambda c: (0,) * len(shape))
    shapes = [
        ((own, 3 * width), BF16),
        ((width, 3 * width), BF16),
        ((16, width), F32),
        ((total, width), BF16),
        ((own, LANES), BF16),
        ((own, LANES), BF16),
        ((block, LANES), BF16),
        ((own, LANES), BF16),
        ((2, rows, own), F32),
        ((2, rows, block), F32),
        ((rows, own), F32),
        ((rows, block), F32),
    ]
    return pl.pallas_call(
        own_kernel,
        grid=(3,),
        in_specs=[full(p.shape) for p in packs]
        + [full(v.shape) for v in (loc, mine, other, dirs, scale)]
        + [SMEM_SPEC, SMEM_SPEC],
        out_specs=[pl.BlockSpec((own, width), lambda c: (0, c))] + [full(s) for s, _ in shapes[1:]],
        out_shape=[jax.ShapeDtypeStruct(s, t) for s, t in shapes],
        scratch_shapes=[pltpu.VMEM((total, width), F32)] + [pltpu.VMEM((own, LANES), F32)] * 2,
        compiler_params=pltpu.CompilerParams(vmem_limit_bytes=40 * 2**20),
        cost_estimate=cost(10),
        name="projection_own",
    )(*packs, loc, mine, other, dirs, scale, core, place)


def project_shared_kernel(all_ref, loc_ref, w_ref, b_ref, q_out, kv_out):
    step = pl.program_id(0)

    @pl.when(step == 0)
    def _():
        q = dotf(loc_ref[...], w_ref[...], NN) + b_ref[0:1, :]
        q_out[...] = (q * (LANES // 2) ** -0.5).astype(BF16)

    @pl.when(step > 0)
    def _():
        bias = jnp.where(step == 2, b_ref[1:2, :], 0.0)
        kv_out[...] = (dotf(all_ref[...], w_ref[...], NN) + bias).astype(BF16)


def project_shared(x_all, x_loc, weight, small, deps=()):
    n_all, width = x_all.shape
    n_loc = x_loc.shape[0]
    fix = lambda c: (0, 0)
    return pl.pallas_call(
        ignoring(project_shared_kernel, 4, len(deps)),
        grid=(3,),
        in_specs=[
            pl.BlockSpec((n_all, width), fix),
            pl.BlockSpec((n_loc, width), fix),
            pl.BlockSpec((width, width), lambda c: (0, c)),
            pl.BlockSpec(small.shape, fix),
        ]
        + [ANY_SPEC] * len(deps),
        out_specs=[
            pl.BlockSpec((n_loc, width), fix),
            pl.BlockSpec((n_all, width), lambda c: (0, jnp.maximum(c - 1, 0))),
        ],
        out_shape=[
            jax.ShapeDtypeStruct((n_loc, width), BF16),
            jax.ShapeDtypeStruct((n_all, 2 * width), BF16),
        ],
        compiler_params=pltpu.CompilerParams(vmem_limit_bytes=16 * 2**20),
        cost_estimate=cost(5),
        name="projection_shared",
    )(x_all, x_loc, weight, small, *deps)


def gelu_parts(x):
    size = jnp.abs(x)
    t = 1.0 / (1.0 + (0.3275911 * 0.7071067811865476) * size)
    poly = t * (
        0.254829592
        + t * (-0.284496736 + t * (1.421413741 + t * (-1.453152027 + t * 1.061405429)))
    )
    bell = jnp.exp(-0.5 * x * x)
    tail = 0.5 * poly * bell
    phi = jnp.where(x >= 0, 1.0 - tail, tail)
    return x * phi, phi + x * bell * 0.3989422804014327


def mean_last(v):
    return jnp.sum(v, axis=-1, keepdims=True) * (1.0 / v.shape[-1])


def layer_kernel(
    chunks, tile,
    x_ref, a_ref, c0_ref, c1_ref, c2_ref, c3_ref, cl_ref, wom_ref, woo_ref, mine_ref, other_ref, vec_ref,
    core_ref, place_ref,
    h_ref, ga_ref, g1_ref, keep_ref, send_ref, sums_ref,
    c_scr, z_scr, r_scr, nh_scr, acc_scr, di_scr, act_scr, der_scr, ih_scr, wo_ref, up_ref, down_ref,
):
    step = pl.program_id(0)
    total, width = x_ref.shape
    half = width // 2
    low_core = core_ref[0] == 0
    high_core = core_ref[0] != 0

    vec = lambda i: vec_ref[i : i + 1, :]

    def over_tiles(body):
        @pl.loop(0, total // tile)
        def _(i):
            body(pl.ds(pl.multiple_of(i * tile, tile), tile))

    def add_sum(row, value):
        sums_ref[row : row + 1, :] += jnp.sum(value, axis=0, keepdims=True)

    def load(ref, is_mine):
        @pl.when(is_mine)
        def _():
            ref[...] = mine_ref[...]

        @pl.when(jnp.logical_not(is_mine))
        def _():
            ref[...] = other_ref[...]

    def emit(is_mine, value, cols=slice(None)):
        @pl.when(is_mine)
        def _():
            keep_ref[:, cols] = value

        @pl.when(jnp.logical_not(is_mine))
        def _():
            send_ref[:, cols] = value

    back = jnp.maximum(step - chunks, 0)
    j = back // 2
    forth = step < chunks
    even = (step >= chunks) & (step < 3 * chunks) & (back % 2 == 0)
    odd = (step >= chunks) & (step < 3 * chunks) & (back % 2 == 1)

    @pl.when(step == 0)
    def _():
        sums_ref[...] = jnp.zeros_like(sums_ref)

        @pl.when(low_core)
        def _():
            wo_ref[:, 0:half] = wom_ref[...]
            wo_ref[:, half:width] = woo_ref[...]

        @pl.when(high_core)
        def _():
            wo_ref[:, 0:half] = woo_ref[...]
            wo_ref[:, half:width] = wom_ref[...]

        def body(here):
            y = dotf(a_ref[here, :], wo_ref[...], NN) + vec(2) + x_ref[here, :].astype(F32)
            y = y - mean_last(y)
            r = lax.rsqrt(mean_last(y * y) + EPS_NORM)
            z = y * r
            z_scr[here, :] = z
            r_scr[here, :] = r
            nh_scr[here, :] = (z * vec(6) + vec(4)).astype(BF16)
            acc_scr[here, :] = jnp.zeros_like(z)

        for first, rows in tiles_of(total, tile):
            body(slice(first, first + rows))

    @pl.when(forth | odd)
    def _():
        load(up_ref, low_core)

    @pl.when(forth | even)
    def _():
        load(down_ref, high_core)

    @pl.when(forth)
    def _():
        bias = vec_ref[pl.ds(8 + step, 1), :]
        parts = [slice(first, first + rows) for first, rows in tiles_of(total, 256)]
        ahead = dotf(nh_scr[parts[0], :], up_ref[...], NN) + bias
        for i, here in enumerate(parts):
            inner = ahead
            if i + 1 < len(parts):
                ahead = dotf(nh_scr[parts[i + 1], :], up_ref[...], NN) + bias
            act, der = gelu_parts(inner)
            act = act.astype(BF16)
            act_scr[step, here, :] = act
            der_scr[step, here, :] = der.astype(BF16)
            acc_scr[here, :] += dotf(act, down_ref[...], NN)

    @pl.when(step == chunks)
    def _():
        block = cl_ref.shape[0]
        for s, ref in enumerate((c0_ref, c1_ref, c2_ref, c3_ref)):
            there = pl.ds(pl.multiple_of((place_ref[0] ^ s) * block, 8), block)
            c_scr[there, :] = ref[...].astype(F32)
        c_scr[4 * block : 5 * block, :] = cl_ref[...].astype(F32)
        c_scr[5 * block :, :] = jnp.zeros((total - 5 * block, width), F32)

        def body(here):
            v = z_scr[here, :] * vec(6) + vec(4) + acc_scr[here, :] + vec(3)
            v = v - mean_last(v)
            r = lax.rsqrt(mean_last(v * v) + EPS_NORM)
            z = v * r
            h_ref[here, :] = (z * vec(7) + vec(5)).astype(BF16)
            c = c_scr[here, :]
            q = c * vec(7)
            gt = r * (q - mean_last(q) - z * mean_last(q * z))
            acc_scr[here, :] = gt
            di_scr[here, :] = gt.astype(BF16)
            add_sum(3, gt)
            add_sum(5, c)
            add_sum(7, c * z)

        over_tiles(body)

    @pl.when(even)
    def _():
        emit(high_core, dotf(act_scr[j], di_scr[...], TN).astype(BF16))

        def body(here):
            gi = dotf(di_scr[here, :], down_ref[...], NT) * der_scr[j, here, :].astype(F32)
            sums_ref[pl.ds(8 + j, 1), :] += jnp.sum(gi, axis=0, keepdims=True)
            ih_scr[here, :] = gi.astype(BF16)

        over_tiles(body)

    @pl.when(odd)
    def _():
        emit(low_core, dotf(nh_scr[...], ih_scr[...], TN).astype(BF16))

        def body(here):
            acc_scr[here, :] += dotf(ih_scr[here, :], up_ref[...], NT)

        over_tiles(body)

    @pl.when(step == 3 * chunks)
    def _():
        def body(here):
            gn = acc_scr[here, :]
            z = z_scr[here, :]
            q = gn * vec(6)
            g1 = r_scr[here, :] * (q - mean_last(q) - z * mean_last(q * z))
            g1_ref[here, :] = g1
            ah = g1.astype(BF16)
            di_scr[here, :] = ah
            ga_ref[here, :] = dotf(ah, wo_ref[...], NT).astype(BF16)
            add_sum(2, g1)
            add_sum(4, gn)
            add_sum(6, gn * z)

        for first, rows in tiles_of(total, tile):
            body(slice(first, first + rows))
        out = dotf(a_ref[...], di_scr[...], TN).astype(BF16)
        emit(low_core, out[:, 0:half], slice(0, half))
        emit(high_core, out[:, half:width], slice(0, half))


def layer_rest(x, att, cot, mine, other, vec, core, place, chunks):
    total, width = x.shape
    fix = lambda s: (0, 0)
    once = pl.Buffered(buffer_count=1)

    def chunk_of(s):
        return jnp.where(s < chunks, s, jnp.clip((s - chunks) // 2, 0, chunks - 1))

    def const(shape):
        return pl.BlockSpec(shape, fix, pipeline_mode=once)

    rows = const((total, width))
    square = (width, width)
    out_half = pl.BlockSpec((width, width // 2), lambda s: (0, 2 * chunks), pipeline_mode=once)
    weight_spec = pl.BlockSpec(square, lambda s: (0, chunk_of(s)))
    grad_spec = pl.BlockSpec(square, lambda s: (0, jnp.maximum(s - chunks, 0) // 2))
    return pl.pallas_call(
        functools.partial(layer_kernel, chunks, 512),
        grid=(3 * chunks + 1,),
        in_specs=[
            rows, rows, *[const(v.shape) for v in cot],
            out_half, out_half, weight_spec, weight_spec, const(vec.shape), SMEM_SPEC, SMEM_SPEC,
        ],
        out_specs=[rows, rows, rows, grad_spec, grad_spec, const(vec.shape)],
        out_shape=[
            jax.ShapeDtypeStruct((total, width), BF16),
            jax.ShapeDtypeStruct((total, width), BF16),
            jax.ShapeDtypeStruct((total, width), F32),
            jax.ShapeDtypeStruct(mine.shape, BF16),
            jax.ShapeDtypeStruct(mine.shape, BF16),
            jax.ShapeDtypeStruct(vec.shape, F32),
        ],
        scratch_shapes=[
            pltpu.VMEM((total, width), F32),
            pltpu.VMEM((total, width), F32),
            pltpu.VMEM((total, 1), F32),
            pltpu.VMEM((total, width), BF16),
            pltpu.VMEM((total, width), F32),
            pltpu.VMEM((total, width), BF16),
            pltpu.VMEM((chunks, total, width), BF16),
            pltpu.VMEM((chunks, total, width), BF16),
            pltpu.VMEM((total, width), BF16),
            pltpu.VMEM(square, BF16),
            pltpu.VMEM(square, BF16),
            pltpu.VMEM(square, BF16),
        ],
        compiler_params=pltpu.CompilerParams(vmem_limit_bytes=60 * 2**20),
        cost_estimate=cost(70),
        name="layer_rest",
    )(x, att, *cot, mine, other, mine, other, vec, core, place)


def settle_kernel(b0_ref, b1_ref, b2_ref, b3_ref, *rest):
    place_ref, out_ref = rest[-2:]
    for s, ref in enumerate((b0_ref, b1_ref, b2_ref, b3_ref)):
        out_ref[place_ref[0] ^ s] = ref[...]
    total = rest[0][...]
    for ref in rest[1:-2]:
        total = total + ref[...].astype(F32)
    out_ref[4] = total.astype(out_ref.dtype)


def settle(blocks, last, last_block, place):
    block, width = blocks[1].shape
    one = pl.BlockSpec((block, width), lambda s: (0, 0))
    return pl.pallas_call(
        settle_kernel,
        grid=(1,),
        in_specs=[one] * 4
        + [pl.BlockSpec((block, width), lambda s: (last_block, 0))] * len(last)
        + [SMEM_SPEC],
        out_specs=pl.BlockSpec((5, block, width), lambda s: (0, 0, 0)),
        out_shape=jax.ShapeDtypeStruct((5, block, width), BF16),
        compiler_params=pltpu.CompilerParams(vmem_limit_bytes=16 * 2**20),
        cost_estimate=cost(2),
        name="settle",
    )(*blocks, *last, place)


def shared_input_kernel(
    dq_ref, dkv_ref, w_ref, base_ref, grad_ref, gate_ref, scale_ref, dirs_ref, part_ref, loc_ref, acc
):
    step = pl.program_id(0)

    @pl.when(step == 0)
    def _():
        mix = gate_mix(grad_ref[...], gate_ref, scale_ref[...])
        loc_ref[...] = base_ref[...] + dotf(mix, dirs_ref[...], TN) + dotf(dq_ref[...], w_ref[...], NT)

    @pl.when(step == 1)
    def _():
        acc[...] = dotf(dkv_ref[...], w_ref[...], NT)

    @pl.when(step == 2)
    def _():
        part_ref[...] = (acc[...] + dotf(dkv_ref[...], w_ref[...], NT)).astype(BF16)


def shared_input(dq, dkv, weight, base, base_block, grad, gate, scale, dirs):
    n_loc, width = dq.shape
    n_all = dkv.shape[1]
    fix = lambda c: (0, 0)
    return pl.pallas_call(
        shared_input_kernel,
        grid=(3,),
        in_specs=[
            pl.BlockSpec((n_loc, width), fix),
            pl.BlockSpec((None, n_all, width), lambda c: (jnp.maximum(c - 1, 0), 0, 0)),
            pl.BlockSpec((width, width), lambda c: (0, c)),
            pl.BlockSpec((n_loc, width), lambda c: (base_block, 0)),
            pl.BlockSpec(grad.shape, fix),
            pl.BlockSpec(gate.shape, lambda c: (0, 0, 0)),
            pl.BlockSpec(scale.shape, fix),
            pl.BlockSpec(dirs.shape, fix),
        ],
        out_specs=[pl.BlockSpec((n_all, width), fix), pl.BlockSpec((n_loc, width), fix)],
        out_shape=[
            jax.ShapeDtypeStruct((n_all, width), BF16),
            jax.ShapeDtypeStruct((n_loc, width), F32),
        ],
        scratch_shapes=[pltpu.VMEM((n_all, width), F32)],
        compiler_params=pltpu.CompilerParams(vmem_limit_bytes=60 * 2**20),
        cost_estimate=cost(5),
        name="shared_input",
    )(dq, dkv, weight, base, grad, gate, scale, dirs)


def weight_grad_kernel(
    x0_ref, x4_ref, loc_ref, dq_ref, dkv_ref, dq4_ref, dkv4_ref, core_ref, keep_ref, send_ref
):
    step = pl.program_id(0)
    width = x0_ref.shape[1]
    half = width // 2
    cut = 3 * half
    low_core = core_ref[0] == 0
    high_core = core_ref[0] != 0

    def emit(is_mine, cols, value):
        @pl.when(is_mine)
        def _():
            keep_ref[:, cols] = value

        @pl.when(jnp.logical_not(is_mine))
        def _():
            send_ref[:, cols] = value

    @pl.when(step == 0)
    def _():
        grad = dotf(x0_ref[...], dq_ref[...], TN) + dotf(loc_ref[...], dq4_ref[...], TN)
        emit(low_core, slice(0, width), grad.astype(BF16))

    @pl.when(step > 0)
    def _():
        grad = dotf(x0_ref[...], dkv_ref[...], TN) + dotf(x4_ref[...], dkv4_ref[...], TN)
        grad = grad.astype(BF16)

        @pl.when(step == 1)
        def _():
            emit(low_core, slice(width, cut), grad[:, 0:half])
            emit(high_core, slice(0, half), grad[:, half:width])

        @pl.when(step == 2)
        def _():
            emit(high_core, slice(half, cut), grad)


def weight_grad(x_cat, x_all, x_loc, dq, dkv, dq4, dkv4, core, deps=()):
    own, width = dq.shape
    n_all, n_loc = x_all.shape[0], x_loc.shape[0]
    fix = lambda c: (0, 0)
    half = lambda c: (jnp.maximum(c - 1, 0), 0, 0)
    shape = (width, 3 * width // 2)
    return pl.pallas_call(
        ignoring(weight_grad_kernel, 8, len(deps)),
        grid=(3,),
        in_specs=[
            pl.BlockSpec((own, width), fix),
            pl.BlockSpec((n_all, width), fix),
            pl.BlockSpec((n_loc, width), fix),
            pl.BlockSpec((own, width), fix),
            pl.BlockSpec((None, own, width), half),
            pl.BlockSpec((n_loc, width), fix),
            pl.BlockSpec((None, n_all, width), half),
            SMEM_SPEC,
        ]
        + [ANY_SPEC] * len(deps),
        out_specs=[pl.BlockSpec(shape, fix)] * 2,
        out_shape=[jax.ShapeDtypeStruct(shape, BF16)] * 2,
        compiler_params=pltpu.CompilerParams(vmem_limit_bytes=24 * 2**20),
        cost_estimate=cost(10),
        name="projection_weight_grad",
    )(x_cat, x_all, x_loc, dq, dkv, dq4, dkv4, core, *deps)


def gate_parts(grad, gate_ref, c):
    a, b = gate_ref[0], gate_ref[1]
    return thirds(grad * (b * c - 1.0) * a * (1.0 - a)), thirds(grad * a * c * b * (1.0 - b))


def gate_mix(grad, gate_ref, c):
    da, db = gate_parts(grad, gate_ref, c)
    return jnp.concatenate([da[0], db[0], da[1], db[1], da[0], db[0]], axis=0)


def gate_kernel(
    buckets_used, grad0_ref, grad1_ref, gate0_ref, gate1_ref, scale_ref, diag0_ref, diag1_ref, slots_ref, x_ref, loc_ref,
    col0_ref, col1_ref, sums_ref, turn_ref, flat_ref,
):
    c = scale_ref[...]
    rows = c.shape[0]
    head_dim = LANES // 2
    turned = diag1_ref[...]
    turned = jnp.concatenate(
        [turned, jnp.zeros((rows, diag0_ref.shape[1] - turned.shape[1]), F32)], axis=1
    )
    diag = diag0_ref[...] + pltpu.roll(turned, turn_ref[0], 1)

    def back(grad_ref, gate_ref, x):
        grad = grad_ref[...]
        da, db = gate_parts(grad, gate_ref, c)
        d = jnp.concatenate([part for pair in zip(da, db) for part in pair], axis=0)
        return dotf(d, x, NN), jnp.sum(grad * gate_ref[0] * gate_ref[1], axis=1, keepdims=True)

    dw0, scale0 = back(grad0_ref, gate0_ref, x_ref[...])
    dw1, scale1 = back(grad1_ref, gate1_ref, loc_ref[...])
    dw = dw0 + dw1
    dw = dw[: 2 * rows] + (dw[2 * rows : 4 * rows] + dw[4 * rows :])
    lane = lax.broadcasted_iota(jnp.int32, dw.shape, 1)
    row = lax.broadcasted_iota(jnp.int32, dw.shape, 0)
    row = jnp.where(row >= rows, row - rows, row) * head_dim
    dw = jnp.where((lane >= row) & (lane < row + head_dim), dw, 0.0)
    buckets = lax.broadcasted_iota(jnp.int32, (BUCKET_ROWS, diag.shape[1]), 0)
    hot = jnp.where(buckets == slots_ref[...], 1.0, 0.0).astype(BF16)
    table = dotf(jnp.concatenate(thirds(diag), axis=0), hot, NT)
    table = table[:rows] + (table[rows : 2 * rows] + table[2 * rows :])
    half = rows // 2
    flat_ref[...] = jnp.zeros_like(flat_ref)
    flat_ref[0:rows, :] = sums_ref[...]
    flat_ref[0:2, :] = col0_ref[...] + col1_ref[...]
    flat_ref[12:13, :] = jnp.sum(dw[:rows], axis=0, keepdims=True)
    flat_ref[13:14, :] = jnp.sum(dw[rows:], axis=0, keepdims=True)
    scales = jnp.broadcast_to(scale0 + scale1, (rows, LANES))
    lane = lax.broadcasted_iota(jnp.int32, table.shape, 1)
    table = jnp.where(lane < buckets_used, table, jnp.concatenate([scales] * (BUCKET_ROWS // LANES), axis=1))
    flat_ref[rows : rows + half, 0:BUCKET_ROWS] = table[0:half]
    flat_ref[rows : rows + half, BUCKET_ROWS : 2 * BUCKET_ROWS] = table[half:]


def gate_sums(grads, gates, scale, diags, slots, x, loc, cols, sums, turn, buckets_used):
    rows, own = grads[0].shape
    width = x.shape[1]
    full = lambda v: pl.BlockSpec(v.shape, lambda s: (0,) * v.ndim)
    args = [*grads, *gates, scale, *diags, slots, x, loc, *cols, sums, turn]
    specs = [full(v) for v in args[:-1]] + [SMEM_SPEC]
    specs[8] = pl.BlockSpec((own, width), lambda s: (0, 0))
    out = jax.ShapeDtypeStruct((rows + rows // 2, width), F32)
    return pl.pallas_call(
        functools.partial(gate_kernel, buckets_used),
        grid=(1,),
        in_specs=specs,
        out_specs=full(out),
        out_shape=out,
        compiler_params=pltpu.CompilerParams(vmem_limit_bytes=20 * 2**20),
        cost_estimate=cost(4),
        name="gate_sums",
    )(*args)


def own_input_kernel(
    dq_ref, dkv_ref, w_ref, base_ref, grad_ref, gate_ref, scale_ref, dirs_ref, dx_ref, acc
):
    step = pl.program_id(0)

    @pl.when(step == 0)
    def _():
        mix = gate_mix(grad_ref[...], gate_ref, scale_ref[...])
        acc[...] = base_ref[...] + dotf(mix, dirs_ref[...], TN) + dotf(dq_ref[...], w_ref[...], NT)

    @pl.when(step == 1)
    def _():
        acc[...] += dotf(dkv_ref[...], w_ref[...], NT)

    @pl.when(step == 2)
    def _():
        dx_ref[...] = (acc[...] + dotf(dkv_ref[...], w_ref[...], NT)).astype(BF16)


def own_input(dq, dkv, weight, base, grad, gate, scale, dirs, deps=()):
    own, width = dq.shape
    fix = lambda c: (0, 0)
    return pl.pallas_call(
        ignoring(own_input_kernel, 8, len(deps)),
        grid=(3,),
        in_specs=[
            pl.BlockSpec((own, width), fix),
            pl.BlockSpec((None, own, width), lambda c: (jnp.maximum(c - 1, 0), 0, 0)),
            pl.BlockSpec((width, width), lambda c: (0, c)),
            pl.BlockSpec((own, width), fix),
            pl.BlockSpec(grad.shape, fix),
            pl.BlockSpec(gate.shape, lambda c: (0, 0, 0)),
            pl.BlockSpec(scale.shape, fix),
            pl.BlockSpec(dirs.shape, fix),
        ]
        + [ANY_SPEC] * len(deps),
        out_specs=pl.BlockSpec((own, width), fix),
        out_shape=jax.ShapeDtypeStruct((own, width), BF16),
        scratch_shapes=[pltpu.VMEM((own, width), F32)],
        compiler_params=pltpu.CompilerParams(vmem_limit_bytes=20 * 2**20),
        cost_estimate=cost(8),
        name="own_input",
    )(dq, dkv, weight, base, grad, gate, scale, dirs, *deps)


def split_sum_kernel(_bits, keep_ref, got_ref, *outs):
    step = pl.program_id(0)
    cut = outs[0].shape[1]
    total = keep_ref[...] + got_ref[...]
    first, second = total[:, :cut], total[:, cut:]

    def put(here, ref, value):
        @pl.when(here)
        def _():
            ref[...] = value

    put(step // 2 == 0, outs[0], first)
    put(step // 2 == 1, outs[1], first)
    put(step % 2 == 0, outs[2], second)
    put(step % 2 == 1, outs[3], second)


def split_sum(keep, got, bits, cut, parts):
    rows, cols = keep.shape
    block = rows // 4 // parts
    low = lambda s, bits: (s // 2) ^ bits[0]
    high = lambda s, bits: (s % 2) ^ bits[1]
    wide = pl.BlockSpec(
        (block, cols), lambda s, t, bits: ((2 * high(s, bits) + low(s, bits)) * parts + t, 0)
    )
    at = lambda index, s, t, first, last: (
        index * parts + jnp.where(s < first, 0, jnp.where(s > last, parts - 1, t)), 0
    )
    stay = lambda s, t, bits: at(jnp.where(s < 2, s, 1) ^ bits[1], s, t, 0, 1)
    go = lambda s, t, bits: at(jnp.where(s < 2, 0, s - 2) ^ bits[1], s, t, 2, 3)
    stay_other = lambda s, t, bits: (
        jnp.where(s % 2 == 0, low(s, bits) * parts + t, low(s, bits) * parts + parts - 1), 0
    )
    go_other = lambda s, t, bits: (
        jnp.where(s % 2 == 1, low(s, bits) * parts + t, low(s, bits) * parts), 0
    )
    return pl.pallas_call(
        split_sum_kernel,
        grid_spec=pltpu.PrefetchScalarGridSpec(
            num_scalar_prefetch=1,
            grid=(4, parts),
            in_specs=[wide, wide],
            out_specs=[
                pl.BlockSpec((block, cut), stay),
                pl.BlockSpec((block, cut), go),
                pl.BlockSpec((block, cols - cut), stay_other),
                pl.BlockSpec((block, cols - cut), go_other),
            ],
        ),
        out_shape=[jax.ShapeDtypeStruct((rows // 2, cut), BF16)] * 2
        + [jax.ShapeDtypeStruct((rows // 2, cols - cut), BF16)] * 2,
        compiler_params=pltpu.CompilerParams(vmem_limit_bytes=60 * 2**20),
        cost_estimate=cost(3),
        name="split_sum",
    )(bits, keep, got)


def merge_kernel(_bits, a0_ref, a1_ref, b0_ref, b1_ref, out_ref):
    step = pl.program_id(0)
    cut = a0_ref.shape[1]

    def put(here, cols, ref):
        @pl.when(here)
        def _():
            out_ref[:, cols] = ref[...]

    put(step // 2 == 0, slice(0, cut), a0_ref)
    put(step // 2 == 1, slice(0, cut), a1_ref)
    put(step % 2 == 0, slice(cut, None), b0_ref)
    put(step % 2 == 1, slice(cut, None), b1_ref)


def merge(first, second, bits):
    rows, cut = first[0].shape
    rest = second[0].shape[1]
    block = rows // 2
    low = lambda s, bits: (s % 2) ^ bits[0]
    high = lambda s, bits: (s // 2) ^ bits[1]
    own = lambda s, bits: (jnp.where(s < 2, s % 2, 1) ^ bits[0], 0)
    other = lambda s, bits: (jnp.where(s < 2, 0, s % 2) ^ bits[0], 0)
    beside = lambda s, bits: (high(s, bits), 0)
    return pl.pallas_call(
        merge_kernel,
        grid_spec=pltpu.PrefetchScalarGridSpec(
            num_scalar_prefetch=1,
            grid=(4,),
            in_specs=[
                pl.BlockSpec((block, cut), own),
                pl.BlockSpec((block, cut), other),
                pl.BlockSpec((block, rest), beside),
                pl.BlockSpec((block, rest), beside),
            ],
            out_specs=pl.BlockSpec(
                (block, cut + rest), lambda s, bits: (2 * high(s, bits) + low(s, bits), 0)
            ),
        ),
        out_shape=jax.ShapeDtypeStruct((2 * rows, cut + rest), BF16),
        compiler_params=pltpu.CompilerParams(vmem_limit_bytes=16 * 2**20),
        cost_estimate=cost(3),
        name="merge",
    )(bits, *first, *second)


def split_four_kernel(_own, keep_ref, got_ref, *outs):
    total = keep_ref[...] + got_ref[...]
    for s, ref in enumerate(outs):
        @pl.when(pl.program_id(0) == s)
        def _():
            ref[...] = total


def split_four(keep, got, own):
    rows, cols = keep.shape
    block = rows // 4
    there = pl.BlockSpec((block, cols), lambda s, own: (s ^ own[0], 0))
    return pl.pallas_call(
        split_four_kernel,
        grid_spec=pltpu.PrefetchScalarGridSpec(
            num_scalar_prefetch=1,
            grid=(4,),
            in_specs=[there, there],
            out_specs=[pl.BlockSpec((block, cols), lambda s, own: (0, 0))] * 4,
        ),
        out_shape=[jax.ShapeDtypeStruct((block, cols), BF16)] * 4,
        compiler_params=pltpu.CompilerParams(vmem_limit_bytes=16 * 2**20),
        cost_estimate=cost(2),
        name="split_four",
    )(own, keep, got)


def finish_kernel(a_ref, b_ref, first_ref, bias_ref, gain_ref, up_ref, table_ref, gate_ref, scale_ref):
    flat = a_ref[...] + b_ref[...]
    width = flat.shape[1]
    rows = flat.shape[0] * 2 // 3
    heads, count = table_ref.shape
    local_rows = bias_ref.shape[1]
    local = pltpu.roll(flat[:rows], width - first_ref[0], 1)[:, 0:LANES]
    bias_ref[...] = local[0:6, 0:local_rows]
    gain_ref[...] = local[6:8, 0:local_rows]
    up_ref[...] = local[8 : 8 + up_ref.shape[0], 0:local_rows]
    table = jnp.concatenate(
        [flat[rows:, 0:BUCKET_ROWS], flat[rows:, BUCKET_ROWS : 2 * BUCKET_ROWS]], axis=0
    )
    table_ref[...] = table[0:heads, 0:count]
    scale_ref[...] = table.T[count : count + 1, 0:heads]
    folded = flat[8:16, 0:LANES]
    for k in range(1, width // LANES):
        folded = folded + flat[8:16, k * LANES : (k + 1) * LANES]
    folded = (folded + pltpu.roll(folded, LANES // 2, 1))[:, 0 : LANES // 2]
    row = lax.broadcasted_iota(jnp.int32, gate_ref.shape, 0)
    gate_ref[...] = jnp.where(row < gate_ref.shape[0] // 2, folded[4:5], folded[5:6])


def finish(flat, other, first_row, local_rows, chunks, table_shape, gate_shape):
    shapes = [
        (6, local_rows), (2, local_rows), (chunks, local_rows), table_shape[::-1], gate_shape[::-1],
        (1, table_shape[1]),
    ]
    full = lambda s: pl.BlockSpec(s, lambda i: (0, 0))
    return pl.pallas_call(
        finish_kernel,
        grid=(1,),
        in_specs=[full(flat.shape), full(flat.shape), SMEM_SPEC],
        out_specs=[full(s) for s in shapes],
        out_shape=[jax.ShapeDtypeStruct(s, F32) for s in shapes],
        cost_estimate=cost(1),
        name="finish",
    )(flat, other, first_row)


hold = lax.optimization_barrier


def after(value, *earlier):
    return lax.optimization_barrier((value,) + earlier)[0]


def swap(array, axis, bit):
    size = lax.axis_size(axis)
    return lax.ppermute(array, axis, [(i, i ^ (1 << bit)) for i in range(size)])


def swap_places(array, mask):
    return lax.ppermute(array, "blk", [(i, i ^ mask) for i in range(lax.axis_size("blk"))])


def by_place(arrays):
    place = lax.axis_index("blk")
    odd, upper = (place & 1) == 1, (place >> 1) == 1
    near = [jnp.where(odd, arrays[1 - i], arrays[i]) for i in range(2)]
    far = [jnp.where(odd, arrays[3 - i], arrays[2 + i]) for i in range(2)]
    return [jnp.where(upper, f, n) for f, n in zip(far, near)] + [
        jnp.where(upper, n, f) for f, n in zip(far, near)
    ]


def bit_of(axis, bit):
    return (lax.axis_index(axis) >> bit) & 1


def bit_count(axis):
    count = lax.axis_size(axis).bit_length() - 1
    assert 1 << count == lax.axis_size(axis)
    return count


def join(array, axis, bit, position):
    def finish(flight):
        mine, other = flight
        upper = bit_of(axis, bit) == 1
        return jnp.stack(
            [jnp.where(upper, other, mine), jnp.where(upper, mine, other)], axis=position
        )

    return (array, swap(array, axis, bit)), finish


def at_once(step):
    flight, finish = step
    return finish(flight)


def together(steps):
    flights, finishes = zip(*steps)
    return flights, lambda done: [finish(flight) for finish, flight in zip(finishes, done)]


def gather_begin(first, second):
    low = bit_of("rows", 0) == 0
    keep, send = jnp.where(low, first, second), jnp.where(low, second, first)

    def finish(flight):
        mine, got = flight
        return jnp.stack([jnp.where(low, mine, got), jnp.where(low, got, mine)], axis=0)

    return (keep, swap(send, "rows", 0)), finish


def blk_bits():
    return list(reversed(range(bit_count("blk"))))


def gather_blk(part, number):
    return join(part, "blk", blk_bits()[number], 1 + number)


def halves_of(array):
    array = array.reshape(-1, array.shape[-1])
    cut = array.shape[-1] // 2 // LANES * LANES
    return [array[:, :cut], array[:, cut:]]


def orders():
    high = list(range(1, bit_count("rows")))
    return high, high[::-1]


def gather_high(halves, step):
    steps = []
    for half, order in zip(halves, orders()):
        position = sum(1 for other in order[:step] if other > order[step])
        steps.append(join(half, "rows", order[step], position))
    return together(steps)


def gather_last(halves):
    first, second = orders()
    rows = halves[0].reshape(-1, halves[0].shape[-1]).shape[0]
    if len(first) == 2 and rows % 32 == 0:
        flat = [v.reshape(-1, v.shape[-1]) for v in halves]
        flights = [(v, swap(v, "rows", order[1])) for v, order in zip(flat, (first, second))]
        bits = jnp.stack([bit_of("rows", bit) for bit in first])
        return flights, lambda flights: merge(flights[0], flights[1], bits)
    flights, finish = gather_high(halves, len(first) - 1)
    return flights, lambda flights: whole(finish(flights))


def whole(halves):
    return jnp.concatenate([h.reshape(-1, h.shape[-1]) for h in halves], axis=-1)


def added(pair):
    if len(pair) == 1:
        return pair[0]
    return pair[0] + pair[1]


def part_of(pair, index, axis):
    return added([lax.dynamic_index_in_dim(v, index, axis, keepdims=False) for v in pair])


def halve(pair, shape, axis, bit, position):
    pair = [v.reshape(shape + (-1, v.shape[-1])) for v in pair]
    mine = bit_of(axis, bit)
    return part_of(pair, mine, position), swap(part_of(pair, 1 - mine, position), axis, bit)


def scatter_begin(keep, send):
    return keep, swap(send, "rows", 0)


def scatter_first(pair):
    first, second = orders()
    rows, cols = pair[0].shape
    if len(first) == 2 and rows % 128 == 0:
        cut = halves_of(pair[0])[0].shape[1]
        bits = jnp.stack([bit_of("rows", bit) for bit in first])
        keep_a, send_a, keep_b, send_b = split_sum(pair[0], pair[1], bits, cut, 1)
        return [(keep_a, swap(send_a, "rows", first[0])), (keep_b, swap(send_b, "rows", second[0]))]
    return scatter_high([(half,) for half in halves_of(added(pair))], 0)


def scatter_high(halves, step):
    out = []
    for half, order in zip(halves, orders()):
        left = sorted(order[step:], reverse=True)
        out.append(halve(half, (2,) * len(left), "rows", order[step], left.index(order[step])))
    return out


def scatter_whole(halves):
    whole_sum = jnp.concatenate([added([v.reshape(-1, v.shape[-1]) for v in h]) for h in halves], axis=-1)
    return whole_sum


def exchange_first(blocks):
    upper = bit_of("blk", 1)
    pairs = blocks.reshape((2, 2) + blocks.shape[1:])
    keep = lax.dynamic_index_in_dim(pairs, upper, 0, keepdims=False)
    send = lax.dynamic_index_in_dim(pairs, 1 - upper, 0, keepdims=False)
    return (keep, swap_places(send, 2))


def exchange_second(flight):
    odd = bit_of("blk", 0)
    pick = lambda array, index: lax.dynamic_index_in_dim(array, index, 0, keepdims=False)
    send = jnp.stack([pick(array, 1 - odd) for array in flight])
    return (pick(flight[0], odd), pick(flight[1], odd), swap_places(send, 1))


def exchange_end(flight):
    mine, far, other = flight
    return [mine, other[0], far, other[1]]


def total_of(parts):
    return sum(v.astype(F32) for v in parts).astype(BF16)


def scatter_four(pair):
    own = bit_of("rows", 1) + 2 * bit_of("rows", 2)
    blocks = split_four(pair[0], pair[1], own.reshape(1))
    size = lax.axis_size("rows")
    return [blocks[0]] + [
        lax.ppermute(blocks[s], "rows", [(i, i ^ (2 * s)) for i in range(size)]) for s in (1, 2, 3)
    ]


def scatter_places(parts):
    place = lax.axis_index("blk")
    views = [v.reshape((2, 4, -1, v.shape[-1])) for v in parts]
    blocks = [
        total_of([lax.dynamic_index_in_dim(v, place ^ s, 1, keepdims=False) for v in views]) for s in range(4)
    ]
    return [blocks[0]] + [swap_places(blocks[s], s) for s in (1, 2, 3)]


def scatter_blk(pair, bit):
    count = bit_count("blk")
    return halve(pair, (2,) * (1 + count - bit), "blk", bit, count - bit)


def scatter_end(pair):
    core = bit_of("rows", 0)
    pair = [v.reshape((2, -1, v.shape[-1])) for v in pair]
    half = lambda index: total_of([lax.dynamic_index_in_dim(v, index, 0, keepdims=False) for v in pair])
    return half(core), swap(half(1 - core), "rows", 0)


def scatter_done(flight):
    keep, got = flight
    low = bit_of("rows", 0) == 0
    return jnp.where(low, keep, got).astype(F32), jnp.where(low, got, keep).astype(F32)


def shards(
    hidden_in,
    segment_ids,
    bucket_map,
    qkv_weight,
    out_weight,
    up_weight,
    down_weight,
    bias_cols,
    norm_gains,
    up_bias,
    rel_table,
    gate_weight,
    gate_scale,
    cotangent,
):
    row_count, block_len, width = hidden_in.shape
    heads = gate_scale.shape[0]
    pairs = heads // 2
    head_dim = width // heads
    bucket_count = rel_table.shape[0]
    cycle = lax.axis_size("blk")
    place = lax.axis_index("blk")
    core = bit_of("rows", 0).reshape(1)
    frames = block_len * cycle
    shared = row_count - 1
    used = frames + block_len
    total = -(-used // 256) * 256
    inner_width = up_weight.shape[1]
    chunks = inner_width // width
    local_rows = qkv_weight.shape[0]
    half = width // 2
    cut = 3 * half
    high_steps = len(orders()[0])
    assert row_count == cycle + 1 and cycle == 4 and bucket_count < BUCKET_ROWS

    def take(array, index):
        return lax.dynamic_index_in_dim(array, index, 0, keepdims=False)

    def with_rest(blocks, last):
        return jnp.concatenate(blocks + [last, jnp.zeros((total - used, width), BF16)], axis=0)

    extras = jnp.concatenate(
        [bias_cols, norm_gains, up_bias.reshape(local_rows, chunks)], axis=1
    )
    extras = jnp.pad(extras, ((0, 0), (0, SMALL - extras.shape[1])))
    qkv_part = at_once(
        gather_begin(
            jnp.concatenate([qkv_weight[:, :cut], extras], axis=1),
            jnp.concatenate([qkv_weight[:, cut:], jnp.zeros_like(extras)], axis=1),
        )
    )
    up_turned = up_weight.reshape(local_rows, width, chunks).transpose(0, 2, 1)
    rest_flight, rest_finish = gather_begin(
        jnp.concatenate([up_turned.reshape(local_rows, inner_width), out_weight[:, :half]], axis=1),
        jnp.concatenate([down_weight.reshape(local_rows, inner_width), out_weight[:, half:]], axis=1),
    )
    head_rows = -(-heads // 16) * 16
    picks = jnp.repeat(jnp.eye(heads, head_rows, dtype=F32), head_dim, axis=0)
    dirs = [
        picks * jnp.tile(jnp.sum(gate_weight[:, part], axis=1), heads)[:, None]
        for part in (slice(0, 4), slice(4, 8))
    ]
    dirs_high, dirs_middle, dirs_low = thirds(jnp.concatenate(dirs, axis=1).T)
    dirs_all = jnp.concatenate([dirs_high, dirs_middle, dirs_low], axis=0)
    dirs_mix = jnp.concatenate([dirs_high, dirs_high, dirs_middle], axis=0)
    scale_rows = jnp.pad(gate_scale, (0, head_rows - heads))[:, None]

    shift = -(-frames // LANES)
    span = 2 * frames - 1
    lead = shift * LANES - (frames - 1)
    table_width = 2 * shift * LANES
    narrow = -(-(shift * LANES + block_len) // LANES) * LANES
    slots = jnp.pad(bucket_map[::-1], (lead, table_width - lead - span), constant_values=-1)
    hot = (jnp.arange(bucket_count, dtype=jnp.int32)[:, None] == slots[None, :]).astype(F32)

    hidden_in, segment_ids, rest_flight, qkv_part = hold(
        (hidden_in, segment_ids, rest_flight, qkv_part)
    )
    seg_rows = jnp.pad(segment_ids.astype(BF16), ((0, 0), (0, width - block_len)))

    def with_segments(index):
        tail_rows = jnp.pad(jnp.stack([take(seg_rows, index), seg_rows[shared]]), ((0, 14), (0, 0)))
        return jnp.concatenate([take(hidden_in, index), tail_rows], axis=0)

    packs = [with_segments(place ^ s) for s in range(cycle)]
    qkv_flight, qkv_finish = gather_blk(qkv_part, 0)
    qkv_flight, rest_flight = hold((qkv_flight, rest_flight))
    qkv_flight, qkv_finish = gather_blk(qkv_finish(qkv_flight), 1)
    rest_flight, rest_finish = gather_blk(rest_finish(rest_flight), 0)
    qkv_flight, packs, rel_table, hot, cotangent = hold(
        (qkv_flight, packs, rel_table, hot, cotangent)
    )
    cot = [take(cotangent, place ^ s) for s in range(cycle)] + [cotangent[shared]]
    blank = jnp.zeros((total, width), BF16)
    packs[1] = swap_places(packs[1], 1)
    qkv_part = qkv_finish(qkv_flight)
    qkv_halves = halves_of(qkv_part)
    for step in range(high_steps - 2):
        qkv_halves = at_once(gather_high(qkv_halves, step))
    qkv_flight, qkv_finish = gather_high(qkv_halves, high_steps - 2)
    table = jnp.pad(rel_table, ((0, 0), (0, head_rows - heads)))
    u_own = lax.dot_general(table, hot, (((0,), (0,)), ((), ())), precision=HIGHEST)
    u_loc = lax.dynamic_slice_in_dim(
        jnp.pad(u_own, ((0, 0), (0, frames))), place * block_len, narrow, 1
    )
    qkv_flight, rest_flight, far_packs, cot, blank, u_own, u_loc, dirs_all, x_loc = hold(
        (qkv_flight, rest_flight, packs[2:], cot, blank, u_own, u_loc, dirs_all, hidden_in[shared])
    )
    packs = packs[:2] + list(far_packs)
    packs[2], packs[3] = swap_places(packs[2], 2), swap_places(packs[3], 3)
    qkv_flight, qkv_finish = gather_last(qkv_finish(qkv_flight))
    rest_flight, rest_finish = gather_blk(rest_finish(rest_flight), 1)
    qkv_flight, rest_flight, packs = hold((qkv_flight, rest_flight, packs))
    qkv_mine = qkv_finish(qkv_flight)
    qkv_other = swap(qkv_mine, "rows", 0)
    rest_halves = halves_of(rest_finish(rest_flight))
    for step in range(high_steps - 2):
        rest_halves = at_once(gather_high(rest_halves, step))
    rest_flight, rest_finish = gather_high(rest_halves, high_steps - 2)
    shared_flight, shared_finish = join(x_loc, "blk", 1, 0)
    own_cols = (0, pairs, 2 * pairs)
    loc_cols = (0, 0, pairs)
    place_of = place.reshape(1)
    (
        qkv_own, qkv_full, small, x_cat, qa_own, ka_own, qa_loc, ka_all, gate_own, gate_loc, g_own, g_loc,
    ) = project_own(packs, x_loc, qkv_mine, qkv_other, dirs_all, scale_rows, core, place_of, total)
    rest_flight, shared_flight, qkv_own, small, cot = hold(
        (rest_flight, shared_flight, qkv_own, small, cot)
    )
    rest_flight, rest_finish = gather_last(rest_finish(rest_flight))
    shared_flight, shared_finish = join(shared_finish(shared_flight), "blk", 0, 1)
    cot[2] = swap_places(cot[2], 2)
    att_half, att, lse_own = attend_forward(
        u_own, qkv_own, qkv_own, qkv_own, qa_own, ka_own, g_own, own_cols, pairs, frames, True,
        (blank,), 0, 18,
    )
    shared_flight, rest_flight, cot, att, att_half, lse_own = hold(
        (shared_flight, rest_flight, cot, att, att_half, lse_own)
    )
    rest_mine = rest_finish(rest_flight)
    rest_other = swap(rest_mine, "rows", 0)
    x_all = shared_finish(shared_flight).reshape(frames, width)
    q_loc, kv_all = project_shared(x_all, x_loc, qkv_full, small, (rest_mine,))
    cot[1], cot[3] = swap_places(cot[1], 1), swap_places(cot[3], 3)
    att_half, att, lse_loc = attend_forward(
        u_loc, q_loc, kv_all, kv_all, qa_loc, ka_all, g_loc, loc_cols, pairs, frames, False,
        (att_half, att), cycle, 8,
    )
    cot, rest_other, att, att_half, lse_loc = hold((cot, rest_other, att, att_half, lse_loc))
    h_cat, ga_cat, g1_cat, rest_keep, rest_send, sums = layer_rest(
        x_cat, att_half, cot, rest_mine, rest_other, small, core, place_of, chunks
    )

    def blocks_of(own):
        return own[:frames].reshape(cycle, block_len, width)

    rest_flight = scatter_begin(rest_keep, rest_send)
    hidden = [take(blocks_of(h_cat), place ^ s) for s in range(cycle)]
    hidden[1], hidden[2] = swap_places(hidden[1], 1), swap_places(hidden[2], 2)
    dq_loc, dkv_all, col_loc, grad_loc, diag_loc = attend_backward(
        u_loc, q_loc, kv_all, kv_all, ga_cat, att, qa_loc, ka_all, g_loc, lse_loc,
        g_loc, u_loc, loc_cols, pairs, cycle, 16, 0, pairs,
    )
    part_all, mine = shared_input(
        dq_loc, dkv_all, qkv_full, g1_cat, cycle, grad_loc, gate_loc, scale_rows, dirs_mix
    )
    rest_flight, hidden[:3], part_all = hold((rest_flight, hidden[:3], part_all))
    hidden[3] = swap_places(hidden[3], 3)
    rest_flight = scatter_first(rest_flight)
    part_flight = halve((part_all,), (2, 2), "blk", 0, 1)
    third = pairs // 3
    into = attend_backward(
        u_own, qkv_own, qkv_own, qkv_own, ga_cat, att, qa_own, ka_own, g_own, lse_own,
        g_own, u_own, own_cols, pairs, 0, 26, 0, pairs - third, (),
        (rest_flight[0][0], rest_flight[1][0], part_flight[0]),
    )
    rest_flight, part_flight, into, hidden[3] = hold((rest_flight, part_flight, into, hidden[3]))
    for step in range(1, high_steps):
        rest_flight = scatter_high(rest_flight, step)
    part_flight = halve(part_flight, (2,), "blk", 1, 0)
    dq_own, dkv_own, col_own, grad_own, diag = into
    into = attend_backward(
        u_own, qkv_own, qkv_own, qkv_own, ga_cat, att, qa_own, ka_own, g_own, lse_own,
        grad_own, diag, own_cols, pairs, 0, 13, pairs - third, third, (dq_own, dkv_own, col_own),
        (rest_flight[0][0], rest_flight[1][0]),
    )
    rest_flight, part_flight, into = hold((rest_flight, part_flight, into))
    dq_own, dkv_own, col_own, grad_own, diag = into
    rest_flight = scatter_blk((scatter_whole(rest_flight),), 0)
    flat = gate_sums(
        (grad_own, grad_loc), (gate_own, gate_loc), scale_rows, (diag, diag_loc), slots[None, :], x_cat, x_loc,
        (col_own, col_loc), sums, (place * block_len).reshape(1), bucket_count,
    )
    direct = high_steps == 2 and width % 64 == 0
    upper = [2 * s for s in (1, 2, 3)] if direct else []
    swap_rows = lambda array, mask: lax.ppermute(
        array, "rows", [(i, i ^ mask) for i in range(lax.axis_size("rows"))]
    )
    add_up = lambda arrays: sum(arrays[1:], arrays[0])
    flat_flight = [flat] + [swap_rows(flat, mask) for mask in upper]
    dx_own = own_input(
        dq_own, dkv_own, qkv_full, g1_cat, grad_own, gate_own, scale_rows, dirs_mix, (rest_flight[0], flat)
    )
    flat_flight, dx_own = hold((flat_flight, dx_own))
    flat = add_up(flat_flight)
    flat_flight = (flat, swap(flat, "rows", 0))
    inputs = [take(blocks_of(dx_own), place ^ s) for s in range(cycle)]
    inputs[1], inputs[2] = swap_places(inputs[1], 1), swap_places(inputs[2], 2)
    qkv_keep, qkv_send = weight_grad(
        x_cat, x_all, x_loc, dq_own, dkv_own, dq_loc, dkv_all, core, (dx_own,)
    )
    rest_flight, flat_flight, qkv_keep, qkv_send, inputs = hold(
        (rest_flight, flat_flight, qkv_keep, qkv_send, inputs)
    )
    back_flight = scatter_begin(qkv_keep, qkv_send)
    flat = add_up(flat_flight)
    rest_flight = scatter_blk(rest_flight, 1)
    back_flight = hold(back_flight)
    if direct:
        back_flight = scatter_four(back_flight)
    else:
        back_flight = scatter_first(back_flight)
        for step in range(1, high_steps):
            back_flight = scatter_high(back_flight, step)
    inputs[3], hidden = hold((inputs[3], hidden, back_flight[0]))[:2]
    inputs[3] = swap_places(inputs[3], 3)
    hidden_out = settle(hidden, (h_cat,), cycle, place_of)
    rest_flight = scatter_end(rest_flight)
    back_flight, rest_flight, inputs, flat, hidden_out = hold(
        (back_flight, rest_flight, inputs, flat, hidden_out)
    )
    if direct:
        back_flight = scatter_places(back_flight)
    else:
        back_flight = scatter_blk(scatter_blk((scatter_whole(back_flight),), 0), 1)
        for bit in range(1, bit_count("rows")):
            flat = flat + swap(flat, "rows", bit)
    flat, rest_flight, inputs = hold((flat, rest_flight, inputs, back_flight[0]))[:3]
    flat_flight = (flat, swap_places(flat, 1))
    rest_first, rest_second = scatter_done(rest_flight)
    grad_up = rest_first[:, :inner_width].reshape(local_rows, chunks, width).transpose(0, 2, 1)
    grad_up = grad_up.reshape(local_rows, inner_width)
    grad_down = rest_second[:, :inner_width].reshape(local_rows * chunks, width)
    grad_out = jnp.concatenate([rest_first[:, inner_width:], rest_second[:, inner_width:]], axis=1)
    grad_input = settle(inputs, (mine,) + tuple(part_flight), 0, place_of)
    back_flight, flat_flight, grad_input, grad_up, grad_down, grad_out = hold(
        (back_flight, flat_flight, grad_input, grad_up, grad_down, grad_out)
    )
    back_flight = scatter_end(back_flight)
    flat = add_up(flat_flight)
    flat_flight = (flat, swap_places(flat, 2))
    last_first, last_second = scatter_done(back_flight)
    first_row = (lax.axis_index("rows") * cycle + place) * local_rows
    bias_sum, gain_sum, up_bias_sum, table_sum, gate_weight_sum, gate_scale_sum = finish(
        *flat_flight, first_row.reshape(1), local_rows, chunks, rel_table.shape, gate_weight.shape
    )
    return (
        hidden_out,
        grad_input,
        jnp.concatenate([last_first, last_second], axis=1),
        grad_out,
        grad_up,
        grad_down,
        bias_sum.T,
        gain_sum.T,
        up_bias_sum.T.reshape(-1),
        table_sum.T,
        gate_weight_sum.T,
        gate_scale_sum.reshape(-1),
    )


def solution(mesh):
    placed = (
        P("rows", "blk", None),
        P("rows", "blk"),
        P(),
        P(("rows", "blk"), None),
        P(("rows", "blk"), None),
        P(("rows", "blk"), None),
        P(("rows", "blk"), None),
        P(("rows", "blk"), None),
        P(("rows", "blk"), None),
        P(("rows", "blk")),
        P(),
        P(),
        P(),
        P("rows", "blk", None),
    )
    return jax.shard_map(
        shards,
        mesh=mesh,
        in_specs=placed,
        out_specs=(
            P("rows", "blk", None),
            P("rows", "blk", None),
            P(("rows", "blk"), None),
            P(("rows", "blk"), None),
            P(("rows", "blk"), None),
            P(("rows", "blk"), None),
            P(("rows", "blk"), None),
            P(("rows", "blk"), None),
            P(("rows", "blk")),
            P(),
            P(),
            P(),
        ),
        check_vma=False,
    )
```

```python
import functools

import jax
import jax.numpy as jnp
from jax import lax
from jax.experimental import pallas as pl
from jax.experimental.pallas import tpu as pltpu
from jax.sharding import PartitionSpec as P

EPS_NORM = 1e-05
LANES = 128
SMALL = 128
BUCKET_ROWS = 384
BF16 = jnp.bfloat16
F32 = jnp.float32
NN = (((1,), (0,)), ((), ()))
NT = (((1,), (1,)), ((), ()))
TN = (((0,), (0,)), ((), ()))
HIGHEST = lax.Precision.HIGHEST


def thirds(v):
    high = v.astype(BF16)
    rest = v - high.astype(F32)
    middle = rest.astype(BF16)
    return high, middle, (rest - middle.astype(F32)).astype(BF16)


def dotf(a, b, dims):
    return lax.dot_general(a, b, dims, preferred_element_type=F32)


def tiles_of(total, tile):
    return [(s, min(tile, total - s)) for s in range(0, total, tile)]


ANY_SPEC = pl.BlockSpec(memory_space=pl.ANY)


def ignoring(kernel, inputs, count):
    return lambda *refs: kernel(*refs[:inputs], *refs[inputs + count :])


def cost(us):
    return pl.CostEstimate(flops=1000, bytes_accessed=1000, transcendentals=0)


SMEM_SPEC = pl.BlockSpec(memory_space=pltpu.SMEM)


def table_rows_of(u, width):
    return pltpu.roll(jnp.broadcast_to(u, (LANES, width)), 0, 1, stride=1, stride_axis=0)


def forward_kernel(
    tile, flip, u_ref, q_ref, k_ref, v_ref, qa_ref, ka_ref, g_ref,
    ob_ref, o_ref, lse_ref, t_scr,
):
    nq, nk, width = q_ref.shape[0], k_ref.shape[0], u_ref.shape[-1]
    pair = pl.program_id(0)
    half = LANES // 2
    shift = -(-nk // LANES)
    low = lax.broadcasted_iota(jnp.int32, (1, LANES), 1) < half
    low_rows = lax.broadcasted_iota(jnp.int32, (LANES, 1), 0) < half
    k, v, q = k_ref[...], v_ref[...], q_ref[...]
    zero = jnp.zeros((), BF16)
    khs, qhs, vzs, gs = [], [], [], []
    for hh in range(2):
        head = pl.ds(2 * pair + hh, 1)
        t_scr[hh] = table_rows_of(u_ref[head, :], width)
        gs.append(g_ref[head, :])
        sel = low if hh == 0 else jnp.logical_not(low)
        khs.append(jnp.where(sel, k, ka_ref[...]))
        qhs.append(jnp.where(sel, q, qa_ref[...]))
        vzs.append(jnp.where(sel, v, zero))
    vt = v.T if flip else None
    for first, cols in tiles_of(nq, tile):
        total, scales, parts = None, [], []
        for hh in range(2):
            raw = dotf(khs[hh], qhs[hh][first : first + cols], NT)
            g = gs[hh][:, first : first + cols]
            scores, peak = [], None
            for f2, r2 in tiles_of(nk, LANES):
                col = (shift - f2 // LANES) * LANES + first
                s = raw[f2 : f2 + r2] + g * t_scr[hh, 0:r2, col : col + cols]
                top = jnp.max(s, axis=0, keepdims=True)
                peak = top if peak is None else jnp.maximum(peak, top)
                scores.append(s)
            probs, mass = [], None
            for s in scores:
                p = jnp.exp(s - peak)
                part = jnp.sum(p, axis=0, keepdims=True)
                mass = part if mass is None else mass + part
                probs.append(p.astype(BF16))
            lse_ref[pl.ds(2 * pair + hh, 1), first : first + cols] = peak + jnp.log(mass)
            pb = jnp.concatenate(probs, axis=0)
            if flip:
                parts.append(dotf(vt[hh * half : (hh + 1) * half], pb, NN) / mass)
            else:
                x = dotf(pb, vzs[hh], TN)
                total = x if total is None else total + x
                scales.append(1.0 / mass)
        if flip:
            o = jnp.concatenate(parts, axis=0).T
        else:
            o = total * jnp.where(low_rows, scales[0], scales[1]).T
        o_ref[first : first + cols, :] = o
        ob_ref[first : first + cols, :] = o.astype(BF16)


def attend_forward(
    u, q, k, v, qa, ka, g, cols, pairs, tile, flip, into, row_block, us, deps=()
):
    nq, nk = qa.shape[0], ka.shape[0]
    heads, width = u.shape
    col = lambda c: (lambda p: (0, c + p))
    fix = lambda p: (0, 0)
    out_spec = pl.BlockSpec((nq, LANES), lambda p: (row_block, p))
    return pl.pallas_call(
        ignoring(functools.partial(forward_kernel, tile, flip), 7, len(into) + len(deps)),
        grid=(pairs,),
        in_specs=[
            pl.BlockSpec(u.shape, fix),
            pl.BlockSpec((nq, LANES), col(cols[0])),
            pl.BlockSpec((nk, LANES), col(cols[1])),
            pl.BlockSpec((nk, LANES), col(cols[2])),
            pl.BlockSpec((nq, LANES), fix),
            pl.BlockSpec((nk, LANES), fix),
            pl.BlockSpec(g.shape, fix),
        ]
        + [ANY_SPEC] * (len(into) + len(deps)),
        out_specs=[out_spec, out_spec, pl.BlockSpec((heads, nq), fix)],
        out_shape=[
            jax.ShapeDtypeStruct(into[0].shape, BF16),
            jax.ShapeDtypeStruct(into[0].shape, F32),
            jax.ShapeDtypeStruct((heads, nq), F32),
        ],
        input_output_aliases={7 + i: i for i in range(len(into))},
        scratch_shapes=[pltpu.VMEM((2, LANES, width), F32)],
        compiler_params=pltpu.CompilerParams(vmem_limit_bytes=40 * 2**20),
        cost_estimate=cost(us),
        name="attention_forward",
    )(u, q, k, v, qa, ka, g, *into, *deps)


def backward_kernel(
    start, begin, u_ref, q_ref, k_ref, v_ref, do_ref, att_ref, qa_ref, ka_ref, g_ref, lse_ref,
    gate_in, diag_in, dq_ref, dkv_ref, col_ref, gate_ref, diag_ref, t_scr, c_scr,
):
    nq, nk, width = q_ref.shape[0], k_ref.shape[0], u_ref.shape[-1]
    step = pl.program_id(0)
    shift = -(-nk // LANES)

    @pl.when(step == 0)
    def _():
        gate_ref[...] = jnp.zeros_like(gate_ref) if begin else gate_in[...]
        diag_ref[...] = jnp.zeros_like(diag_ref) if begin else diag_in[...]

    low = lax.broadcasted_iota(jnp.int32, (1, LANES), 1) < LANES // 2
    k, v, q, do = k_ref[...], v_ref[...], q_ref[...], do_ref[...]
    prod = (do.astype(F32) * att_ref[...]).T
    zero = jnp.zeros((), BF16)
    dq, dk, dv = None, None, None
    for hh in range(2):
        head = pl.ds(2 * (start + step) + hh, 1)
        t_scr[hh] = table_rows_of(u_ref[head, :], width)
        c_scr[hh] = jnp.zeros_like(c_scr[hh])
        sel = low if hh == 0 else jnp.logical_not(low)
        delta = jnp.sum(prod[hh * (LANES // 2) : (hh + 1) * (LANES // 2)], axis=0, keepdims=True)
        ka = jnp.where(sel, k, ka_ref[...])
        qa = jnp.where(sel, q, qa_ref[...])
        kz, qz, doz = jnp.where(sel, k, zero), jnp.where(sel, q, zero), jnp.where(sel, do, zero)
        lse = lse_ref[head, :]
        g = g_ref[head, :]
        gate = jnp.zeros((1, nq), F32)
        raw = dotf(ka, qa, NT)
        dp = dotf(v, doz, NT)
        ps, ds = [], []
        for first, rows in tiles_of(nk, LANES):
            col = (shift - first // LANES) * LANES
            t = t_scr[hh, 0:rows, col : col + nq]
            p = jnp.exp(raw[first : first + rows] + (g * t - lse))
            d = p * (dp[first : first + rows] - delta)
            gate += jnp.sum(d * t, axis=0, keepdims=True)
            c_scr[hh, 0:rows, col : col + nq] += d * g
            ps.append(p.astype(BF16))
            ds.append(d.astype(BF16))
        pb, db = jnp.concatenate(ps, axis=0), jnp.concatenate(ds, axis=0)
        dk_add, dv_add, dq_add = dotf(db, qz, NN), dotf(pb, doz, NN), dotf(db, kz, TN)
        dk = dk_add if dk is None else dk + dk_add
        dv = dv_add if dv is None else dv + dv_add
        dq = dq_add if dq is None else dq + dq_add
        gate_ref[head, :] = gate
        half = LANES // 2
        acc = c_scr[hh]
        while half >= 8:
            acc = acc[:half] + pltpu.roll(acc[half:], width - half, 1)
            half //= 2
        row = lax.broadcasted_iota(jnp.int32, (8, 1), 0)
        for bit in (1, 2, 4):
            acc = jnp.where((row & bit) != 0, pltpu.roll(acc, width - bit, 1), acc)
        diag_ref[head, :] += jnp.sum(acc, axis=0, keepdims=True)
    dq_ref[...] = (dq.astype(BF16) * (LANES // 2) ** -0.5).astype(BF16)
    dkv_ref[0] = dk.astype(BF16)
    dkv_ref[1] = dv.astype(BF16)
    col_ref[0:1, :] = jnp.sum(dq, axis=0, keepdims=True) * (LANES // 2) ** -0.5
    col_ref[1:2, :] = jnp.sum(dv, axis=0, keepdims=True)


def attend_backward(
    u, q, k, v, do, att, qa, ka, g, lse, gate, diag, cols, pairs, row_block, us,
    start, count, into=(), deps=(),
):
    nq, nk = qa.shape[0], ka.shape[0]
    heads, width = u.shape
    col = lambda c: (lambda p: (0, c + start + p))
    row = lambda p: (row_block, start + p)
    fix = lambda p: (0, 0)
    return pl.pallas_call(
        ignoring(functools.partial(backward_kernel, start, start == 0), 12, len(into) + len(deps)),
        grid=(count,),
        in_specs=[
            pl.BlockSpec(u.shape, fix),
            pl.BlockSpec((nq, LANES), col(cols[0])),
            pl.BlockSpec((nk, LANES), col(cols[1])),
            pl.BlockSpec((nk, LANES), col(cols[2])),
            pl.BlockSpec((nq, LANES), row),
            pl.BlockSpec((nq, LANES), row),
            pl.BlockSpec((nq, LANES), fix),
            pl.BlockSpec((nk, LANES), fix),
            pl.BlockSpec(g.shape, fix),
            pl.BlockSpec(lse.shape, fix),
            pl.BlockSpec(gate.shape, fix),
            pl.BlockSpec(diag.shape, fix),
        ]
        + [ANY_SPEC] * (len(into) + len(deps)),
        out_specs=[
            pl.BlockSpec((nq, LANES), col(0)),
            pl.BlockSpec((2, nk, LANES), lambda p: (0, 0, start + p)),
            pl.BlockSpec((2, LANES), col(0)),
            pl.BlockSpec(gate.shape, fix),
            pl.BlockSpec(diag.shape, fix),
        ],
        out_shape=[
            jax.ShapeDtypeStruct((nq, pairs * LANES), BF16),
            jax.ShapeDtypeStruct((2, nk, pairs * LANES), BF16),
            jax.ShapeDtypeStruct((2, pairs * LANES), F32),
            jax.ShapeDtypeStruct(gate.shape, F32),
            jax.ShapeDtypeStruct(diag.shape, F32),
        ],
        input_output_aliases={12 + i: i for i in range(len(into))},
        scratch_shapes=[pltpu.VMEM((2, LANES, width), F32), pltpu.VMEM((2, LANES, width), F32)],
        compiler_params=pltpu.CompilerParams(vmem_limit_bytes=60 * 2**20),
        cost_estimate=cost(us),
        name="attention_backward",
    )(u, q, k, v, do, att, qa, ka, g, lse, gate, diag, *into, *deps)


def own_kernel(
    p0_ref, p1_ref, p2_ref, p3_ref, loc_ref, mine_ref, other_ref, dirs_ref, scale_ref, core_ref, place_ref,
    out_ref, w_ref, small_ref, x_ref, qa_ref, ka_ref, ql_ref, kl_ref, ga_ref, gl_ref, g0_ref, g1_ref,
    x_scr, seg_scr, all_scr,
):
    step = pl.program_id(0)
    width = loc_ref.shape[1]
    block = loc_ref.shape[0]
    own = out_ref.shape[0]
    cut = 3 * width // 2
    rows = scale_ref.shape[0]

    lane = lax.broadcasted_iota(jnp.int32, (1, LANES), 1)
    lane = jnp.where(lane >= LANES // 2, lane - LANES // 2, lane).astype(F32)
    penalty = lambda seg: jnp.where((lane < 4.0) & (lane != seg), -1e30, 0.0).astype(BF16)

    def unpack(first, second):
        w_ref[:, 0:cut] = first[:, 0:cut]
        w_ref[:, cut : 2 * cut] = second[:, 0:cut]
        small_ref[...] = first[:, cut : cut + SMALL].astype(F32).T[0 : small_ref.shape[0]]

    def gates(x, ref, value_ref):
        logits = dotf(dirs_ref[...], x, NT)
        count = 2 * rows
        logits = logits[:count] + (logits[count : 2 * count] + logits[2 * count :])
        sig = 1.0 / (1.0 + jnp.exp(-logits))
        a, b = sig[:rows], sig[rows:]
        ref[0] = a
        ref[1] = b
        value_ref[...] = a * (b * scale_ref[...] - 1.0) + 2.0

    @pl.when((step == 0) & (core_ref[0] == 0))
    def _():
        unpack(mine_ref, other_ref)

    @pl.when((step == 0) & (core_ref[0] != 0))
    def _():
        unpack(other_ref, mine_ref)

    @pl.when(step == 0)
    def _():
        for s, ref in enumerate((p0_ref, p1_ref, p2_ref, p3_ref)):
            here = pl.ds(pl.multiple_of((place_ref[0] ^ s) * block, 8), block)
            x_scr[here, :] = ref[0:block, :].astype(F32)
            for row, scr in ((block, seg_scr), (block + 1, all_scr)):
                seg = ref[row : row + 1, 0 : 2 * LANES].astype(F32)
                seg = jnp.broadcast_to(seg, (LANES, 2 * LANES)).T[0:block]
                scr[here, :] = seg
                if s == 0 and row > block:
                    ql_ref[...] = penalty(seg)
        x_scr[own : own + block, :] = loc_ref[...].astype(F32)
        x_scr[own + block :, :] = jnp.zeros((x_scr.shape[0] - own - block, width), F32)
        x_ref[...] = x_scr[...].astype(BF16)
        qa_ref[...] = penalty(seg_scr[...])
        ka_ref[...] = jnp.where(lane == seg_scr[...], 1.0, 0.0).astype(BF16)
        kl_ref[...] = jnp.where(lane == all_scr[...], 1.0, 0.0).astype(BF16)
        gates(x_ref[0:own, :], ga_ref, g0_ref)
        gates(loc_ref[...], gl_ref, g1_ref)

    bias = jnp.where(step == 0, small_ref[0:1, :], jnp.where(step == 2, small_ref[1:2, :], 0.0))
    scale = jnp.where(step == 0, (LANES // 2) ** -0.5, 1.0)
    w = w_ref[:, pl.ds(pl.multiple_of(step * width, LANES), width)]
    out_ref[...] = ((dotf(x_ref[0:own, :], w, NN) + bias) * scale).astype(BF16)


def project_own(packs, loc, mine, other, dirs, scale, core, place, total):
    block, width = loc.shape
    own = len(packs) * block
    rows = scale.shape[0]
    fix = lambda c: (0, 0)
    full = lambda shape: pl.BlockSpec(shape, lambda c: (0,) * len(shape))
    shapes = [
        ((own, 3 * width), BF16),
        ((width, 3 * width), BF16),
        ((16, width), F32),
        ((total, width), BF16),
        ((own, LANES), BF16),
        ((own, LANES), BF16),
        ((block, LANES), BF16),
        ((own, LANES), BF16),
        ((2, rows, own), F32),
        ((2, rows, block), F32),
        ((rows, own), F32),
        ((rows, block), F32),
    ]
    return pl.pallas_call(
        own_kernel,
        grid=(3,),
        in_specs=[full(p.shape) for p in packs]
        + [full(v.shape) for v in (loc, mine, other, dirs, scale)]
        + [SMEM_SPEC, SMEM_SPEC],
        out_specs=[pl.BlockSpec((own, width), lambda c: (0, c))] + [full(s) for s, _ in shapes[1:]],
        out_shape=[jax.ShapeDtypeStruct(s, t) for s, t in shapes],
        scratch_shapes=[pltpu.VMEM((total, width), F32)] + [pltpu.VMEM((own, LANES), F32)] * 2,
        compiler_params=pltpu.CompilerParams(vmem_limit_bytes=40 * 2**20),
        cost_estimate=cost(10),
        name="projection_own",
    )(*packs, loc, mine, other, dirs, scale, core, place)


def project_shared_kernel(all_ref, loc_ref, w_ref, b_ref, q_out, kv_out):
    step = pl.program_id(0)

    @pl.when(step == 0)
    def _():
        q = dotf(loc_ref[...], w_ref[...], NN) + b_ref[0:1, :]
        q_out[...] = (q * (LANES // 2) ** -0.5).astype(BF16)

    @pl.when(step > 0)
    def _():
        bias = jnp.where(step == 2, b_ref[1:2, :], 0.0)
        kv_out[...] = (dotf(all_ref[...], w_ref[...], NN) + bias).astype(BF16)


def project_shared(x_all, x_loc, weight, small, deps=()):
    n_all, width = x_all.shape
    n_loc = x_loc.shape[0]
    fix = lambda c: (0, 0)
    return pl.pallas_call(
        ignoring(project_shared_kernel, 4, len(deps)),
        grid=(3,),
        in_specs=[
            pl.BlockSpec((n_all, width), fix),
            pl.BlockSpec((n_loc, width), fix),
            pl.BlockSpec((width, width), lambda c: (0, c)),
            pl.BlockSpec(small.shape, fix),
        ]
        + [ANY_SPEC] * len(deps),
        out_specs=[
            pl.BlockSpec((n_loc, width), fix),
            pl.BlockSpec((n_all, width), lambda c: (0, jnp.maximum(c - 1, 0))),
        ],
        out_shape=[
            jax.ShapeDtypeStruct((n_loc, width), BF16),
            jax.ShapeDtypeStruct((n_all, 2 * width), BF16),
        ],
        compiler_params=pltpu.CompilerParams(vmem_limit_bytes=16 * 2**20),
        cost_estimate=cost(5),
        name="projection_shared",
    )(x_all, x_loc, weight, small, *deps)


def gelu_parts(x):
    size = jnp.abs(x)
    t = 1.0 / (1.0 + (0.3275911 * 0.7071067811865476) * size)
    poly = t * (
        0.254829592
        + t * (-0.284496736 + t * (1.421413741 + t * (-1.453152027 + t * 1.061405429)))
    )
    bell = jnp.exp(-0.5 * x * x)
    tail = 0.5 * poly * bell
    phi = jnp.where(x >= 0, 1.0 - tail, tail)
    return x * phi, phi + x * bell * 0.3989422804014327


def mean_last(v):
    return jnp.sum(v, axis=-1, keepdims=True) * (1.0 / v.shape[-1])


def layer_kernel(
    chunks, tile,
    x_ref, a_ref, c0_ref, c1_ref, c2_ref, c3_ref, cl_ref, wom_ref, woo_ref, mine_ref, other_ref, vec_ref,
    core_ref, place_ref,
    h_ref, ga_ref, g1_ref, keep_ref, send_ref, sums_ref,
    c_scr, z_scr, r_scr, nh_scr, acc_scr, di_scr, act_scr, der_scr, ih_scr, wo_ref, up_ref, down_ref,
):
    step = pl.program_id(0)
    total, width = x_ref.shape
    half = width // 2
    low_core = core_ref[0] == 0
    high_core = core_ref[0] != 0

    vec = lambda i: vec_ref[i : i + 1, :]

    def over_tiles(body):
        @pl.loop(0, total // tile)
        def _(i):
            body(pl.ds(pl.multiple_of(i * tile, tile), tile))

    def add_sum(row, value):
        sums_ref[row : row + 1, :] += jnp.sum(value, axis=0, keepdims=True)

    def load(ref, is_mine):
        @pl.when(is_mine)
        def _():
            ref[...] = mine_ref[...]

        @pl.when(jnp.logical_not(is_mine))
        def _():
            ref[...] = other_ref[...]

    def emit(is_mine, value, cols=slice(None)):
        @pl.when(is_mine)
        def _():
            keep_ref[:, cols] = value

        @pl.when(jnp.logical_not(is_mine))
        def _():
            send_ref[:, cols] = value

    back = jnp.maximum(step - chunks, 0)
    j = back // 2
    forth = step < chunks
    even = (step >= chunks) & (step < 3 * chunks) & (back % 2 == 0)
    odd = (step >= chunks) & (step < 3 * chunks) & (back % 2 == 1)

    @pl.when(step == 0)
    def _():
        sums_ref[...] = jnp.zeros_like(sums_ref)

        @pl.when(low_core)
        def _():
            wo_ref[:, 0:half] = wom_ref[...]
            wo_ref[:, half:width] = woo_ref[...]

        @pl.when(high_core)
        def _():
            wo_ref[:, 0:half] = woo_ref[...]
            wo_ref[:, half:width] = wom_ref[...]

        def body(here):
            y = dotf(a_ref[here, :], wo_ref[...], NN) + vec(2) + x_ref[here, :].astype(F32)
            y = y - mean_last(y)
            r = lax.rsqrt(mean_last(y * y) + EPS_NORM)
            z = y * r
            z_scr[here, :] = z
            r_scr[here, :] = r
            nh_scr[here, :] = (z * vec(6) + vec(4)).astype(BF16)
            acc_scr[here, :] = jnp.zeros_like(z)

        for first, rows in tiles_of(total, tile):
            body(slice(first, first + rows))

    @pl.when(forth | odd)
    def _():
        load(up_ref, low_core)

    @pl.when(forth | even)
    def _():
        load(down_ref, high_core)

    @pl.when(forth)
    def _():
        bias = vec_ref[pl.ds(8 + step, 1), :]
        parts = [slice(first, first + rows) for first, rows in tiles_of(total, 256)]
        ahead = dotf(nh_scr[parts[0], :], up_ref[...], NN) + bias
        for i, here in enumerate(parts):
            inner = ahead
            if i + 1 < len(parts):
                ahead = dotf(nh_scr[parts[i + 1], :], up_ref[...], NN) + bias
            act, der = gelu_parts(inner)
            act = act.astype(BF16)
            act_scr[step, here, :] = act
            der_scr[step, here, :] = der.astype(BF16)
            acc_scr[here, :] += dotf(act, down_ref[...], NN)

    @pl.when(step == chunks)
    def _():
        block = cl_ref.shape[0]
        for s, ref in enumerate((c0_ref, c1_ref, c2_ref, c3_ref)):
            there = pl.ds(pl.multiple_of((place_ref[0] ^ s) * block, 8), block)
            c_scr[there, :] = ref[...].astype(F32)
        c_scr[4 * block : 5 * block, :] = cl_ref[...].astype(F32)
        c_scr[5 * block :, :] = jnp.zeros((total - 5 * block, width), F32)

        def body(here):
            v = z_scr[here, :] * vec(6) + vec(4) + acc_scr[here, :] + vec(3)
            v = v - mean_last(v)
            r = lax.rsqrt(mean_last(v * v) + EPS_NORM)
            z = v * r
            h_ref[here, :] = (z * vec(7) + vec(5)).astype(BF16)
            c = c_scr[here, :]
            q = c * vec(7)
            gt = r * (q - mean_last(q) - z * mean_last(q * z))
            acc_scr[here, :] = gt
            di_scr[here, :] = gt.astype(BF16)
            add_sum(3, gt)
            add_sum(5, c)
            add_sum(7, c * z)

        over_tiles(body)

    @pl.when(even)
    def _():
        emit(high_core, dotf(act_scr[j], di_scr[...], TN).astype(BF16))

        def body(here):
            gi = dotf(di_scr[here, :], down_ref[...], NT) * der_scr[j, here, :].astype(F32)
            sums_ref[pl.ds(8 + j, 1), :] += jnp.sum(gi, axis=0, keepdims=True)
            ih_scr[here, :] = gi.astype(BF16)

        over_tiles(body)

    @pl.when(odd)
    def _():
        emit(low_core, dotf(nh_scr[...], ih_scr[...], TN).astype(BF16))

        def body(here):
            acc_scr[here, :] += dotf(ih_scr[here, :], up_ref[...], NT)

        over_tiles(body)

    @pl.when(step == 3 * chunks)
    def _():
        def body(here):
            gn = acc_scr[here, :]
            z = z_scr[here, :]
            q = gn * vec(6)
            g1 = r_scr[here, :] * (q - mean_last(q) - z * mean_last(q * z))
            g1_ref[here, :] = g1
            ah = g1.astype(BF16)
            di_scr[here, :] = ah
            ga_ref[here, :] = dotf(ah, wo_ref[...], NT).astype(BF16)
            add_sum(2, g1)
            add_sum(4, gn)
            add_sum(6, gn * z)

        for first, rows in tiles_of(total, tile):
            body(slice(first, first + rows))
        out = dotf(a_ref[...], di_scr[...], TN).astype(BF16)
        emit(low_core, out[:, 0:half], slice(0, half))
        emit(high_core, out[:, half:width], slice(0, half))


def layer_rest(x, att, cot, mine, other, vec, core, place, chunks):
    total, width = x.shape
    fix = lambda s: (0, 0)
    once = pl.Buffered(buffer_count=1)

    def chunk_of(s):
        return jnp.where(s < chunks, s, jnp.clip((s - chunks) // 2, 0, chunks - 1))

    def const(shape):
        return pl.BlockSpec(shape, fix, pipeline_mode=once)

    rows = const((total, width))
    square = (width, width)
    out_half = pl.BlockSpec((width, width // 2), lambda s: (0, 2 * chunks), pipeline_mode=once)
    weight_spec = pl.BlockSpec(square, lambda s: (0, chunk_of(s)))
    grad_spec = pl.BlockSpec(square, lambda s: (0, jnp.maximum(s - chunks, 0) // 2))
    return pl.pallas_call(
        functools.partial(layer_kernel, chunks, 512),
        grid=(3 * chunks + 1,),
        in_specs=[
            rows, rows, *[const(v.shape) for v in cot],
            out_half, out_half, weight_spec, weight_spec, const(vec.shape), SMEM_SPEC, SMEM_SPEC,
        ],
        out_specs=[rows, rows, rows, grad_spec, grad_spec, const(vec.shape)],
        out_shape=[
            jax.ShapeDtypeStruct((total, width), BF16),
            jax.ShapeDtypeStruct((total, width), BF16),
            jax.ShapeDtypeStruct((total, width), F32),
            jax.ShapeDtypeStruct(mine.shape, BF16),
            jax.ShapeDtypeStruct(mine.shape, BF16),
            jax.ShapeDtypeStruct(vec.shape, F32),
        ],
        scratch_shapes=[
            pltpu.VMEM((total, width), F32),
            pltpu.VMEM((total, width), F32),
            pltpu.VMEM((total, 1), F32),
            pltpu.VMEM((total, width), BF16),
            pltpu.VMEM((total, width), F32),
            pltpu.VMEM((total, width), BF16),
            pltpu.VMEM((chunks, total, width), BF16),
            pltpu.VMEM((chunks, total, width), BF16),
            pltpu.VMEM((total, width), BF16),
            pltpu.VMEM(square, BF16),
            pltpu.VMEM(square, BF16),
            pltpu.VMEM(square, BF16),
        ],
        compiler_params=pltpu.CompilerParams(vmem_limit_bytes=60 * 2**20),
        cost_estimate=cost(70),
        name="layer_rest",
    )(x, att, *cot, mine, other, mine, other, vec, core, place)


def settle_kernel(b0_ref, b1_ref, b2_ref, b3_ref, *rest):
    place_ref, out_ref = rest[-2:]
    for s, ref in enumerate((b0_ref, b1_ref, b2_ref, b3_ref)):
        out_ref[place_ref[0] ^ s] = ref[...]
    total = rest[0][...]
    for ref in rest[1:-2]:
        total = total + ref[...].astype(F32)
    out_ref[4] = total.astype(out_ref.dtype)


def settle(blocks, last, last_block, place):
    block, width = blocks[1].shape
    one = pl.BlockSpec((block, width), lambda s: (0, 0))
    return pl.pallas_call(
        settle_kernel,
        grid=(1,),
        in_specs=[one] * 4
        + [pl.BlockSpec((block, width), lambda s: (last_block, 0))] * len(last)
        + [SMEM_SPEC],
        out_specs=pl.BlockSpec((5, block, width), lambda s: (0, 0, 0)),
        out_shape=jax.ShapeDtypeStruct((5, block, width), BF16),
        compiler_params=pltpu.CompilerParams(vmem_limit_bytes=16 * 2**20),
        cost_estimate=cost(2),
        name="settle",
    )(*blocks, *last, place)


def shared_input_kernel(
    dq_ref, dkv_ref, w_ref, base_ref, grad_ref, gate_ref, scale_ref, dirs_ref, part_ref, loc_ref, acc
):
    step = pl.program_id(0)

    @pl.when(step == 0)
    def _():
        mix = gate_mix(grad_ref[...], gate_ref, scale_ref[...])
        loc_ref[...] = base_ref[...] + dotf(mix, dirs_ref[...], TN) + dotf(dq_ref[...], w_ref[...], NT)

    @pl.when(step == 1)
    def _():
        acc[...] = dotf(dkv_ref[...], w_ref[...], NT)

    @pl.when(step == 2)
    def _():
        part_ref[...] = (acc[...] + dotf(dkv_ref[...], w_ref[...], NT)).astype(BF16)


def shared_input(dq, dkv, weight, base, base_block, grad, gate, scale, dirs):
    n_loc, width = dq.shape
    n_all = dkv.shape[1]
    fix = lambda c: (0, 0)
    return pl.pallas_call(
        shared_input_kernel,
        grid=(3,),
        in_specs=[
            pl.BlockSpec((n_loc, width), fix),
            pl.BlockSpec((None, n_all, width), lambda c: (jnp.maximum(c - 1, 0), 0, 0)),
            pl.BlockSpec((width, width), lambda c: (0, c)),
            pl.BlockSpec((n_loc, width), lambda c: (base_block, 0)),
            pl.BlockSpec(grad.shape, fix),
            pl.BlockSpec(gate.shape, lambda c: (0, 0, 0)),
            pl.BlockSpec(scale.shape, fix),
            pl.BlockSpec(dirs.shape, fix),
        ],
        out_specs=[pl.BlockSpec((n_all, width), fix), pl.BlockSpec((n_loc, width), fix)],
        out_shape=[
            jax.ShapeDtypeStruct((n_all, width), BF16),
            jax.ShapeDtypeStruct((n_loc, width), F32),
        ],
        scratch_shapes=[pltpu.VMEM((n_all, width), F32)],
        compiler_params=pltpu.CompilerParams(vmem_limit_bytes=60 * 2**20),
        cost_estimate=cost(5),
        name="shared_input",
    )(dq, dkv, weight, base, grad, gate, scale, dirs)


def weight_grad_kernel(
    x0_ref, x4_ref, loc_ref, dq_ref, dkv_ref, dq4_ref, dkv4_ref, core_ref, keep_ref, send_ref
):
    step = pl.program_id(0)
    width = x0_ref.shape[1]
    half = width // 2
    cut = 3 * half
    low_core = core_ref[0] == 0
    high_core = core_ref[0] != 0

    def emit(is_mine, cols, value):
        @pl.when(is_mine)
        def _():
            keep_ref[:, cols] = value

        @pl.when(jnp.logical_not(is_mine))
        def _():
            send_ref[:, cols] = value

    @pl.when(step == 0)
    def _():
        grad = dotf(x0_ref[...], dq_ref[...], TN) + dotf(loc_ref[...], dq4_ref[...], TN)
        emit(low_core, slice(0, width), grad.astype(BF16))

    @pl.when(step > 0)
    def _():
        grad = dotf(x0_ref[...], dkv_ref[...], TN) + dotf(x4_ref[...], dkv4_ref[...], TN)
        grad = grad.astype(BF16)

        @pl.when(step == 1)
        def _():
            emit(low_core, slice(width, cut), grad[:, 0:half])
            emit(high_core, slice(0, half), grad[:, half:width])

        @pl.when(step == 2)
        def _():
            emit(high_core, slice(half, cut), grad)


def weight_grad(x_cat, x_all, x_loc, dq, dkv, dq4, dkv4, core, deps=()):
    own, width = dq.shape
    n_all, n_loc = x_all.shape[0], x_loc.shape[0]
    fix = lambda c: (0, 0)
    half = lambda c: (jnp.maximum(c - 1, 0), 0, 0)
    shape = (width, 3 * width // 2)
    return pl.pallas_call(
        ignoring(weight_grad_kernel, 8, len(deps)),
        grid=(3,),
        in_specs=[
            pl.BlockSpec((own, width), fix),
            pl.BlockSpec((n_all, width), fix),
            pl.BlockSpec((n_loc, width), fix),
            pl.BlockSpec((own, width), fix),
            pl.BlockSpec((None, own, width), half),
            pl.BlockSpec((n_loc, width), fix),
            pl.BlockSpec((None, n_all, width), half),
            SMEM_SPEC,
        ]
        + [ANY_SPEC] * len(deps),
        out_specs=[pl.BlockSpec(shape, fix)] * 2,
        out_shape=[jax.ShapeDtypeStruct(shape, BF16)] * 2,
        compiler_params=pltpu.CompilerParams(vmem_limit_bytes=24 * 2**20),
        cost_estimate=cost(10),
        name="projection_weight_grad",
    )(x_cat, x_all, x_loc, dq, dkv, dq4, dkv4, core, *deps)


def gate_parts(grad, gate_ref, c):
    a, b = gate_ref[0], gate_ref[1]
    return thirds(grad * (b * c - 1.0) * a * (1.0 - a)), thirds(grad * a * c * b * (1.0 - b))


def gate_mix(grad, gate_ref, c):
    da, db = gate_parts(grad, gate_ref, c)
    return jnp.concatenate([da[0], db[0], da[1], db[1], da[0], db[0]], axis=0)


def gate_kernel(
    buckets_used, grad0_ref, grad1_ref, gate0_ref, gate1_ref, scale_ref, diag0_ref, diag1_ref, slots_ref, x_ref, loc_ref,
    col0_ref, col1_ref, sums_ref, turn_ref, flat_ref,
):
    c = scale_ref[...]
    rows = c.shape[0]
    head_dim = LANES // 2
    turned = diag1_ref[...]
    turned = jnp.concatenate(
        [turned, jnp.zeros((rows, diag0_ref.shape[1] - turned.shape[1]), F32)], axis=1
    )
    diag = diag0_ref[...] + pltpu.roll(turned, turn_ref[0], 1)

    def back(grad_ref, gate_ref, x):
        grad = grad_ref[...]
        da, db = gate_parts(grad, gate_ref, c)
        d = jnp.concatenate([part for pair in zip(da, db) for part in pair], axis=0)
        return dotf(d, x, NN), jnp.sum(grad * gate_ref[0] * gate_ref[1], axis=1, keepdims=True)

    dw0, scale0 = back(grad0_ref, gate0_ref, x_ref[...])
    dw1, scale1 = back(grad1_ref, gate1_ref, loc_ref[...])
    dw = dw0 + dw1
    dw = dw[: 2 * rows] + (dw[2 * rows : 4 * rows] + dw[4 * rows :])
    lane = lax.broadcasted_iota(jnp.int32, dw.shape, 1)
    row = lax.broadcasted_iota(jnp.int32, dw.shape, 0)
    row = jnp.where(row >= rows, row - rows, row) * head_dim
    dw = jnp.where((lane >= row) & (lane < row + head_dim), dw, 0.0)
    buckets = lax.broadcasted_iota(jnp.int32, (BUCKET_ROWS, diag.shape[1]), 0)
    hot = jnp.where(buckets == slots_ref[...], 1.0, 0.0).astype(BF16)
    table = dotf(jnp.concatenate(thirds(diag), axis=0), hot, NT)
    table = table[:rows] + (table[rows : 2 * rows] + table[2 * rows :])
    half = rows // 2
    flat_ref[...] = jnp.zeros_like(flat_ref)
    flat_ref[0:rows, :] = sums_ref[...]
    flat_ref[0:2, :] = col0_ref[...] + col1_ref[...]
    flat_ref[12:13, :] = jnp.sum(dw[:rows], axis=0, keepdims=True)
    flat_ref[13:14, :] = jnp.sum(dw[rows:], axis=0, keepdims=True)
    scales = jnp.broadcast_to(scale0 + scale1, (rows, LANES))
    lane = lax.broadcasted_iota(jnp.int32, table.shape, 1)
    table = jnp.where(lane < buckets_used, table, jnp.concatenate([scales] * (BUCKET_ROWS // LANES), axis=1))
    flat_ref[rows : rows + half, 0:BUCKET_ROWS] = table[0:half]
    flat_ref[rows : rows + half, BUCKET_ROWS : 2 * BUCKET_ROWS] = table[half:]


def gate_sums(grads, gates, scale, diags, slots, x, loc, cols, sums, turn, buckets_used):
    rows, own = grads[0].shape
    width = x.shape[1]
    full = lambda v: pl.BlockSpec(v.shape, lambda s: (0,) * v.ndim)
    args = [*grads, *gates, scale, *diags, slots, x, loc, *cols, sums, turn]
    specs = [full(v) for v in args[:-1]] + [SMEM_SPEC]
    specs[8] = pl.BlockSpec((own, width), lambda s: (0, 0))
    out = jax.ShapeDtypeStruct((rows + rows // 2, width), F32)
    return pl.pallas_call(
        functools.partial(gate_kernel, buckets_used),
        grid=(1,),
        in_specs=specs,
        out_specs=full(out),
        out_shape=out,
        compiler_params=pltpu.CompilerParams(vmem_limit_bytes=20 * 2**20),
        cost_estimate=cost(4),
        name="gate_sums",
    )(*args)


def own_input_kernel(
    dq_ref, dkv_ref, w_ref, base_ref, grad_ref, gate_ref, scale_ref, dirs_ref, dx_ref, acc
):
    step = pl.program_id(0)

    @pl.when(step == 0)
    def _():
        mix = gate_mix(grad_ref[...], gate_ref, scale_ref[...])
        acc[...] = base_ref[...] + dotf(mix, dirs_ref[...], TN) + dotf(dq_ref[...], w_ref[...], NT)

    @pl.when(step == 1)
    def _():
        acc[...] += dotf(dkv_ref[...], w_ref[...], NT)

    @pl.when(step == 2)
    def _():
        dx_ref[...] = (acc[...] + dotf(dkv_ref[...], w_ref[...], NT)).astype(BF16)


def own_input(dq, dkv, weight, base, grad, gate, scale, dirs, deps=()):
    own, width = dq.shape
    fix = lambda c: (0, 0)
    return pl.pallas_call(
        ignoring(own_input_kernel, 8, len(deps)),
        grid=(3,),
        in_specs=[
            pl.BlockSpec((own, width), fix),
            pl.BlockSpec((None, own, width), lambda c: (jnp.maximum(c - 1, 0), 0, 0)),
            pl.BlockSpec((width, width), lambda c: (0, c)),
            pl.BlockSpec((own, width), fix),
            pl.BlockSpec(grad.shape, fix),
            pl.BlockSpec(gate.shape, lambda c: (0, 0, 0)),
            pl.BlockSpec(scale.shape, fix),
            pl.BlockSpec(dirs.shape, fix),
        ]
        + [ANY_SPEC] * len(deps),
        out_specs=pl.BlockSpec((own, width), fix),
        out_shape=jax.ShapeDtypeStruct((own, width), BF16),
        scratch_shapes=[pltpu.VMEM((own, width), F32)],
        compiler_params=pltpu.CompilerParams(vmem_limit_bytes=20 * 2**20),
        cost_estimate=cost(8),
        name="own_input",
    )(dq, dkv, weight, base, grad, gate, scale, dirs, *deps)


def split_sum_kernel(_bits, keep_ref, got_ref, *outs):
    step = pl.program_id(0)
    cut = outs[0].shape[1]
    total = keep_ref[...] + got_ref[...]
    first, second = total[:, :cut], total[:, cut:]

    def put(here, ref, value):
        @pl.when(here)
        def _():
            ref[...] = value

    put(step // 2 == 0, outs[0], first)
    put(step // 2 == 1, outs[1], first)
    put(step % 2 == 0, outs[2], second)
    put(step % 2 == 1, outs[3], second)


def split_sum(keep, got, bits, cut, parts):
    rows, cols = keep.shape
    block = rows // 4 // parts
    low = lambda s, bits: (s // 2) ^ bits[0]
    high = lambda s, bits: (s % 2) ^ bits[1]
    wide = pl.BlockSpec(
        (block, cols), lambda s, t, bits: ((2 * high(s, bits) + low(s, bits)) * parts + t, 0)
    )
    at = lambda index, s, t, first, last: (
        index * parts + jnp.where(s < first, 0, jnp.where(s > last, parts - 1, t)), 0
    )
    stay = lambda s, t, bits: at(jnp.where(s < 2, s, 1) ^ bits[1], s, t, 0, 1)
    go = lambda s, t, bits: at(jnp.where(s < 2, 0, s - 2) ^ bits[1], s, t, 2, 3)
    stay_other = lambda s, t, bits: (
        jnp.where(s % 2 == 0, low(s, bits) * parts + t, low(s, bits) * parts + parts - 1), 0
    )
    go_other = lambda s, t, bits: (
        jnp.where(s % 2 == 1, low(s, bits) * parts + t, low(s, bits) * parts), 0
    )
    return pl.pallas_call(
        split_sum_kernel,
        grid_spec=pltpu.PrefetchScalarGridSpec(
            num_scalar_prefetch=1,
            grid=(4, parts),
            in_specs=[wide, wide],
            out_specs=[
                pl.BlockSpec((block, cut), stay),
                pl.BlockSpec((block, cut), go),
                pl.BlockSpec((block, cols - cut), stay_other),
                pl.BlockSpec((block, cols - cut), go_other),
            ],
        ),
        out_shape=[jax.ShapeDtypeStruct((rows // 2, cut), BF16)] * 2
        + [jax.ShapeDtypeStruct((rows // 2, cols - cut), BF16)] * 2,
        compiler_params=pltpu.CompilerParams(vmem_limit_bytes=60 * 2**20),
        cost_estimate=cost(3),
        name="split_sum",
    )(bits, keep, got)


def merge_kernel(_bits, a0_ref, a1_ref, b0_ref, b1_ref, out_ref):
    step = pl.program_id(0)
    cut = a0_ref.shape[1]

    def put(here, cols, ref):
        @pl.when(here)
        def _():
            out_ref[:, cols] = ref[...]

    put(step // 2 == 0, slice(0, cut), a0_ref)
    put(step // 2 == 1, slice(0, cut), a1_ref)
    put(step % 2 == 0, slice(cut, None), b0_ref)
    put(step % 2 == 1, slice(cut, None), b1_ref)


def merge(first, second, bits):
    rows, cut = first[0].shape
    rest = second[0].shape[1]
    block = rows // 2
    low = lambda s, bits: (s % 2) ^ bits[0]
    high = lambda s, bits: (s // 2) ^ bits[1]
    own = lambda s, bits: (jnp.where(s < 2, s % 2, 1) ^ bits[0], 0)
    other = lambda s, bits: (jnp.where(s < 2, 0, s % 2) ^ bits[0], 0)
    beside = lambda s, bits: (high(s, bits), 0)
    return pl.pallas_call(
        merge_kernel,
        grid_spec=pltpu.PrefetchScalarGridSpec(
            num_scalar_prefetch=1,
            grid=(4,),
            in_specs=[
                pl.BlockSpec((block, cut), own),
                pl.BlockSpec((block, cut), other),
                pl.BlockSpec((block, rest), beside),
                pl.BlockSpec((block, rest), beside),
            ],
            out_specs=pl.BlockSpec(
                (block, cut + rest), lambda s, bits: (2 * high(s, bits) + low(s, bits), 0)
            ),
        ),
        out_shape=jax.ShapeDtypeStruct((2 * rows, cut + rest), BF16),
        compiler_params=pltpu.CompilerParams(vmem_limit_bytes=16 * 2**20),
        cost_estimate=cost(3),
        name="merge",
    )(bits, *first, *second)


def split_four_kernel(_own, keep_ref, got_ref, *outs):
    total = keep_ref[...] + got_ref[...]
    for s, ref in enumerate(outs):
        @pl.when(pl.program_id(0) == s)
        def _():
            ref[...] = total


def split_four(keep, got, own):
    rows, cols = keep.shape
    block = rows // 4
    there = pl.BlockSpec((block, cols), lambda s, own: (s ^ own[0], 0))
    return pl.pallas_call(
        split_four_kernel,
        grid_spec=pltpu.PrefetchScalarGridSpec(
            num_scalar_prefetch=1,
            grid=(4,),
            in_specs=[there, there],
            out_specs=[pl.BlockSpec((block, cols), lambda s, own: (0, 0))] * 4,
        ),
        out_shape=[jax.ShapeDtypeStruct((block, cols), BF16)] * 4,
        compiler_params=pltpu.CompilerParams(vmem_limit_bytes=16 * 2**20),
        cost_estimate=cost(2),
        name="split_four",
    )(own, keep, got)


def finish_kernel(a_ref, b_ref, first_ref, bias_ref, gain_ref, up_ref, table_ref, gate_ref, scale_ref):
    flat = a_ref[...] + b_ref[...]
    width = flat.shape[1]
    rows = flat.shape[0] * 2 // 3
    heads, count = table_ref.shape
    local_rows = bias_ref.shape[1]
    local = pltpu.roll(flat[:rows], width - first_ref[0], 1)[:, 0:LANES]
    bias_ref[...] = local[0:6, 0:local_rows]
    gain_ref[...] = local[6:8, 0:local_rows]
    up_ref[...] = local[8 : 8 + up_ref.shape[0], 0:local_rows]
    table = jnp.concatenate(
        [flat[rows:, 0:BUCKET_ROWS], flat[rows:, BUCKET_ROWS : 2 * BUCKET_ROWS]], axis=0
    )
    table_ref[...] = table[0:heads, 0:count]
    scale_ref[...] = table.T[count : count + 1, 0:heads]
    folded = flat[8:16, 0:LANES]
    for k in range(1, width // LANES):
        folded = folded + flat[8:16, k * LANES : (k + 1) * LANES]
    folded = (folded + pltpu.roll(folded, LANES // 2, 1))[:, 0 : LANES // 2]
    row = lax.broadcasted_iota(jnp.int32, gate_ref.shape, 0)
    gate_ref[...] = jnp.where(row < gate_ref.shape[0] // 2, folded[4:5], folded[5:6])


def finish(flat, other, first_row, local_rows, chunks, table_shape, gate_shape):
    shapes = [
        (6, local_rows), (2, local_rows), (chunks, local_rows), table_shape[::-1], gate_shape[::-1],
        (1, table_shape[1]),
    ]
    full = lambda s: pl.BlockSpec(s, lambda i: (0, 0))
    return pl.pallas_call(
        finish_kernel,
        grid=(1,),
        in_specs=[full(flat.shape), full(flat.shape), SMEM_SPEC],
        out_specs=[full(s) for s in shapes],
        out_shape=[jax.ShapeDtypeStruct(s, F32) for s in shapes],
        cost_estimate=cost(1),
        name="finish",
    )(flat, other, first_row)


hold = lax.optimization_barrier


def after(value, *earlier):
    return lax.optimization_barrier((value,) + earlier)[0]


def swap(array, axis, bit):
    size = lax.axis_size(axis)
    return lax.ppermute(array, axis, [(i, i ^ (1 << bit)) for i in range(size)])


def swap_places(array, mask):
    return lax.ppermute(array, "blk", [(i, i ^ mask) for i in range(lax.axis_size("blk"))])


def by_place(arrays):
    place = lax.axis_index("blk")
    odd, upper = (place & 1) == 1, (place >> 1) == 1
    near = [jnp.where(odd, arrays[1 - i], arrays[i]) for i in range(2)]
    far = [jnp.where(odd, arrays[3 - i], arrays[2 + i]) for i in range(2)]
    return [jnp.where(upper, f, n) for f, n in zip(far, near)] + [
        jnp.where(upper, n, f) for f, n in zip(far, near)
    ]


def bit_of(axis, bit):
    return (lax.axis_index(axis) >> bit) & 1


def bit_count(axis):
    count = lax.axis_size(axis).bit_length() - 1
    assert 1 << count == lax.axis_size(axis)
    return count


def join(array, axis, bit, position):
    def finish(flight):
        mine, other = flight
        upper = bit_of(axis, bit) == 1
        return jnp.stack(
            [jnp.where(upper, other, mine), jnp.where(upper, mine, other)], axis=position
        )

    return (array, swap(array, axis, bit)), finish


def at_once(step):
    flight, finish = step
    return finish(flight)


def together(steps):
    flights, finishes = zip(*steps)
    return flights, lambda done: [finish(flight) for finish, flight in zip(finishes, done)]


def gather_begin(first, second):
    low = bit_of("rows", 0) == 0
    keep, send = jnp.where(low, first, second), jnp.where(low, second, first)

    def finish(flight):
        mine, got = flight
        return jnp.stack([jnp.where(low, mine, got), jnp.where(low, got, mine)], axis=0)

    return (keep, swap(send, "rows", 0)), finish


def blk_bits():
    return list(reversed(range(bit_count("blk"))))


def gather_blk(part, number):
    return join(part, "blk", blk_bits()[number], 1 + number)


def halves_of(array):
    array = array.reshape(-1, array.shape[-1])
    cut = array.shape[-1] // 2 // LANES * LANES
    return [array[:, :cut], array[:, cut:]]


def orders():
    high = list(range(1, bit_count("rows")))
    return high, high[::-1]


def gather_high(halves, step):
    steps = []
    for half, order in zip(halves, orders()):
        position = sum(1 for other in order[:step] if other > order[step])
        steps.append(join(half, "rows", order[step], position))
    return together(steps)


def gather_last(halves):
    first, second = orders()
    rows = halves[0].reshape(-1, halves[0].shape[-1]).shape[0]
    if len(first) == 2 and rows % 32 == 0:
        flat = [v.reshape(-1, v.shape[-1]) for v in halves]
        flights = [(v, swap(v, "rows", order[1])) for v, order in zip(flat, (first, second))]
        bits = jnp.stack([bit_of("rows", bit) for bit in first])
        return flights, lambda flights: merge(flights[0], flights[1], bits)
    flights, finish = gather_high(halves, len(first) - 1)
    return flights, lambda flights: whole(finish(flights))


def whole(halves):
    return jnp.concatenate([h.reshape(-1, h.shape[-1]) for h in halves], axis=-1)


def added(pair):
    if len(pair) == 1:
        return pair[0]
    return pair[0] + pair[1]


def part_of(pair, index, axis):
    return added([lax.dynamic_index_in_dim(v, index, axis, keepdims=False) for v in pair])


def halve(pair, shape, axis, bit, position):
    pair = [v.reshape(shape + (-1, v.shape[-1])) for v in pair]
    mine = bit_of(axis, bit)
    return part_of(pair, mine, position), swap(part_of(pair, 1 - mine, position), axis, bit)


def scatter_begin(keep, send):
    return keep, swap(send, "rows", 0)


def scatter_first(pair):
    first, second = orders()
    rows, cols = pair[0].shape
    if len(first) == 2 and rows % 128 == 0:
        cut = halves_of(pair[0])[0].shape[1]
        bits = jnp.stack([bit_of("rows", bit) for bit in first])
        keep_a, send_a, keep_b, send_b = split_sum(pair[0], pair[1], bits, cut, 1)
        return [(keep_a, swap(send_a, "rows", first[0])), (keep_b, swap(send_b, "rows", second[0]))]
    return scatter_high([(half,) for half in halves_of(added(pair))], 0)


def scatter_high(halves, step):
    out = []
    for half, order in zip(halves, orders()):
        left = sorted(order[step:], reverse=True)
        out.append(halve(half, (2,) * len(left), "rows", order[step], left.index(order[step])))
    return out


def scatter_whole(halves):
    whole_sum = jnp.concatenate([added([v.reshape(-1, v.shape[-1]) for v in h]) for h in halves], axis=-1)
    return whole_sum


def exchange_first(blocks):
    upper = bit_of("blk", 1)
    pairs = blocks.reshape((2, 2) + blocks.shape[1:])
    keep = lax.dynamic_index_in_dim(pairs, upper, 0, keepdims=False)
    send = lax.dynamic_index_in_dim(pairs, 1 - upper, 0, keepdims=False)
    return (keep, swap_places(send, 2))


def exchange_second(flight):
    odd = bit_of("blk", 0)
    pick = lambda array, index: lax.dynamic_index_in_dim(array, index, 0, keepdims=False)
    send = jnp.stack([pick(array, 1 - odd) for array in flight])
    return (pick(flight[0], odd), pick(flight[1], odd), swap_places(send, 1))


def exchange_end(flight):
    mine, far, other = flight
    return [mine, other[0], far, other[1]]


def total_of(parts):
    return sum(v.astype(F32) for v in parts).astype(BF16)


def scatter_four(pair):
    own = bit_of("rows", 1) + 2 * bit_of("rows", 2)
    blocks = split_four(pair[0], pair[1], own.reshape(1))
    size = lax.axis_size("rows")
    return [blocks[0]] + [
        lax.ppermute(blocks[s], "rows", [(i, i ^ (2 * s)) for i in range(size)]) for s in (1, 2, 3)
    ]


def scatter_places(parts):
    place = lax.axis_index("blk")
    views = [v.reshape((2, 4, -1, v.shape[-1])) for v in parts]
    blocks = [
        total_of([lax.dynamic_index_in_dim(v, place ^ s, 1, keepdims=False) for v in views]) for s in range(4)
    ]
    return [blocks[0]] + [swap_places(blocks[s], s) for s in (1, 2, 3)]


def scatter_blk(pair, bit):
    count = bit_count("blk")
    return halve(pair, (2,) * (1 + count - bit), "blk", bit, count - bit)


def scatter_end(pair):
    core = bit_of("rows", 0)
    pair = [v.reshape((2, -1, v.shape[-1])) for v in pair]
    half = lambda index: total_of([lax.dynamic_index_in_dim(v, index, 0, keepdims=False) for v in pair])
    return half(core), swap(half(1 - core), "rows", 0)


def scatter_done(flight):
    keep, got = flight
    low = bit_of("rows", 0) == 0
    return jnp.where(low, keep, got).astype(F32), jnp.where(low, got, keep).astype(F32)


def shards(
    hidden_in,
    segment_ids,
    bucket_map,
    qkv_weight,
    out_weight,
    up_weight,
    down_weight,
    bias_cols,
    norm_gains,
    up_bias,
    rel_table,
    gate_weight,
    gate_scale,
    cotangent,
):
    row_count, block_len, width = hidden_in.shape
    heads = gate_scale.shape[0]
    pairs = heads // 2
    head_dim = width // heads
    bucket_count = rel_table.shape[0]
    cycle = lax.axis_size("blk")
    place = lax.axis_index("blk")
    core = bit_of("rows", 0).reshape(1)
    frames = block_len * cycle
    shared = row_count - 1
    used = frames + block_len
    total = -(-used // 256) * 256
    inner_width = up_weight.shape[1]
    chunks = inner_width // width
    local_rows = qkv_weight.shape[0]
    half = width // 2
    cut = 3 * half
    high_steps = len(orders()[0])
    assert row_count == cycle + 1 and cycle == 4 and bucket_count < BUCKET_ROWS

    def take(array, index):
        return lax.dynamic_index_in_dim(array, index, 0, keepdims=False)

    def with_rest(blocks, last):
        return jnp.concatenate(blocks + [last, jnp.zeros((total - used, width), BF16)], axis=0)

    extras = jnp.concatenate(
        [bias_cols, norm_gains, up_bias.reshape(local_rows, chunks)], axis=1
    )
    extras = jnp.pad(extras, ((0, 0), (0, SMALL - extras.shape[1])))
    qkv_part = at_once(
        gather_begin(
            jnp.concatenate([qkv_weight[:, :cut], extras], axis=1),
            jnp.concatenate([qkv_weight[:, cut:], jnp.zeros_like(extras)], axis=1),
        )
    )
    up_turned = up_weight.reshape(local_rows, width, chunks).transpose(0, 2, 1)
    rest_flight, rest_finish = gather_begin(
        jnp.concatenate([up_turned.reshape(local_rows, inner_width), out_weight[:, :half]], axis=1),
        jnp.concatenate([down_weight.reshape(local_rows, inner_width), out_weight[:, half:]], axis=1),
    )
    head_rows = -(-heads // 16) * 16
    picks = jnp.repeat(jnp.eye(heads, head_rows, dtype=F32), head_dim, axis=0)
    dirs = [
        picks * jnp.tile(jnp.sum(gate_weight[:, part], axis=1), heads)[:, None]
        for part in (slice(0, 4), slice(4, 8))
    ]
    dirs_high, dirs_middle, dirs_low = thirds(jnp.concatenate(dirs, axis=1).T)
    dirs_all = jnp.concatenate([dirs_high, dirs_middle, dirs_low], axis=0)
    dirs_mix = jnp.concatenate([dirs_high, dirs_high, dirs_middle], axis=0)
    scale_rows = jnp.pad(gate_scale, (0, head_rows - heads))[:, None]

    shift = -(-frames // LANES)
    span = 2 * frames - 1
    lead = shift * LANES - (frames - 1)
    table_width = 2 * shift * LANES
    narrow = -(-(shift * LANES + block_len) // LANES) * LANES
    slots = jnp.pad(bucket_map[::-1], (lead, table_width - lead - span), constant_values=-1)
    hot = (jnp.arange(bucket_count, dtype=jnp.int32)[:, None] == slots[None, :]).astype(F32)

    hidden_in, segment_ids, rest_flight, qkv_part = hold(
        (hidden_in, segment_ids, rest_flight, qkv_part)
    )
    seg_rows = jnp.pad(segment_ids.astype(BF16), ((0, 0), (0, width - block_len)))

    def with_segments(index):
        tail_rows = jnp.pad(jnp.stack([take(seg_rows, index), seg_rows[shared]]), ((0, 14), (0, 0)))
        return jnp.concatenate([take(hidden_in, index), tail_rows], axis=0)

    packs = [with_segments(place ^ s) for s in range(cycle)]
    qkv_flight, qkv_finish = gather_blk(qkv_part, 0)
    qkv_flight, rest_flight = hold((qkv_flight, rest_flight))
    qkv_flight, qkv_finish = gather_blk(qkv_finish(qkv_flight), 1)
    rest_flight, rest_finish = gather_blk(rest_finish(rest_flight), 0)
    qkv_flight, packs, rel_table, hot, cotangent = hold(
        (qkv_flight, packs, rel_table, hot, cotangent)
    )
    cot = [take(cotangent, place ^ s) for s in range(cycle)] + [cotangent[shared]]
    blank = jnp.zeros((total, width), BF16)
    packs[1] = swap_places(packs[1], 1)
    qkv_part = qkv_finish(qkv_flight)
    qkv_halves = halves_of(qkv_part)
    for step in range(high_steps - 2):
        qkv_halves = at_once(gather_high(qkv_halves, step))
    qkv_flight, qkv_finish = gather_high(qkv_halves, high_steps - 2)
    table = jnp.pad(rel_table, ((0, 0), (0, head_rows - heads)))
    u_own = lax.dot_general(table, hot, (((0,), (0,)), ((), ())), precision=HIGHEST)
    u_loc = lax.dynamic_slice_in_dim(
        jnp.pad(u_own, ((0, 0), (0, frames))), place * block_len, narrow, 1
    )
    qkv_flight, rest_flight, far_packs, cot, blank, u_own, u_loc, dirs_all, x_loc = hold(
        (qkv_flight, rest_flight, packs[2:], cot, blank, u_own, u_loc, dirs_all, hidden_in[shared])
    )
    packs = packs[:2] + list(far_packs)
    packs[2], packs[3] = swap_places(packs[2], 2), swap_places(packs[3], 3)
    qkv_flight, qkv_finish = gather_last(qkv_finish(qkv_flight))
    rest_flight, rest_finish = gather_blk(rest_finish(rest_flight), 1)
    qkv_flight, rest_flight, packs = hold((qkv_flight, rest_flight, packs))
    qkv_mine = qkv_finish(qkv_flight)
    qkv_other = swap(qkv_mine, "rows", 0)
    rest_halves = halves_of(rest_finish(rest_flight))
    for step in range(high_steps - 2):
        rest_halves = at_once(gather_high(rest_halves, step))
    rest_flight, rest_finish = gather_high(rest_halves, high_steps - 2)
    shared_flight, shared_finish = join(x_loc, "blk", 1, 0)
    own_cols = (0, pairs, 2 * pairs)
    loc_cols = (0, 0, pairs)
    place_of = place.reshape(1)
    (
        qkv_own, qkv_full, small, x_cat, qa_own, ka_own, qa_loc, ka_all, gate_own, gate_loc, g_own, g_loc,
    ) = project_own(packs, x_loc, qkv_mine, qkv_other, dirs_all, scale_rows, core, place_of, total)
    rest_flight, shared_flight, qkv_own, small, cot = hold(
        (rest_flight, shared_flight, qkv_own, small, cot)
    )
    rest_flight, rest_finish = gather_last(rest_finish(rest_flight))
    shared_flight, shared_finish = join(shared_finish(shared_flight), "blk", 0, 1)
    cot[2] = swap_places(cot[2], 2)
    att_half, att, lse_own = attend_forward(
        u_own, qkv_own, qkv_own, qkv_own, qa_own, ka_own, g_own, own_cols, pairs, frames, True,
        (blank,), 0, 18,
    )
    shared_flight, rest_flight, cot, att, att_half, lse_own = hold(
        (shared_flight, rest_flight, cot, att, att_half, lse_own)
    )
    rest_mine = rest_finish(rest_flight)
    rest_other = swap(rest_mine, "rows", 0)
    x_all = shared_finish(shared_flight).reshape(frames, width)
    q_loc, kv_all = project_shared(x_all, x_loc, qkv_full, small, (rest_mine,))
    cot[1], cot[3] = swap_places(cot[1], 1), swap_places(cot[3], 3)
    att_half, att, lse_loc = attend_forward(
        u_loc, q_loc, kv_all, kv_all, qa_loc, ka_all, g_loc, loc_cols, pairs, frames, False,
        (att_half, att), cycle, 8,
    )
    cot, rest_other, att, att_half, lse_loc = hold((cot, rest_other, att, att_half, lse_loc))
    h_cat, ga_cat, g1_cat, rest_keep, rest_send, sums = layer_rest(
        x_cat, att_half, cot, rest_mine, rest_other, small, core, place_of, chunks
    )

    def blocks_of(own):
        return own[:frames].reshape(cycle, block_len, width)

    rest_flight = scatter_begin(rest_keep, rest_send)
    hidden = [take(blocks_of(h_cat), place ^ s) for s in range(cycle)]
    hidden[1], hidden[2] = swap_places(hidden[1], 1), swap_places(hidden[2], 2)
    dq_loc, dkv_all, col_loc, grad_loc, diag_loc = attend_backward(
        u_loc, q_loc, kv_all, kv_all, ga_cat, att, qa_loc, ka_all, g_loc, lse_loc,
        g_loc, u_loc, loc_cols, pairs, cycle, 16, 0, pairs,
    )
    part_all, mine = shared_input(
        dq_loc, dkv_all, qkv_full, g1_cat, cycle, grad_loc, gate_loc, scale_rows, dirs_mix
    )
    rest_flight, hidden[:3], part_all = hold((rest_flight, hidden[:3], part_all))
    hidden[3] = swap_places(hidden[3], 3)
    rest_flight = scatter_first(rest_flight)
    part_flight = halve((part_all,), (2, 2), "blk", 0, 1)
    third = pairs // 3
    into = attend_backward(
        u_own, qkv_own, qkv_own, qkv_own, ga_cat, att, qa_own, ka_own, g_own, lse_own,
        g_own, u_own, own_cols, pairs, 0, 26, 0, pairs - third, (),
        (rest_flight[0][0], rest_flight[1][0], part_flight[0]),
    )
    rest_flight, part_flight, into, hidden[3] = hold((rest_flight, part_flight, into, hidden[3]))
    for step in range(1, high_steps):
        rest_flight = scatter_high(rest_flight, step)
    part_flight = halve(part_flight, (2,), "blk", 1, 0)
    dq_own, dkv_own, col_own, grad_own, diag = into
    into = attend_backward(
        u_own, qkv_own, qkv_own, qkv_own, ga_cat, att, qa_own, ka_own, g_own, lse_own,
        grad_own, diag, own_cols, pairs, 0, 13, pairs - third, third, (dq_own, dkv_own, col_own),
        (rest_flight[0][0], rest_flight[1][0]),
    )
    rest_flight, part_flight, into = hold((rest_flight, part_flight, into))
    dq_own, dkv_own, col_own, grad_own, diag = into
    rest_flight = scatter_blk((scatter_whole(rest_flight),), 0)
    flat = gate_sums(
        (grad_own, grad_loc), (gate_own, gate_loc), scale_rows, (diag, diag_loc), slots[None, :], x_cat, x_loc,
        (col_own, col_loc), sums, (place * block_len).reshape(1), bucket_count,
    )
    direct = high_steps == 2 and width % 64 == 0
    upper = [2 * s for s in (1, 2, 3)] if direct else []
    swap_rows = lambda array, mask: lax.ppermute(
        array, "rows", [(i, i ^ mask) for i in range(lax.axis_size("rows"))]
    )
    add_up = lambda arrays: sum(arrays[1:], arrays[0])
    flat_flight = [flat] + [swap_rows(flat, mask) for mask in upper]
    dx_own = own_input(
        dq_own, dkv_own, qkv_full, g1_cat, grad_own, gate_own, scale_rows, dirs_mix, (rest_flight[0], flat)
    )
    flat_flight, dx_own = hold((flat_flight, dx_own))
    flat = add_up(flat_flight)
    flat_flight = (flat, swap(flat, "rows", 0))
    inputs = [take(blocks_of(dx_own), place ^ s) for s in range(cycle)]
    inputs[1], inputs[2] = swap_places(inputs[1], 1), swap_places(inputs[2], 2)
    qkv_keep, qkv_send = weight_grad(
        x_cat, x_all, x_loc, dq_own, dkv_own, dq_loc, dkv_all, core, (dx_own,)
    )
    rest_flight, flat_flight, qkv_keep, qkv_send, inputs = hold(
        (rest_flight, flat_flight, qkv_keep, qkv_send, inputs)
    )
    back_flight = scatter_begin(qkv_keep, qkv_send)
    flat = add_up(flat_flight)
    rest_flight = scatter_blk(rest_flight, 1)
    back_flight = hold(back_flight)
    if direct:
        back_flight = scatter_four(back_flight)
    else:
        back_flight = scatter_first(back_flight)
        for step in range(1, high_steps):
            back_flight = scatter_high(back_flight, step)
    inputs[3], hidden = hold((inputs[3], hidden, back_flight[0]))[:2]
    inputs[3] = swap_places(inputs[3], 3)
    hidden_out = settle(hidden, (h_cat,), cycle, place_of)
    rest_flight = scatter_end(rest_flight)
    back_flight, rest_flight, inputs, flat, hidden_out = hold(
        (back_flight, rest_flight, inputs, flat, hidden_out)
    )
    if direct:
        back_flight = scatter_places(back_flight)
    else:
        back_flight = scatter_blk(scatter_blk((scatter_whole(back_flight),), 0), 1)
        for bit in range(1, bit_count("rows")):
            flat = flat + swap(flat, "rows", bit)
    flat, rest_flight, inputs = hold((flat, rest_flight, inputs, back_flight[0]))[:3]
    flat_flight = (flat, swap_places(flat, 1))
    grad_input = settle(inputs, (mine,) + tuple(part_flight), 0, place_of)
    back_flight, flat_flight, grad_input = hold((back_flight, flat_flight, grad_input))
    back_flight = scatter_end(back_flight)
    rest_flight = hold((rest_flight, back_flight[0]))[0]
    rest_first, rest_second = scatter_done(rest_flight)
    grad_up = rest_first[:, :inner_width].reshape(local_rows, chunks, width).transpose(0, 2, 1)
    grad_up = grad_up.reshape(local_rows, inner_width)
    grad_down = rest_second[:, :inner_width].reshape(local_rows * chunks, width)
    grad_out = jnp.concatenate([rest_first[:, inner_width:], rest_second[:, inner_width:]], axis=1)
    flat = add_up(flat_flight)
    flat_flight = (flat, swap_places(flat, 2))
    last_first, last_second = scatter_done(back_flight)
    first_row = (lax.axis_index("rows") * cycle + place) * local_rows
    bias_sum, gain_sum, up_bias_sum, table_sum, gate_weight_sum, gate_scale_sum = finish(
        *flat_flight, first_row.reshape(1), local_rows, chunks, rel_table.shape, gate_weight.shape
    )
    return (
        hidden_out,
        grad_input,
        jnp.concatenate([last_first, last_second], axis=1),
        grad_out,
        grad_up,
        grad_down,
        bias_sum.T,
        gain_sum.T,
        up_bias_sum.T.reshape(-1),
        table_sum.T,
        gate_weight_sum.T,
        gate_scale_sum.reshape(-1),
    )


def solution(mesh):
    placed = (
        P("rows", "blk", None),
        P("rows", "blk"),
        P(),
        P(("rows", "blk"), None),
        P(("rows", "blk"), None),
        P(("rows", "blk"), None),
        P(("rows", "blk"), None),
        P(("rows", "blk"), None),
        P(("rows", "blk"), None),
        P(("rows", "blk")),
        P(),
        P(),
        P(),
        P("rows", "blk", None),
    )
    return jax.shard_map(
        shards,
        mesh=mesh,
        in_specs=placed,
        out_specs=(
            P("rows", "blk", None),
            P("rows", "blk", None),
            P(("rows", "blk"), None),
            P(("rows", "blk"), None),
            P(("rows", "blk"), None),
            P(("rows", "blk"), None),
            P(("rows", "blk"), None),
            P(("rows", "blk"), None),
            P(("rows", "blk")),
            P(),
            P(),
            P(),
        ),
        check_vma=False,
    )
```
